32 devices in a mesh: var: 16 (over z, y, x), samp: 2 (over core).
Axes of the slice: x: 2, y: 2, z: 4, core: 2. Of those that a mesh axis runs over, the one named last changes fastest.
Arguments:
- data: float32 [512, 8192], P('samp', 'var'), may hold values from -6 to 6
- tiles: float32 [16, 3, 512, 512], P('var'), as said below
- offsets: int32 [16, 3], P('var'), may hold values from 0 to 5, as said below
- step: float32 [1], replicated, may hold values from 0.3 to 0.7
Outputs:
- new_tiles: float32 [16, 3, 512, 512], P('var', None, 'samp')
The draws below stay inside these ranges and needn't reach their ends.
Inputs may be any that keep to these rules, and one draw needn't show every extreme that they name: Slot 0 of every block row has offset 0. Every other slot holds 0 (empty) or an offset of 1 to 5; live slots come first in a row and their offsets differ. Some block row has all 3 slots live, one of them at offset 5. `tiles`: tiles of empty slots are zero. Slot 0 is symmetric with its diagonal between 1 and 2.
All inputs are finite; a program needn't handle non-finite values.
Results may differ from the reference program's by a relative error of at most 0.0003.
Values sent between devices are 32-bit elements; how exact they have to be, the bound alone decides.
No kernel may reach another device: no remote copies, remote signals or barrier semaphores. Data moves between devices by JAX's collectives and lax.ppermute only.
A program may use at most 64 MiB of HBM per device.

```python
import jax
import jax.numpy as jnp
from jax import lax

BLOCK = 512
MOST = 3
BAND = 6
VARS = 8192
SAMPLES = 512
N_VAR = 16


def offsets_table(key):
    base = jax.random.fold_in(key, 101)
    first_key, second_key, perm_key, full_key, short_key = jax.random.split(base, 5)
    extra_tiles = jnp.minimum(jax.random.randint(first_key, (N_VAR,), 0, MOST), jax.random.randint(second_key, (N_VAR,), 0, MOST))
    full_row = jax.random.randint(full_key, (), 0, N_VAR)
    row_ids = jnp.arange(N_VAR)
    extra_tiles = jnp.where(row_ids == full_row, MOST - 1, extra_tiles)
    shuffled = jax.vmap(lambda subkey: jax.random.permutation(subkey, BAND - 1))(jax.random.split(perm_key, N_VAR)) + 1
    picked = shuffled[:, :MOST - 1]
    shorter = jax.random.permutation(short_key, BAND - 2) + 1
    full_pick = jnp.concatenate([shorter[:MOST - 2], jnp.full((1,), BAND - 1, jnp.int32)]).astype(jnp.int32)
    picked = jnp.where((row_ids == full_row)[:, None], full_pick[None, :], picked)
    slot_ids = jnp.arange(1, MOST)
    live_slots = slot_ids[None, :] <= extra_tiles[:, None]
    rest = jnp.where(live_slots, picked, 0)
    return jnp.concatenate([jnp.zeros((N_VAR, 1), jnp.int32), rest.astype(jnp.int32)], axis=1).astype(jnp.int32)


def draw_offsets(key, part):
    return offsets_table(key)


def draw_tiles(key, part):
    offset_table = offsets_table(key)
    base = jax.random.fold_in(key, 202)
    entry_key, diag_key = jax.random.split(base, 2)
    shape_full = (N_VAR, MOST, BLOCK, BLOCK)
    entries = 0.04 * jax.random.normal(entry_key, shape_full, jnp.float32)
    diag_values = jax.random.uniform(diag_key, (N_VAR, BLOCK), jnp.float32, 1.0, 2.0)
    first_slot = 0.5 * (entries[:, 0] + jnp.transpose(entries[:, 0], (0, 2, 1)))
    diag_mask = jnp.eye(BLOCK, dtype=bool)
    first_slot = jnp.where(diag_mask[None], diag_values[:, None, :], first_slot)
    others = entries[:, 1:] * (offset_table[:, 1:] > 0).astype(jnp.float32)[:, :, None, None]
    return jnp.concatenate([first_slot[:, None], others], axis=1)


def level_of(rng, dims, cuts, low, largest):
    level = 1.0
    for position, blocks in cuts:
        draws = jax.random.uniform(jax.random.fold_in(jax.random.fold_in(rng, 6), position), (blocks,), jnp.float32, low / len(cuts), largest / len(cuts))
        level = level * jnp.repeat(jnp.exp(draws), dims[position] // blocks).reshape((-1,) + (1,) * (len(dims) - 1 - position))
    return level


def noise(stream_key, extent, width, reach, cuts=(), kind=jnp.bfloat16):
    drawn = jax.random.normal(stream_key, extent, jnp.float32) * width
    if len(cuts) > 0:
        drawn = level_of(stream_key, extent, cuts, -0.22, 0.18) * drawn
    return jnp.clip(drawn, min=-reach, max=reach).astype(kind)


def setup_inputs(seed: int = 0) -> dict:
    splits = jax.random.split(jax.random.key(seed), 5)
    return {
        "data": noise(splits[0], (SAMPLES, VARS), 1.0, 6.0, ((0, 2), (1, 16)), jnp.float32),
        "tiles": draw_tiles(jax.random.fold_in(splits[4], 71), 0),
        "offsets": draw_offsets(jax.random.fold_in(splits[4], 71), 0),
        "step": jnp.clip(jax.random.uniform(splits[3], (1,), jnp.float32, 0.3, 0.7), 0.3, 0.7),
    }


highest = lax.Precision.HIGHEST
penalty_weight = 0.05


def matmul(left_op, right_op):
    return jnp.dot(left_op, right_op, precision=highest, preferred_element_type=jnp.float32)


def columns(array, block_index):
    return lax.dynamic_slice_in_dim(array, (block_index * BLOCK).astype(jnp.int32), BLOCK, 1)


def reference(data, tiles, offsets, step):
    samples = data.shape[0]
    step_size = step[0]

    def add_row(image_acc, block_row):
        for slot_index in range(MOST):
            shift_by = offsets[block_row, slot_index]
            partner = ((block_row + shift_by) % N_VAR).astype(jnp.int32)
            tile_now = tiles[block_row, slot_index]
            live_flag = jnp.where((slot_index == 0) | (shift_by > 0), 1.0, 0.0).astype(jnp.float32)
            mirror = jnp.where(shift_by > 0, 1.0, 0.0).astype(jnp.float32)
            own_block = columns(data, block_row)
            far_block = columns(data, partner)
            forward = matmul(own_block, tile_now) * live_flag
            image_acc = lax.dynamic_update_slice_in_dim(image_acc, columns(image_acc, partner) + forward, (partner * BLOCK).astype(jnp.int32), 1)
            backward = matmul(far_block, tile_now.T) * mirror
            image_acc = lax.dynamic_update_slice_in_dim(image_acc, columns(image_acc, block_row) + backward, (block_row * BLOCK).astype(jnp.int32), 1)
        return image_acc, None

    row_list = jnp.arange(N_VAR, dtype=jnp.int32)
    image_acc, _ = lax.scan(add_row, jnp.zeros(data.shape, jnp.float32), row_list)
    diag_mask = jnp.eye(BLOCK, dtype=bool)

    def new_row(block_row):
        pieces = []
        for slot_index in range(MOST):
            shift_by = offsets[block_row, slot_index]
            partner = ((block_row + shift_by) % N_VAR).astype(jnp.int32)
            tile_now = tiles[block_row, slot_index]
            live_flag = jnp.where((slot_index == 0) | (shift_by > 0), 1.0, 0.0).astype(jnp.float32)
            own_block = columns(data, block_row)
            far_block = columns(data, partner)
            left_term = matmul(own_block.T, columns(image_acc, partner))
            right_term = matmul(columns(image_acc, block_row).T, far_block)
            gradient = (left_term + right_term) / (2.0 * samples)
            if slot_index == 0:
                gradient = gradient - jnp.where(diag_mask, (1.0 / jnp.diagonal(tile_now))[None, :], 0.0)
            stepped = tile_now - step_size * gradient
            shrunk = jnp.sign(stepped) * jnp.maximum(jnp.abs(stepped) - step_size * penalty_weight, 0.0)
            if slot_index == 0:
                shrunk = jnp.where(diag_mask, stepped, shrunk)
            pieces.append(shrunk * live_flag)
        return jnp.stack(pieces)

    return lax.map(new_row, row_list)
```

```python
import functools

import jax
import jax.numpy as jnp
from jax import lax
from jax.experimental import pallas as pl
from jax.experimental.pallas import tpu as pltpu
from jax.sharding import PartitionSpec as P

penalty_weight = 0.05
VMEM_LIMIT = 48 * 1024 * 1024
NN = (((1,), (0,)), ((), ()))
NT = (((1,), (1,)), ((), ()))
f32, bf16 = jnp.float32, jnp.bfloat16


def params(**kw):
    return pltpu.CompilerParams(vmem_limit_bytes=VMEM_LIMIT, **kw)


def cost(flops, nbytes):
    return pl.CostEstimate(flops=flops, bytes_accessed=nbytes, transcendentals=0)


def any_spec():
    return pl.BlockSpec(memory_space=pl.ANY)


def vmem_spec():
    return pl.BlockSpec(memory_space=pltpu.VMEM)


def smem_spec():
    return pl.BlockSpec(memory_space=pltpu.SMEM)


def split(value):
    high = value.astype(bf16)
    return high, (value - high.astype(f32)).astype(bf16)


def dot3(left, right, dims):
    dot = functools.partial(lax.dot_general, dimension_numbers=dims, preferred_element_type=f32)
    return dot(left[0], right[0]) + (dot(left[0], right[1]) + dot(left[1], right[0]))


def route(p, k, flip):
    xbit = k & 1
    ybit = (((p + k) >> 1) ^ (p >> 1)) & 1
    first = jnp.where(flip == 0, xbit, ybit)
    last = jnp.where(flip == 0, ybit, xbit)
    return last, first + 2 * ((p + k) >> 2)


def place():
    return lax.axis_index("var") & 3, lax.axis_index("samp") & 1


def last_partner(p, flip):
    return jnp.where(flip == 0, p ^ 2, p ^ 1)


def hop(var_count, samp_count, kind, reverse=False):
    pairs = []
    for var in range(var_count):
        for samp in range(samp_count):
            flip = samp & 1
            first, last = (2, 1) if flip else (1, 2)
            if kind == "first":
                target = var ^ first
            elif kind == "last":
                target = var ^ last
            elif kind == "group":
                target = (var - 4) % var_count
            else:
                if var & 3:
                    continue
                target = ((var - 4) % var_count) ^ first
            pair = (var * samp_count + samp, target * samp_count + samp)
            pairs.append(pair[::-1] if reverse else pair)
    return pairs


def send(value, kind, reverse=False):
    pairs = hop(lax.axis_size("var"), lax.axis_size("samp"), kind, reverse)
    return lax.ppermute(value, ("var", "samp"), pairs)


def forward_kernel(data_ref, tile_ref, own_ref, far_ref):
    slot = pl.program_id(0)
    value = dot3(split(data_ref[...]), split(tile_ref[...]), NN)

    @pl.when(slot == 0)
    def _():
        own_ref[...] = value

    @pl.when(slot > 0)
    def _():
        far_ref[...] = value


def forward(data, tiles):
    slots, block = tiles.shape[:2]
    rows = data.shape[0]
    return pl.pallas_call(
        forward_kernel,
        grid=(slots,),
        in_specs=[
            pl.BlockSpec((rows, block), lambda j: (0, 0)),
            pl.BlockSpec((None, block, block), lambda j: (j, 0, 0)),
        ],
        out_specs=[
            pl.BlockSpec((rows, block), lambda j: (0, 0)),
            pl.BlockSpec((None, rows, block), lambda j: (jnp.maximum(j - 1, 0), 0, 0)),
        ],
        out_shape=[
            jax.ShapeDtypeStruct((rows, block), f32),
            jax.ShapeDtypeStruct((slots - 1, rows, block), f32),
        ],
        compiler_params=params(),
        cost_estimate=cost(6 * slots * rows * block * block, 4 * slots * block * (block + 2 * rows)),
        name="forward",
    )(data, tiles)


def choose_kernel(slots, offs_ref, own, first, group, both, two, out, sems):
    p, flip = place()
    target = last_partner(p, flip)
    copies = []
    for slot in range(slots):
        last, code = route(target, offs_ref[0, slot + 1], flip)
        for value, source in ((0, own), (1, first), (2, group), (3, both), (5, two)):
            copy = pltpu.make_async_copy(source, out.at[slot], sems.at[slot])
            pl.when((last == 1) & (code == value))(copy.start)
        copies.append((last, pltpu.make_async_copy(own, out.at[slot], sems.at[slot])))
    for last, copy in copies:
        pl.when(last == 1)(copy.wait)


def choose(offsets_next, own, first, group, both, two):
    slots = offsets_next.shape[1] - 1
    return pl.pallas_call(
        functools.partial(choose_kernel, slots),
        in_specs=[smem_spec()] + [any_spec()] * 5,
        out_specs=any_spec(),
        out_shape=jax.ShapeDtypeStruct((slots,) + own.shape, f32),
        scratch_shapes=[pltpu.SemaphoreType.DMA((slots,))],
        compiler_params=params(),
        cost_estimate=cost(0, 8 * slots * own.size),
        name="choose",
    )(offsets_next, own, first, group, both, two)


def start_pick(offset, slot, sources, target, sem):
    own, first, group, both, last_ref = sources
    p, flip = place()
    last, code = route(p, offset, flip)
    for value, source in ((0, own), (1, first), (2, group), (3, both)):
        pl.when((last == 0) & (code == value))(pltpu.make_async_copy(source, target, sem).start)
    pl.when(last == 1)(pltpu.make_async_copy(last_ref.at[slot], target, sem).start)


def backward_kernel(slots, offs_ref, tile_ref, own, first, group, both, last_ref, out_ref, picked, sems):
    slot = pl.program_id(0)
    sources = (own, first, group, both, last_ref)

    @pl.when(slot == 0)
    def _():
        out_ref[...] = jnp.zeros_like(out_ref)
        for each in range(slots):
            start_pick(offs_ref[0, each + 1], each, sources, picked.at[each], sems.at[each])

    pltpu.make_async_copy(own, picked.at[slot], sems.at[slot]).wait()
    mirror = jnp.where(offs_ref[0, slot + 1] > 0, 1.0, 0.0).astype(f32)
    out_ref[...] += mirror * dot3(split(picked[slot]), split(tile_ref[...]), NT)


def backward(offsets, tiles, sources):
    slots, block = tiles.shape[0] - 1, tiles.shape[1]
    own = sources[0]
    rows = own.shape[0]
    return pl.pallas_call(
        functools.partial(backward_kernel, slots),
        grid=(slots,),
        in_specs=[smem_spec(), pl.BlockSpec((None, block, block), lambda j: (j + 1, 0, 0))] + [any_spec()] * 5,
        out_specs=pl.BlockSpec((rows, block), lambda j: (0, 0)),
        out_shape=jax.ShapeDtypeStruct((rows, block), f32),
        scratch_shapes=[pltpu.VMEM((slots, rows, block), f32), pltpu.SemaphoreType.DMA((slots,))],
        compiler_params=params(),
        cost_estimate=cost(6 * slots * rows * block * block, 4 * slots * block * (block + rows)),
        name="backward",
    )(offsets, tiles, *sources)


def bins_kernel(slots, offs_ref, next_ref, own_in, mine_ref, theirs_ref, own_out, first, group, both, two):
    p, flip = place()
    target = last_partner(p, flip)
    totals = [own_in[...], None, None, None, None]
    for which, value in enumerate((0, 1, 2, 3, 5)):
        total = totals[which]
        for slot in range(slots):
            for there, offs, source in ((0, offs_ref, mine_ref), (1, next_ref, theirs_ref)):
                offset = offs[0, slot + 1]
                last, code = route(jnp.where(there == 1, target, p), offset, flip)
                use = (last == there) & (code == value) & (offset > 0)
                term = jnp.where(use, source[slot], 0.0)
                total = term if total is None else total + term
        totals[which] = total
    for ref, total in zip((own_out, first, group, both, two), totals):
        ref[...] = total


def make_bins(offsets, offsets_next, own, mine, theirs):
    slots, rows, block = mine.shape
    step = rows // 4
    flat = pl.BlockSpec((step, block), lambda i: (i, 0))
    deep = pl.BlockSpec((slots, step, block), lambda i: (0, i, 0))
    return pl.pallas_call(
        functools.partial(bins_kernel, slots),
        grid=(rows // step,),
        in_specs=[smem_spec(), smem_spec(), flat, deep, deep],
        out_specs=[flat] * 5,
        out_shape=[jax.ShapeDtypeStruct((rows, block), f32)] * 5,
        compiler_params=params(),
        cost_estimate=cost(20 * rows * block, 40 * rows * block),
        name="bins",
    )(offsets, offsets_next, own, mine, theirs)


def right_kernel(slots, pair, offs_ref, data_ref, image_ref, own, first, group, both, last_ref,
                 keep_ref, send_ref, high_ref, low_ref, picked, sems):
    sources = (own, first, group, both, last_ref)
    for slot in range(slots):
        start_pick(offs_ref[0, slot + 1], slot, sources, picked.at[slot], sems.at[slot])
    half = image_ref.shape[1] // 2
    samp = lax.axis_index("samp") if pair else 0
    data = data_ref[...]
    image = image_ref[...]
    data_turned = split(data.T)
    high_ref[...], low_ref[...] = data_turned
    turned = split(image.T)
    image_pair, data_pair = split(image), split(data)

    def store(ref, which, lower, upper):
        @pl.when(samp == 0)
        def _():
            keep_ref[which] = lower
            send_ref[which] = upper

        @pl.when(samp != 0)
        def _():
            keep_ref[which] = upper
            send_ref[which] = lower

    total = dot3(turned, data_pair, NN) + dot3(data_turned, image_pair, NN)
    store(None, 0, total[:half], total[half:])
    for slot in range(slots):
        pltpu.make_async_copy(own, picked.at[slot], sems.at[slot]).wait()
        total = dot3(turned, split(picked[slot]), NN)
        store(None, slot + 1, total[:half], total[half:])


def right(offsets, data, image, sources, pair):
    slots = offsets.shape[1] - 1
    rows, block = data.shape
    part = jax.ShapeDtypeStruct((slots + 1, block // 2, block), f32)
    turned = jax.ShapeDtypeStruct((block, rows), bf16)
    return pl.pallas_call(
        functools.partial(right_kernel, slots, pair),
        in_specs=[smem_spec(), vmem_spec(), vmem_spec()] + [any_spec()] * 5,
        out_specs=[vmem_spec()] * 4,
        out_shape=[part, part, turned, turned],
        scratch_shapes=[pltpu.VMEM((slots, rows, block), f32), pltpu.SemaphoreType.DMA((slots,))],
        compiler_params=params(),
        cost_estimate=cost(6 * (slots + 2) * rows * block * block, 4 * (slots + 1) * block * (block + rows)),
        name="right",
    )(offsets, data, image, *sources)


def left_kernel(slots, pair, factor, offs_ref, step_ref, base_ref, high_ref, low_ref, own, first, group, both, last_ref,
                keep_ref, send_ref, picked, sems):
    slot = pl.program_id(0)
    sources = (own, first, group, both, last_ref)

    @pl.when(slot == 0)
    def _():
        for each in range(slots):
            start_pick(offs_ref[0, each + 1], each, sources, picked.at[each], sems.at[each])

    half = send_ref.shape[0]
    pltpu.make_async_copy(own, picked.at[slot], sems.at[slot]).wait()
    chosen = split(picked[slot])
    samp = lax.axis_index("samp") if pair else 0
    lower = dot3((high_ref[:half], low_ref[:half]), chosen, NN)
    upper = dot3((high_ref[half:], low_ref[half:]), chosen, NN)
    scale = step_ref[0] * factor
    if pair:
        send_ref[...] = jnp.where(samp == 0, upper, lower)
        keep_ref[...] = base_ref[...] - scale * jnp.where(samp == 0, lower, upper)
    else:
        keep_ref[...] = lower
        send_ref[...] = upper


def left(offsets, step, base, turned, sources, factor, pair):
    slots = offsets.shape[1] - 1
    block, rows = turned[0].shape
    half = block // 2
    spec = pl.BlockSpec((None, half, block), lambda j: (j, 0, 0))
    base_spec = pl.BlockSpec((None,) + base.shape[1:], lambda j: (j + 1, 0, 0))
    whole = pl.BlockSpec((block, rows), lambda j: (0, 0))
    part = jax.ShapeDtypeStruct((slots, half, block), f32)
    return pl.pallas_call(
        functools.partial(left_kernel, slots, pair, factor),
        grid=(slots,),
        in_specs=[smem_spec(), smem_spec(), base_spec, whole, whole] + [any_spec()] * 5,
        out_specs=[spec, spec],
        out_shape=[part, part],
        scratch_shapes=[pltpu.VMEM((slots, rows, block), f32), pltpu.SemaphoreType.DMA((slots,))],
        compiler_params=params(),
        cost_estimate=cost(6 * slots * rows * block * block, 4 * slots * block * (2 * block + rows)),
        name="left",
    )(offsets, step, base, *turned, *sources)


def finish_kernel(factor, offs_ref, step_ref, base_ref, keep_ref, other_ref, out_ref):
    del base_ref
    slot = pl.program_id(0)
    step_size = step_ref[0]
    stepped = keep_ref[...] - (step_size * factor) * other_ref[...]
    bound = step_size * penalty_weight
    shrunk = stepped - jnp.clip(stepped, -bound, bound)
    out_ref[...] = jnp.where(offs_ref[0, slot + 1] > 0, shrunk, 0.0)


def finish(offsets, step, base, keep, other, factor):
    slots, half, block = keep.shape
    spec = pl.BlockSpec((None, half, block), lambda j: (j, 0, 0))
    return pl.pallas_call(
        functools.partial(finish_kernel, factor),
        grid=(slots,),
        in_specs=[smem_spec(), smem_spec(), any_spec(), spec, spec],
        out_specs=pl.BlockSpec((None, half, block), lambda j: (j + 1, 0, 0)),
        out_shape=jax.ShapeDtypeStruct(base.shape, f32),
        input_output_aliases={2: 0},
        compiler_params=params(),
        cost_estimate=cost(6 * keep.size, 12 * keep.size),
        name="finish",
    )(offsets, step, base, keep, other)


def swap(value):
    return lax.ppermute(value, "samp", [(0, 1), (1, 0)])


def shards(data, tiles, offsets, step):
    local_tiles = tiles[0]
    slot_count, block = local_tiles.shape[:2]
    samp_count = lax.axis_size("samp")
    pair = samp_count == 2
    factor = 1.0 / (2.0 * data.shape[0] * samp_count)
    step_size = step[0]

    offsets_next = send(offsets, "last")
    data_first = send(data, "first")
    data_group = send(data, "group")
    own, far = forward(data, local_tiles)
    theirs = send(far, "last")
    data_both = send(data_first, "group")
    data_two = send(data_group, "two")
    data_last = send(choose(offsets_next, data, data_first, data_group, data_both, data_two), "last")
    data_sources = (data, data_first, data_group, data_both, data_last)

    own, bin_first, bin_group, bin_both, bin_two = make_bins(offsets, offsets_next, own, far, theirs)
    bin_group = bin_group + send(bin_both, "first") + send(bin_two, "two", reverse=True)
    got_first = send(bin_first, "first")
    got_group = send(bin_group, "group", reverse=True)
    image = own + backward(offsets, local_tiles, data_sources) + got_first + got_group

    image_group = send(image, "group")
    image_first = send(image, "first")
    image_both = send(image_group, "first")
    image_two = send(image_group, "two")
    image_last = send(choose(offsets_next, image, image_first, image_group, image_both, image_two), "last")
    image_sources = (image, image_first, image_group, image_both, image_last)

    keep, other, high, low = right(offsets, data, image, data_sources, pair)
    if pair:
        summed = keep + swap(other)
    else:
        summed = lax.psum_scatter(jnp.concatenate([keep, other], axis=1), "samp", scatter_dimension=1, tiled=True)
    row_count = block // samp_count
    row_start = lax.axis_index("samp") * row_count
    old_rows = lax.dynamic_slice_in_dim(local_tiles, row_start, row_count, 1)
    base = old_rows - (step_size * factor) * summed
    row_ids = row_start + lax.broadcasted_iota(jnp.int32, (row_count, block), 0)
    on_diag = row_ids == lax.broadcasted_iota(jnp.int32, (row_count, block), 1)
    bound = step_size * penalty_weight

    def shrink(value):
        return value - jnp.clip(value, -bound, bound)

    diagonal = jnp.where(on_diag, base[0] + step_size / jnp.where(on_diag, old_rows[0], 1.0), shrink(base[0]))
    base = jnp.concatenate([diagonal[None], base[1:]], axis=0)
    keep, other = left(offsets, step, base, (high, low), image_sources, factor, pair)
    if pair:
        return finish(offsets, step, base, keep, swap(other), factor)[None]
    summed = lax.psum_scatter(jnp.concatenate([keep, other], axis=1), "samp", scatter_dimension=1, tiled=True)
    live = (offsets[0, 1:] > 0)[:, None, None]
    stepped = base[1:] - (step_size * factor) * summed
    return jnp.concatenate([base[:1], jnp.where(live, shrink(stepped), 0.0)], axis=0)[None]


def solution(mesh):
    return jax.shard_map(
        shards,
        mesh=mesh,
        in_specs=(P("samp", "var"), P("var", None, None, None), P("var", None), P()),
        out_specs=P("var", None, "samp", None),
        check_vma=False,
    )
```

```python
import functools

import jax
import jax.numpy as jnp
from jax import lax
from jax.experimental import pallas as pl
from jax.experimental.pallas import tpu as pltpu
from jax.sharding import PartitionSpec as P

penalty_weight = 0.05
BAND = 6
VMEM_LIMIT = 48 * 1024 * 1024
NN = (((1,), (0,)), ((), ()))
NT = (((1,), (1,)), ((), ()))
f32, bf16 = jnp.float32, jnp.bfloat16


def params(**kw):
    return pltpu.CompilerParams(vmem_limit_bytes=VMEM_LIMIT, **kw)


def cost(flops, nbytes):
    return pl.CostEstimate(flops=0, bytes_accessed=0, transcendentals=0)


def any_spec():
    return pl.BlockSpec(memory_space=pl.ANY)


def vmem_spec():
    return pl.BlockSpec(memory_space=pltpu.VMEM)


def smem_spec():
    return pl.BlockSpec(memory_space=pltpu.SMEM)


def split(value):
    high = value.astype(bf16)
    return high, (value - high.astype(f32)).astype(bf16)


def dot3(left, right, dims):
    dot = functools.partial(lax.dot_general, dimension_numbers=dims, preferred_element_type=f32)
    return dot(left[0], right[0]) + (dot(left[0], right[1]) + dot(left[1], right[0]))


def route(p, k, flip):
    xbit = k & 1
    ybit = (((p + k) >> 1) ^ (p >> 1)) & 1
    first = jnp.where(flip == 0, xbit, ybit)
    last = jnp.where(flip == 0, ybit, xbit)
    return last, first + 2 * ((p + k) >> 2)


def place():
    return lax.axis_index("var") & 3, lax.axis_index("samp") & 1


def last_partner(p, flip):
    return jnp.where(flip == 0, p ^ 2, p ^ 1)


def wanted(first, last, groups):
    found = set()
    for p in range(4):
        for k in range(1, BAND):
            bits = p ^ ((p + k) & 3)
            if bits & first and (p + k) >> 2 == groups:
                found.add(p ^ (bits & last))
    return found


def hop(var_count, samp_count, kind, reverse=False):
    pairs = []
    for var in range(var_count):
        for samp in range(samp_count):
            first, last = (2, 1) if samp & 1 else (1, 2)
            back = (var - 4) % var_count
            use = True
            if kind == "all first":
                target = var ^ first
            elif kind == "first":
                target = var ^ first
                use = (target & 3) in wanted(first, last, 0)
            elif kind == "both":
                target = var ^ first
                use = (target & 3) in wanted(first, last, 1)
            elif kind == "last":
                target = var ^ last
            elif kind == "group":
                target = back
            elif kind == "two":
                target = back ^ first
                use = (var & 3) == 0
            elif kind == "column":
                target = back
                use = (var & 3) in wanted(first, last, 2)
            else:
                target = back ^ last
                use = (var & 3) in wanted(first, last, 2)
            pair = (var * samp_count + samp, target * samp_count + samp)
            if use:
                pairs.append(pair[::-1] if reverse else pair)
    return pairs


def send(value, kind, reverse=False):
    pairs = hop(lax.axis_size("var"), lax.axis_size("samp"), kind, reverse)
    return lax.ppermute(value, ("var", "samp"), pairs)


def forward_kernel(gate_ref, data_ref, tile_ref, own_ref, far_ref):
    del gate_ref
    slot = pl.program_id(0)
    value = dot3(split(data_ref[...]), split(tile_ref[...]), NN)

    @pl.when(slot == 0)
    def _():
        own_ref[...] = value

    @pl.when(slot > 0)
    def _():
        far_ref[...] = value


def forward(gate, data, tiles):
    slots, block = tiles.shape[:2]
    rows = data.shape[0]
    return pl.pallas_call(
        forward_kernel,
        grid=(slots,),
        in_specs=[
            smem_spec(),
            pl.BlockSpec((rows, block), lambda j: (0, 0)),
            pl.BlockSpec((None, block, block), lambda j: (j, 0, 0)),
        ],
        out_specs=[
            pl.BlockSpec((rows, block), lambda j: (0, 0)),
            pl.BlockSpec((None, rows, block), lambda j: (jnp.maximum(j - 1, 0), 0, 0)),
        ],
        out_shape=[
            jax.ShapeDtypeStruct((rows, block), f32),
            jax.ShapeDtypeStruct((slots - 1, rows, block), f32),
        ],
        compiler_params=params(),
        cost_estimate=cost(6 * slots * rows * block * block, 4 * slots * block * (block + 2 * rows)),
        name="forward",
    )(gate, data, tiles)


CODES = (0, 1, 2, 3, 5)


def choose_kernel(slots, count, offs_ref, *refs):
    sources, outs, sems = refs[:count], refs[count:-1], refs[-1]
    p, flip = place()
    target = last_partner(p, flip)
    copies = []
    for slot in range(slots):
        last, code = route(target, offs_ref[0, slot + 1], flip)
        for value, source in zip(CODES, sources):
            copy = pltpu.make_async_copy(source, outs[slot], sems.at[slot])
            pl.when((last == 1) & (code == value))(copy.start)
        known = (last == 1) & (code <= CODES[count - 1])
        copies.append((known, pltpu.make_async_copy(sources[0], outs[slot], sems.at[slot])))
    for known, copy in copies:
        pl.when(known)(copy.wait)


def choose(offsets_next, *sources):
    slots = offsets_next.shape[1] - 1
    own = sources[0]
    return pl.pallas_call(
        functools.partial(choose_kernel, slots, len(sources)),
        in_specs=[smem_spec()] + [any_spec()] * len(sources),
        out_specs=[any_spec()] * slots,
        out_shape=[jax.ShapeDtypeStruct(own.shape, f32)] * slots,
        scratch_shapes=[pltpu.SemaphoreType.DMA((slots,))],
        compiler_params=params(),
        cost_estimate=cost(0, 8 * slots * own.size),
        name="choose",
    )(offsets_next, *sources)


def start_pick(offset, sources, target, sem):
    p, flip = place()
    last, code = route(p, offset, flip)
    for value, source in zip(CODES, sources[:4]):
        pl.when((last == 0) & (code == value))(pltpu.make_async_copy(source, target, sem).start)
    over_last = last == 1
    if len(sources) > 5:
        over_last = over_last & (code != CODES[4])
        pl.when(code == CODES[4])(pltpu.make_async_copy(sources[5], target, sem).start)
    pl.when(over_last)(pltpu.make_async_copy(sources[4], target, sem).start)


def backward_kernel(slots, offs_ref, tile_ref, own, first, group, both, *refs):
    lasts = refs[:slots]
    out_ref, picked, sems = refs[slots:]
    slot = pl.program_id(0)

    @pl.when(slot == 0)
    def _():
        out_ref[...] = jnp.zeros_like(out_ref)
        for each in range(slots):
            sources = (own, first, group, both, lasts[each])
            start_pick(offs_ref[0, each + 1], sources, picked.at[each], sems.at[each])

    pltpu.make_async_copy(own, picked.at[slot], sems.at[slot]).wait()
    mirror = jnp.where(offs_ref[0, slot + 1] > 0, 1.0, 0.0).astype(f32)
    out_ref[...] += mirror * dot3(split(picked[slot]), split(tile_ref[...]), NT)


def backward(offsets, tiles, sources):
    slots, block = tiles.shape[0] - 1, tiles.shape[1]
    own = sources[0]
    rows = own.shape[0]
    return pl.pallas_call(
        functools.partial(backward_kernel, slots),
        grid=(slots,),
        in_specs=[smem_spec(), pl.BlockSpec((None, block, block), lambda j: (j + 1, 0, 0))]
        + [any_spec()] * len(sources),
        out_specs=pl.BlockSpec((rows, block), lambda j: (0, 0)),
        out_shape=jax.ShapeDtypeStruct((rows, block), f32),
        scratch_shapes=[pltpu.VMEM((slots, rows, block), f32), pltpu.SemaphoreType.DMA((slots,))],
        compiler_params=params(),
        cost_estimate=cost(6 * slots * rows * block * block, 4 * slots * block * (block + rows)),
        name="backward",
    )(offsets, tiles, *sources)


def bins_kernel(slots, offs_ref, next_ref, own_in, mine_ref, theirs_ref, own_out, first, group, both, two):
    p, flip = place()
    target = last_partner(p, flip)
    totals = [own_in[...], None, None, None, None]
    for which, value in enumerate((0, 1, 2, 3, 5)):
        total = totals[which]
        for slot in range(slots):
            for there, offs, source in ((0, offs_ref, mine_ref), (1, next_ref, theirs_ref)):
                offset = offs[0, slot + 1]
                last, code = route(jnp.where(there == 1, target, p), offset, flip)
                use = (last == there) & (code == value) & (offset > 0)
                term = jnp.where(use, source[slot], 0.0)
                total = term if total is None else total + term
        totals[which] = total
    for ref, total in zip((own_out, first, group, both, two), totals):
        ref[...] = total


def make_bins(offsets, offsets_next, own, mine, theirs):
    slots, rows, block = mine.shape
    step = rows // 4
    flat = pl.BlockSpec((step, block), lambda i: (i, 0))
    deep = pl.BlockSpec((slots, step, block), lambda i: (0, i, 0))
    return pl.pallas_call(
        functools.partial(bins_kernel, slots),
        grid=(rows // step,),
        in_specs=[smem_spec(), smem_spec(), flat, deep, deep],
        out_specs=[flat] * 5,
        out_shape=[jax.ShapeDtypeStruct((rows, block), f32)] * 5,
        compiler_params=params(),
        cost_estimate=cost(20 * rows * block, 40 * rows * block),
        name="bins",
    )(offsets, offsets_next, own, mine, theirs)


def halves(pair):
    return lax.axis_index("samp") if pair else 0


def right_kernel(slots, pair, offs_ref, data_ref, image_ref, own, first, group, both, *refs):
    lasts = refs[:slots]
    keep_ref, send_ref, high_ref, low_ref, picked, sems = refs[-6:]
    for slot in range(slots):
        sources = (own, first, group, both, lasts[slot])
        start_pick(offs_ref[0, slot + 1], sources, picked.at[slot], sems.at[slot])
    half = image_ref.shape[1] // 2
    samp = halves(pair)
    data = data_ref[...]
    image = image_ref[...]
    data_turned = split(data.T)
    high_ref[...], low_ref[...] = data_turned
    turned = split(image.T)
    image_pair, data_pair = split(image), split(data)

    def store(which, total):
        lower, upper = total[:half], total[half:]

        @pl.when(samp == 0)
        def _():
            keep_ref[which] = lower
            send_ref[which] = upper

        @pl.when(samp != 0)
        def _():
            keep_ref[which] = upper
            send_ref[which] = lower

    store(0, dot3(turned, data_pair, NN) + dot3(data_turned, image_pair, NN))
    for slot in range(slots):
        pltpu.make_async_copy(own, picked.at[slot], sems.at[slot]).wait()
        store(slot + 1, dot3(turned, split(picked[slot]), NN))


def right(offsets, data, image, gate, sources, pair):
    slots = offsets.shape[1] - 1
    rows, block = data.shape
    part = jax.ShapeDtypeStruct((slots + 1, block // 2, block), f32)
    turned = jax.ShapeDtypeStruct((block, rows), bf16)
    return pl.pallas_call(
        functools.partial(right_kernel, slots, pair),
        in_specs=[smem_spec(), vmem_spec(), vmem_spec()] + [any_spec()] * (len(gate) + len(sources)),
        out_specs=[vmem_spec()] * 4,
        out_shape=[part, part, turned, turned],
        scratch_shapes=[pltpu.VMEM((slots, rows, block), f32), pltpu.SemaphoreType.DMA((slots,))],
        compiler_params=params(),
        cost_estimate=cost(6 * (slots + 2) * rows * block * block, 4 * (slots + 1) * block * (block + rows)),
        name="right",
    )(offsets, data, image, *sources, *gate)


def left_kernel(start, begin, pair, offs_ref, keep_in, send_in, high_ref, low_ref, own, first, group, both, two, *refs):
    lasts = refs[:-4]
    keep_ref, send_ref, picked, sems = refs[-4:]
    slots = range(start, start + len(lasts))
    for slot, last_ref in zip(slots, lasts):
        sources = (own, first, group, both, last_ref, two)
        start_pick(offs_ref[0, slot], sources, picked.at[slot - start], sems.at[slot - start])
    half = send_ref.shape[1]
    samp = halves(pair)
    mine = samp * half
    yours = half - mine
    for slot in range(begin, start):
        keep_ref[slot - begin] = keep_in[slot]
        send_ref[slot - begin] = send_in[slot]
    for slot in slots:
        pltpu.make_async_copy(own, picked.at[slot - start], sems.at[slot - start]).wait()
        chosen = split(picked[slot - start])
        for out_ref, in_ref, row in ((send_ref, send_in, yours), (keep_ref, keep_in, mine)):
            rows = pl.ds(pl.multiple_of(row, half), half)
            out_ref[slot - begin] = in_ref[slot] + dot3((high_ref[rows], low_ref[rows]), chosen, NN)


def left(offsets, start, begin, parts, turned, sources, lasts, pair):
    keep = parts[0]
    block, rows = turned[0].shape
    count = start + len(lasts) - begin
    part = jax.ShapeDtypeStruct((count,) + keep.shape[1:], f32)
    return pl.pallas_call(
        functools.partial(left_kernel, start, begin, pair),
        in_specs=[smem_spec()] + [vmem_spec()] * 4 + [any_spec()] * (len(sources) + len(lasts)),
        out_specs=[vmem_spec()] * 2,
        out_shape=[part, part],
        scratch_shapes=[pltpu.VMEM((len(lasts), rows, block), f32), pltpu.SemaphoreType.DMA((len(lasts),))],
        compiler_params=params(),
        cost_estimate=cost(6 * len(lasts) * rows * block * block, 4 * count * block * (2 * block + rows)),
        name="left",
    )(offsets, *parts, *turned, *sources, *lasts)


def finish_kernel(begin, factor, offs_ref, step_ref, tile_ref, keep_ref, other_ref, *refs):
    out_ref = refs[-1]
    slot = pl.program_id(0) + begin
    half, block = out_ref.shape
    step_size = step_ref[0]
    old = tile_ref[...]
    bound = step_size * penalty_weight
    stepped = old - (step_size * factor) * (keep_ref[...] + other_ref[...])

    def shrunk(value):
        return value - jnp.clip(value, -bound, bound)

    @pl.when(slot == 0)
    def _():
        rows = lax.axis_index("samp") * half + lax.broadcasted_iota(jnp.int32, (half, block), 0)
        on_diag = rows == lax.broadcasted_iota(jnp.int32, (half, block), 1)
        out_ref[...] = jnp.where(on_diag, stepped + step_size / jnp.where(on_diag, old, 1.0), shrunk(stepped))

    @pl.when(slot > 0)
    def _():
        out_ref[...] = jnp.where(offs_ref[0, slot] > 0, shrunk(stepped), 0.0)


def finish(offsets, step, tiles, keep, other, factor, begin, earlier=()):
    slots, block = tiles.shape[:2]
    count, half = keep.shape[:2]
    spec = pl.BlockSpec((None, half, block), lambda j: (j, 0, 0))
    tile_spec = pl.BlockSpec((None, half, block), lambda j: (j + begin, lax.axis_index("samp"), 0))
    return pl.pallas_call(
        functools.partial(finish_kernel, begin, factor),
        grid=(count,),
        in_specs=[smem_spec(), smem_spec(), tile_spec, spec, spec] + [any_spec()] * len(earlier),
        out_specs=pl.BlockSpec((None, half, block), lambda j: (j + begin, 0, 0)),
        out_shape=jax.ShapeDtypeStruct((slots, half, block), f32),
        input_output_aliases={5: 0} if earlier else {},
        compiler_params=params(),
        cost_estimate=cost(6 * keep.size, 16 * keep.size),
        name="finish",
    )(offsets, step, tiles, keep, other, *earlier)


def after(value, other):
    return lax.optimization_barrier((value, other))[0]


def swap(value):
    return lax.ppermute(value, "samp", [(0, 1), (1, 0)])


def shards(data, tiles, offsets, step):
    local_tiles = tiles[0]
    slot_count, block = local_tiles.shape[:2]
    samp_count = lax.axis_size("samp")
    pair = samp_count == 2
    factor = 1.0 / (2.0 * data.shape[0] * samp_count)

    offsets_next = send(offsets, "last")
    data_first = send(data, "all first")
    data_group = send(data, "group")
    own, far = forward(offsets_next, after(data, data_first), local_tiles)
    theirs = send(far, "last")
    data_both = send(data_first, "group")
    own, bin_first, bin_group, bin_both, bin_two = make_bins(offsets, offsets_next, own, far, after(theirs, data_both))
    bin_group = bin_group + send(bin_both, "both", reverse=True) + send(bin_two, "two", reverse=True)
    data_two = send(after(data_both, own), "column")
    chosen = choose(offsets_next, data, data_first, data_group, data_both, data_two)
    data_sources = (data, data_first, data_group, data_both) + tuple(send(each, "last") for each in chosen)
    got_first = send(after(bin_first, bin_group), "first", reverse=True)
    got_group = send(bin_group, "group", reverse=True)
    image = own + backward(offsets, local_tiles, data_sources) + got_first + got_group

    image_group = send(image, "group")
    image_first = send(image, "first")
    image_group, image_first = lax.optimization_barrier((image_group, image_first))
    image_both = send(image_group, "both")
    chosen = choose(offsets_next, image, image_first, image_group, image_both)
    image_lasts = [send(each, "last") for each in chosen]
    image_two = send(after(image_both, chosen[0]), "direct")
    image_sources = (image, image_first, image_group, image_both, image_two)

    keep, other, high, low = right(offsets, data, image, (chosen[0],), data_sources, pair)
    if pair:
        begin, result = 0, ()
        for slot in range(1, slot_count):
            keep_now, other_now = left(
                offsets, slot, begin, (keep, other), (high, low), image_sources, image_lasts[slot - 1 : slot], pair)
            result = (finish(offsets, step, local_tiles, keep_now, swap(other_now), factor, begin, result),)
            begin = slot + 1
        return result[0][None]
    keep, other = left(offsets, 1, 0, (keep, other), (high, low), image_sources, image_lasts, pair)
    summed = lax.psum_scatter(jnp.concatenate([keep, other], axis=1), "samp", scatter_dimension=1, tiled=True)
    none = jnp.zeros_like(summed)
    return finish(offsets, step, local_tiles, summed, none, factor, 0)[None]


def solution(mesh):
    return jax.shard_map(
        shards,
        mesh=mesh,
        in_specs=(P("samp", "var"), P("var", None, None, None), P("var", None), P()),
        out_specs=P("var", None, "samp", None),
        check_vma=False,
    )
```

```python
import functools

import jax
import jax.numpy as jnp
from jax import lax
from jax.experimental import pallas as pl
from jax.experimental.pallas import tpu as pltpu
from jax.sharding import PartitionSpec as P

penalty_weight = 0.05
BAND = 6
VMEM_LIMIT = 48 * 1024 * 1024
NN = (((1,), (0,)), ((), ()))
NT = (((1,), (1,)), ((), ()))
f32, bf16 = jnp.float32, jnp.bfloat16


def params(**kw):
    return pltpu.CompilerParams(vmem_limit_bytes=VMEM_LIMIT, **kw)


def cost(flops, nbytes):
    return pl.CostEstimate(flops=0, bytes_accessed=0, transcendentals=0)


def any_spec():
    return pl.BlockSpec(memory_space=pl.ANY)


def vmem_spec():
    return pl.BlockSpec(memory_space=pltpu.VMEM)


def smem_spec():
    return pl.BlockSpec(memory_space=pltpu.SMEM)


def split(value):
    high = value.astype(bf16)
    return high, (value - high.astype(f32)).astype(bf16)


def dot3(left, right, dims):
    dot = functools.partial(lax.dot_general, dimension_numbers=dims, preferred_element_type=f32)
    return dot(left[0], right[0]) + (dot(left[0], right[1]) + dot(left[1], right[0]))


def route(p, k, flip):
    xbit = k & 1
    ybit = (((p + k) >> 1) ^ (p >> 1)) & 1
    first = jnp.where(flip == 0, xbit, ybit)
    last = jnp.where(flip == 0, ybit, xbit)
    return last, first + 2 * ((p + k) >> 2)


def place():
    return lax.axis_index("var") & 3, lax.axis_index("samp") & 1


def last_partner(p, flip):
    return jnp.where(flip == 0, p ^ 2, p ^ 1)


def wanted(first, last, groups):
    found = set()
    for p in range(4):
        for k in range(1, BAND):
            bits = p ^ ((p + k) & 3)
            if bits & first and (p + k) >> 2 == groups:
                found.add(p ^ (bits & last))
    return found


def hop(var_count, samp_count, kind, reverse=False):
    pairs = []
    for var in range(var_count):
        for samp in range(samp_count):
            first, last = (2, 1) if samp & 1 else (1, 2)
            back = (var - 4) % var_count
            use = True
            if kind == "first":
                target = var ^ first
            elif kind == "last":
                target = var ^ last
            elif kind == "group":
                target = back
            elif kind == "two":
                target = back ^ first
                use = (var & 3) == 0
            elif kind == "column":
                target = back
                use = (var & 3) in wanted(first, last, 2)
            else:
                target = back ^ last
                use = (var & 3) in wanted(first, last, 2)
            if kind == "column" and not use:
                target, use = var, True
            pair = (var * samp_count + samp, target * samp_count + samp)
            if use:
                pairs.append(pair[::-1] if reverse else pair)
    return pairs


def send(value, kind, reverse=False):
    pairs = hop(lax.axis_size("var"), lax.axis_size("samp"), kind, reverse)
    return lax.ppermute(value, ("var", "samp"), pairs)


def forward_kernel(gate_ref, data_ref, tile_ref, own_ref, far_ref):
    del gate_ref
    slot = pl.program_id(0)
    value = dot3(split(data_ref[...]), split(tile_ref[...]), NN)

    @pl.when(slot == 0)
    def _():
        own_ref[...] = value

    @pl.when(slot > 0)
    def _():
        far_ref[...] = value


def forward(gate, data, tiles):
    slots, block = tiles.shape[:2]
    rows = data.shape[0]
    return pl.pallas_call(
        forward_kernel,
        grid=(slots,),
        in_specs=[
            smem_spec(),
            pl.BlockSpec((rows, block), lambda j: (0, 0)),
            pl.BlockSpec((None, block, block), lambda j: (j, 0, 0)),
        ],
        out_specs=[
            pl.BlockSpec((rows, block), lambda j: (0, 0)),
            pl.BlockSpec((None, rows, block), lambda j: (jnp.maximum(j - 1, 0), 0, 0)),
        ],
        out_shape=[
            jax.ShapeDtypeStruct((rows, block), f32),
            jax.ShapeDtypeStruct((slots - 1, rows, block), f32),
        ],
        compiler_params=params(),
        cost_estimate=cost(6 * slots * rows * block * block, 4 * slots * block * (block + 2 * rows)),
        name="forward",
    )(gate, data, tiles)


CODES = (0, 1, 2, 3, 5)


def choose_kernel(slots, count, offs_ref, *refs):
    sources, outs, sems = refs[:count], refs[count:-1], refs[-1]
    p, flip = place()
    target = last_partner(p, flip)
    copies = []
    for slot in range(slots):
        last, code = route(target, offs_ref[0, slot + 1], flip)
        for value, source in zip(CODES, sources):
            copy = pltpu.make_async_copy(source, outs[slot], sems.at[slot])
            pl.when((last == 1) & (code == value))(copy.start)
        known = (last == 1) & (code <= CODES[count - 1])
        copies.append((known, pltpu.make_async_copy(sources[0], outs[slot], sems.at[slot])))
    for known, copy in copies:
        pl.when(known)(copy.wait)


def choose(offsets_next, *sources):
    slots = offsets_next.shape[1] - 1
    own = sources[0]
    return pl.pallas_call(
        functools.partial(choose_kernel, slots, len(sources)),
        in_specs=[smem_spec()] + [any_spec()] * len(sources),
        out_specs=[any_spec()] * slots,
        out_shape=[jax.ShapeDtypeStruct(own.shape, f32)] * slots,
        scratch_shapes=[pltpu.SemaphoreType.DMA((slots,))],
        compiler_params=params(),
        cost_estimate=cost(0, 8 * slots * own.size),
        name="choose",
    )(offsets_next, *sources)


def start_pick(offset, sources, target, sem):
    p, flip = place()
    last, code = route(p, offset, flip)
    for value, source in zip(CODES, sources[:4]):
        pl.when((last == 0) & (code == value))(pltpu.make_async_copy(source, target, sem).start)
    over_last = last == 1
    if len(sources) > 5:
        over_last = over_last & (code != CODES[4])
        pl.when(code == CODES[4])(pltpu.make_async_copy(sources[5], target, sem).start)
    pl.when(over_last)(pltpu.make_async_copy(sources[4], target, sem).start)


def backward_kernel(slots, offs_ref, tile_ref, own, first, group, both, *refs):
    lasts = refs[:slots]
    out_ref, picked, sems = refs[slots:]
    slot = pl.program_id(0)

    @pl.when(slot == 0)
    def _():
        out_ref[...] = jnp.zeros_like(out_ref)
        for each in range(slots):
            sources = (own, first, group, both, lasts[each])
            start_pick(offs_ref[0, each + 1], sources, picked.at[each], sems.at[each])

    pltpu.make_async_copy(own, picked.at[slot], sems.at[slot]).wait()
    mirror = jnp.where(offs_ref[0, slot + 1] > 0, 1.0, 0.0).astype(f32)
    out_ref[...] += mirror * dot3(split(picked[slot]), split(tile_ref[...]), NT)


def backward(offsets, tiles, sources):
    slots, block = tiles.shape[0] - 1, tiles.shape[1]
    own = sources[0]
    rows = own.shape[0]
    return pl.pallas_call(
        functools.partial(backward_kernel, slots),
        grid=(slots,),
        in_specs=[smem_spec(), pl.BlockSpec((None, block, block), lambda j: (j + 1, 0, 0))]
        + [any_spec()] * len(sources),
        out_specs=pl.BlockSpec((rows, block), lambda j: (0, 0)),
        out_shape=jax.ShapeDtypeStruct((rows, block), f32),
        scratch_shapes=[pltpu.VMEM((slots, rows, block), f32), pltpu.SemaphoreType.DMA((slots,))],
        compiler_params=params(),
        cost_estimate=cost(6 * slots * rows * block * block, 4 * slots * block * (block + rows)),
        name="backward",
    )(offsets, tiles, *sources)


def bins_kernel(slots, offs_ref, next_ref, own_in, mine_ref, theirs_ref, own_out, first, group, both, two):
    p, flip = place()
    target = last_partner(p, flip)
    totals = [own_in[...], None, None, None, None]
    for which, value in enumerate((0, 1, 2, 3, 5)):
        total = totals[which]
        for slot in range(slots):
            for there, offs, source in ((0, offs_ref, mine_ref), (1, next_ref, theirs_ref)):
                offset = offs[0, slot + 1]
                last, code = route(jnp.where(there == 1, target, p), offset, flip)
                use = (last == there) & (code == value) & (offset > 0)
                term = jnp.where(use, source[slot], 0.0)
                total = term if total is None else total + term
        totals[which] = total
    for ref, total in zip((own_out, first, group, both, two), totals):
        ref[...] = total


def make_bins(offsets, offsets_next, own, mine, theirs):
    slots, rows, block = mine.shape
    step = rows // 4
    flat = pl.BlockSpec((step, block), lambda i: (i, 0))
    deep = pl.BlockSpec((slots, step, block), lambda i: (0, i, 0))
    return pl.pallas_call(
        functools.partial(bins_kernel, slots),
        grid=(rows // step,),
        in_specs=[smem_spec(), smem_spec(), flat, deep, deep],
        out_specs=[flat] * 5,
        out_shape=[jax.ShapeDtypeStruct((rows, block), f32)] * 5,
        compiler_params=params(),
        cost_estimate=cost(20 * rows * block, 40 * rows * block),
        name="bins",
    )(offsets, offsets_next, own, mine, theirs)


def halves(pair):
    return lax.axis_index("samp") if pair else 0


def right_kernel(slots, pair, offs_ref, data_ref, image_ref, own, first, group, both, *refs):
    lasts = refs[:slots]
    keep_ref, send_ref, high_ref, low_ref, picked, sems = refs[-6:]
    for slot in range(slots):
        sources = (own, first, group, both, lasts[slot])
        start_pick(offs_ref[0, slot + 1], sources, picked.at[slot], sems.at[slot])
    half = image_ref.shape[1] // 2
    samp = halves(pair)
    data = data_ref[...]
    image = image_ref[...]
    data_turned = split(data.T)
    high_ref[...], low_ref[...] = data_turned
    turned = split(image.T)
    image_pair, data_pair = split(image), split(data)

    def store(which, total):
        lower, upper = total[:half], total[half:]

        @pl.when(samp == 0)
        def _():
            keep_ref[which] = lower
            send_ref[which] = upper

        @pl.when(samp != 0)
        def _():
            keep_ref[which] = upper
            send_ref[which] = lower

    store(0, dot3(turned, data_pair, NN) + dot3(data_turned, image_pair, NN))
    for slot in range(slots):
        pltpu.make_async_copy(own, picked.at[slot], sems.at[slot]).wait()
        store(slot + 1, dot3(turned, split(picked[slot]), NN))


def right(offsets, data, image, gate, sources, pair):
    slots = offsets.shape[1] - 1
    rows, block = data.shape
    part = jax.ShapeDtypeStruct((slots + 1, block // 2, block), f32)
    turned = jax.ShapeDtypeStruct((block, rows), bf16)
    return pl.pallas_call(
        functools.partial(right_kernel, slots, pair),
        in_specs=[smem_spec(), vmem_spec(), vmem_spec()] + [any_spec()] * (len(gate) + len(sources)),
        out_specs=[vmem_spec()] * 4,
        out_shape=[part, part, turned, turned],
        scratch_shapes=[pltpu.VMEM((slots, rows, block), f32), pltpu.SemaphoreType.DMA((slots,))],
        compiler_params=params(),
        cost_estimate=cost(6 * (slots + 2) * rows * block * block, 4 * (slots + 1) * block * (block + rows)),
        name="right",
    )(offsets, data, image, *sources, *gate)


def left_kernel(start, begin, pair, offs_ref, keep_in, send_in, high_ref, low_ref, own, first, group, both, two, *refs):
    lasts = refs[:-4]
    keep_ref, send_ref, picked, sems = refs[-4:]
    slots = range(start, start + len(lasts))
    for slot, last_ref in zip(slots, lasts):
        sources = (own, first, group, both, last_ref, two)
        start_pick(offs_ref[0, slot], sources, picked.at[slot - start], sems.at[slot - start])
    half = send_ref.shape[1]
    samp = halves(pair)
    mine = samp * half
    yours = half - mine
    for slot in range(begin, start):
        keep_ref[slot - begin] = keep_in[slot]
        send_ref[slot - begin] = send_in[slot]
    for slot in slots:
        pltpu.make_async_copy(own, picked.at[slot - start], sems.at[slot - start]).wait()
        chosen = split(picked[slot - start])
        for out_ref, in_ref, row in ((send_ref, send_in, yours), (keep_ref, keep_in, mine)):
            rows = pl.ds(pl.multiple_of(row, half), half)
            out_ref[slot - begin] = in_ref[slot] + dot3((high_ref[rows], low_ref[rows]), chosen, NN)


def left(offsets, start, begin, parts, turned, sources, lasts, pair):
    keep = parts[0]
    block, rows = turned[0].shape
    count = start + len(lasts) - begin
    part = jax.ShapeDtypeStruct((count,) + keep.shape[1:], f32)
    return pl.pallas_call(
        functools.partial(left_kernel, start, begin, pair),
        in_specs=[smem_spec()] + [vmem_spec()] * 4 + [any_spec()] * (len(sources) + len(lasts)),
        out_specs=[vmem_spec()] * 2,
        out_shape=[part, part],
        scratch_shapes=[pltpu.VMEM((len(lasts), rows, block), f32), pltpu.SemaphoreType.DMA((len(lasts),))],
        compiler_params=params(),
        cost_estimate=cost(6 * len(lasts) * rows * block * block, 4 * count * block * (2 * block + rows)),
        name="left",
    )(offsets, *parts, *turned, *sources, *lasts)


def finish_kernel(begin, factor, offs_ref, step_ref, tile_ref, keep_ref, other_ref, *refs):
    out_ref = refs[-1]
    slot = pl.program_id(0) + begin
    half, block = out_ref.shape
    step_size = step_ref[0]
    old = tile_ref[...]
    bound = step_size * penalty_weight
    stepped = old - (step_size * factor) * (keep_ref[...] + other_ref[...])

    def shrunk(value):
        return value - jnp.clip(value, -bound, bound)

    @pl.when(slot == 0)
    def _():
        rows = lax.axis_index("samp") * half + lax.broadcasted_iota(jnp.int32, (half, block), 0)
        on_diag = rows == lax.broadcasted_iota(jnp.int32, (half, block), 1)
        out_ref[...] = jnp.where(on_diag, stepped + step_size / jnp.where(on_diag, old, 1.0), shrunk(stepped))

    @pl.when(slot > 0)
    def _():
        out_ref[...] = jnp.where(offs_ref[0, slot] > 0, shrunk(stepped), 0.0)


def finish(offsets, step, tiles, keep, other, factor, begin, earlier=()):
    slots, block = tiles.shape[:2]
    count, half = keep.shape[:2]
    spec = pl.BlockSpec((None, half, block), lambda j: (j, 0, 0))
    tile_spec = pl.BlockSpec((None, half, block), lambda j: (j + begin, lax.axis_index("samp"), 0))
    return pl.pallas_call(
        functools.partial(finish_kernel, begin, factor),
        grid=(count,),
        in_specs=[smem_spec(), smem_spec(), tile_spec, spec, spec] + [any_spec()] * len(earlier),
        out_specs=pl.BlockSpec((None, half, block), lambda j: (j + begin, 0, 0)),
        out_shape=jax.ShapeDtypeStruct((slots, half, block), f32),
        input_output_aliases={5: 0} if earlier else {},
        compiler_params=params(),
        cost_estimate=cost(6 * keep.size, 16 * keep.size),
        name="finish",
    )(offsets, step, tiles, keep, other, *earlier)


def after(value, other):
    return lax.optimization_barrier((value, other))[0]


def swap(value):
    return lax.ppermute(value, "samp", [(0, 1), (1, 0)])


def shards(data, tiles, offsets, step):
    local_tiles = tiles[0]
    slot_count, block = local_tiles.shape[:2]
    samp_count = lax.axis_size("samp")
    pair = samp_count == 2
    factor = 1.0 / (2.0 * data.shape[0] * samp_count)

    offsets_next = send(offsets, "last")
    data_first = send(data, "first")
    data_group = send(data, "group")
    own, far = forward(offsets_next, data, local_tiles)
    theirs = send(far, "last")
    data_both = send(after(data_first, data_group), "group")
    own, bin_first, bin_group, bin_both, bin_two = make_bins(offsets, offsets_next, own, far, theirs)
    bin_group = bin_group + send(bin_both, "first") + send(bin_two, "two", reverse=True)
    data_two = send(after(data_both, own), "column")
    chosen = choose(offsets_next, data, data_first, data_group, data_both, data_two)
    data_sources = (data, data_first, data_group, data_both) + tuple(send(each, "last") for each in chosen)
    got_first = send(after(bin_first, bin_group), "first")
    got_group = send(bin_group, "group", reverse=True)
    image = own + backward(offsets, local_tiles, data_sources) + got_first + got_group

    image_group = send(image, "group")
    image_first = send(image, "first")
    image_group, image_first = lax.optimization_barrier((image_group, image_first))
    image_both = send(image_group, "first")
    chosen = choose(offsets_next, image, image_first, image_group, image_both)
    image_lasts = [send(each, "last") for each in chosen]
    keep, other, high, low = right(offsets, data, image, (chosen[0],), data_sources, pair)
    image_two = send(after(image_both, image_lasts[0]), "direct")
    image_sources = (image, image_first, image_group, image_both, image_two)
    if pair:
        begin, result = 0, ()
        for slot in range(1, slot_count):
            keep_now, other_now = left(
                offsets, slot, begin, (keep, other), (high, low), image_sources, image_lasts[slot - 1 : slot], pair)
            result = (finish(offsets, step, local_tiles, keep_now, swap(other_now), factor, begin, result),)
            begin = slot + 1
        return result[0][None]
    keep, other = left(offsets, 1, 0, (keep, other), (high, low), image_sources, image_lasts, pair)
    summed = lax.psum_scatter(jnp.concatenate([keep, other], axis=1), "samp", scatter_dimension=1, tiled=True)
    none = jnp.zeros_like(summed)
    return finish(offsets, step, local_tiles, summed, none, factor, 0)[None]


def solution(mesh):
    return jax.shard_map(
        shards,
        mesh=mesh,
        in_specs=(P("samp", "var"), P("var", None, None, None), P("var", None), P()),
        out_specs=P("var", None, "samp", None),
        check_vma=False,
    )
```

```python
import functools

import jax
import jax.numpy as jnp
from jax import lax
from jax.experimental import pallas as pl
from jax.experimental.pallas import tpu as pltpu
from jax.sharding import PartitionSpec as P

penalty_weight = 0.05
BAND = 6
VMEM_LIMIT = 48 * 1024 * 1024
NN = (((1,), (0,)), ((), ()))
NT = (((1,), (1,)), ((), ()))
f32, bf16 = jnp.float32, jnp.bfloat16


def params(**kw):
    return pltpu.CompilerParams(vmem_limit_bytes=VMEM_LIMIT, **kw)


def cost(flops, nbytes):
    return pl.CostEstimate(flops=0, bytes_accessed=0, transcendentals=0)


def any_spec():
    return pl.BlockSpec(memory_space=pl.ANY)


def vmem_spec():
    return pl.BlockSpec(memory_space=pltpu.VMEM)


def smem_spec():
    return pl.BlockSpec(memory_space=pltpu.SMEM)


def split(value):
    high = value.astype(bf16)
    return high, (value - high.astype(f32)).astype(bf16)


def dot3(left, right, dims):
    dot = functools.partial(lax.dot_general, dimension_numbers=dims, preferred_element_type=f32)
    return dot(left[0], right[0]) + (dot(left[0], right[1]) + dot(left[1], right[0]))


def route(p, k, flip):
    xbit = k & 1
    ybit = (((p + k) >> 1) ^ (p >> 1)) & 1
    first = jnp.where(flip == 0, xbit, ybit)
    last = jnp.where(flip == 0, ybit, xbit)
    return last, first + 2 * ((p + k) >> 2)


def place():
    return lax.axis_index("var") & 3, lax.axis_index("samp") & 1


def last_partner(p, flip):
    return jnp.where(flip == 0, p ^ 2, p ^ 1)


def wanted(first, last, groups):
    found = set()
    for p in range(4):
        for k in range(1, BAND):
            bits = p ^ ((p + k) & 3)
            if bits & first and (p + k) >> 2 == groups:
                found.add(p ^ (bits & last))
    return found


def hop(var_count, samp_count, kind, reverse=False):
    pairs = []
    for var in range(var_count):
        for samp in range(samp_count):
            first, last = (2, 1) if samp & 1 else (1, 2)
            back = (var - 4) % var_count
            use = True
            if kind == "first":
                target = var ^ first
            elif kind == "last":
                target = var ^ last
            elif kind == "group":
                target = back
            elif kind == "two":
                target = back ^ first
                use = (var & 3) == 0
            elif kind == "column":
                target = back
                use = (var & 3) in wanted(first, last, 2)
            else:
                target = back ^ last
                use = (var & 3) in wanted(first, last, 2)
            if kind == "column" and not use:
                target, use = var, True
            pair = (var * samp_count + samp, target * samp_count + samp)
            if use:
                pairs.append(pair[::-1] if reverse else pair)
    return pairs


def send(value, kind, reverse=False):
    pairs = hop(lax.axis_size("var"), lax.axis_size("samp"), kind, reverse)
    return lax.ppermute(value, ("var", "samp"), pairs)


def forward_kernel(data_ref, tile_ref, own_ref, far_ref):
    slot = pl.program_id(0)
    value = dot3(split(data_ref[...]), split(tile_ref[...]), NN)

    @pl.when(slot == 0)
    def _():
        own_ref[...] = value

    @pl.when(slot > 0)
    def _():
        far_ref[...] = value


def forward(data, tiles):
    slots, block = tiles.shape[:2]
    rows = data.shape[0]
    return pl.pallas_call(
        forward_kernel,
        grid=(slots,),
        in_specs=[
            pl.BlockSpec((rows, block), lambda j: (0, 0)),
            pl.BlockSpec((None, block, block), lambda j: (j, 0, 0)),
        ],
        out_specs=[
            pl.BlockSpec((rows, block), lambda j: (0, 0)),
            pl.BlockSpec((None, rows, block), lambda j: (jnp.maximum(j - 1, 0), 0, 0)),
        ],
        out_shape=[
            jax.ShapeDtypeStruct((rows, block), f32),
            jax.ShapeDtypeStruct((slots - 1, rows, block), f32),
        ],
        compiler_params=params(),
        cost_estimate=cost(6 * slots * rows * block * block, 4 * slots * block * (block + 2 * rows)),
        name="forward",
    )(data, tiles)


CODES = (0, 1, 2, 3, 5)


def choose_kernel(slots, count, offs_ref, *refs):
    sources, (out, sems) = refs[:count], refs[count:]
    p, flip = place()
    target = last_partner(p, flip)
    copies = []
    for slot in range(slots):
        last, code = route(target, offs_ref[0, slot + 1], flip)
        for value, source in zip(CODES, sources):
            copy = pltpu.make_async_copy(source, out.at[slot], sems.at[slot])
            pl.when((last == 1) & (code == value))(copy.start)
        known = (last == 1) & (code <= CODES[count - 1])
        copies.append((known, pltpu.make_async_copy(sources[0], out.at[slot], sems.at[slot])))
    for known, copy in copies:
        pl.when(known)(copy.wait)


def choose(offsets_next, *sources):
    slots = offsets_next.shape[1] - 1
    own = sources[0]
    return pl.pallas_call(
        functools.partial(choose_kernel, slots, len(sources)),
        in_specs=[smem_spec()] + [any_spec()] * len(sources),
        out_specs=any_spec(),
        out_shape=jax.ShapeDtypeStruct((slots,) + own.shape, f32),
        scratch_shapes=[pltpu.SemaphoreType.DMA((slots,))],
        compiler_params=params(),
        cost_estimate=cost(0, 8 * slots * own.size),
        name="choose",
    )(offsets_next, *sources)


def start_pick(offset, sources, target, sem):
    p, flip = place()
    last, code = route(p, offset, flip)
    for value, source in zip(CODES, sources[:4]):
        pl.when((last == 0) & (code == value))(pltpu.make_async_copy(source, target, sem).start)
    over_last = last == 1
    if len(sources) > 5:
        over_last = over_last & (code != CODES[4])
        pl.when(code == CODES[4])(pltpu.make_async_copy(sources[5], target, sem).start)
    pl.when(over_last)(pltpu.make_async_copy(sources[4], target, sem).start)


def backward_kernel(slots, offs_ref, tile_ref, own, first, group, both, *refs):
    lasts_ref, out_ref, picked, sems = refs
    slot = pl.program_id(0)

    @pl.when(slot == 0)
    def _():
        out_ref[...] = jnp.zeros_like(out_ref)
        for each in range(slots):
            sources = (own, first, group, both, lasts_ref.at[each])
            start_pick(offs_ref[0, each + 1], sources, picked.at[each], sems.at[each])

    pltpu.make_async_copy(own, picked.at[slot], sems.at[slot]).wait()
    mirror = jnp.where(offs_ref[0, slot + 1] > 0, 1.0, 0.0).astype(f32)
    out_ref[...] += mirror * dot3(split(picked[slot]), split(tile_ref[...]), NT)


def backward(offsets, tiles, sources):
    slots, block = tiles.shape[0] - 1, tiles.shape[1]
    own = sources[0]
    rows = own.shape[0]
    return pl.pallas_call(
        functools.partial(backward_kernel, slots),
        grid=(slots,),
        in_specs=[smem_spec(), pl.BlockSpec((None, block, block), lambda j: (j + 1, 0, 0))]
        + [any_spec()] * len(sources),
        out_specs=pl.BlockSpec((rows, block), lambda j: (0, 0)),
        out_shape=jax.ShapeDtypeStruct((rows, block), f32),
        scratch_shapes=[pltpu.VMEM((slots, rows, block), f32), pltpu.SemaphoreType.DMA((slots,))],
        compiler_params=params(),
        cost_estimate=cost(6 * slots * rows * block * block, 4 * slots * block * (block + rows)),
        name="backward",
    )(offsets, tiles, *sources)


def bins_kernel(slots, offs_ref, next_ref, own_in, mine_ref, theirs_ref, own_out, first, group, both, two):
    p, flip = place()
    target = last_partner(p, flip)
    totals = [own_in[...], None, None, None, None]
    for which, value in enumerate((0, 1, 2, 3, 5)):
        total = totals[which]
        for slot in range(slots):
            for there, offs, source in ((0, offs_ref, mine_ref), (1, next_ref, theirs_ref)):
                offset = offs[0, slot + 1]
                last, code = route(jnp.where(there == 1, target, p), offset, flip)
                use = (last == there) & (code == value) & (offset > 0)
                term = jnp.where(use, source[slot], 0.0)
                total = term if total is None else total + term
        totals[which] = total
    for ref, total in zip((own_out, first, group, both, two), totals):
        ref[...] = total


def make_bins(offsets, offsets_next, own, mine, theirs):
    slots, rows, block = mine.shape
    step = rows // 4
    flat = pl.BlockSpec((step, block), lambda i: (i, 0))
    deep = pl.BlockSpec((slots, step, block), lambda i: (0, i, 0))
    return pl.pallas_call(
        functools.partial(bins_kernel, slots),
        grid=(rows // step,),
        in_specs=[smem_spec(), smem_spec(), flat, deep, deep],
        out_specs=[flat] * 5,
        out_shape=[jax.ShapeDtypeStruct((rows, block), f32)] * 5,
        compiler_params=params(),
        cost_estimate=cost(20 * rows * block, 40 * rows * block),
        name="bins",
    )(offsets, offsets_next, own, mine, theirs)


def halves(pair):
    return lax.axis_index("samp") if pair else 0


def right_kernel(slots, pair, offs_ref, data_ref, image_ref, own, first, group, both, *refs):
    lasts_ref = refs[0]
    keep_ref, send_ref, high_ref, low_ref, picked, sems = refs[-6:]
    for slot in range(slots):
        sources = (own, first, group, both, lasts_ref.at[slot])
        start_pick(offs_ref[0, slot + 1], sources, picked.at[slot], sems.at[slot])
    half = image_ref.shape[1] // 2
    samp = halves(pair)
    data = data_ref[...]
    image = image_ref[...]
    data_turned = split(data.T)
    high_ref[...], low_ref[...] = data_turned
    turned = split(image.T)
    image_pair, data_pair = split(image), split(data)

    def store(which, total):
        lower, upper = total[:half], total[half:]

        @pl.when(samp == 0)
        def _():
            keep_ref[which] = lower
            send_ref[which] = upper

        @pl.when(samp != 0)
        def _():
            keep_ref[which] = upper
            send_ref[which] = lower

    store(0, dot3(turned, data_pair, NN) + dot3(data_turned, image_pair, NN))
    for slot in range(slots):
        pltpu.make_async_copy(own, picked.at[slot], sems.at[slot]).wait()
        store(slot + 1, dot3(turned, split(picked[slot]), NN))


def right(offsets, data, image, gate, sources, pair):
    slots = offsets.shape[1] - 1
    rows, block = data.shape
    part = jax.ShapeDtypeStruct((slots + 1, block // 2, block), f32)
    turned = jax.ShapeDtypeStruct((block, rows), bf16)
    return pl.pallas_call(
        functools.partial(right_kernel, slots, pair),
        in_specs=[smem_spec(), vmem_spec(), vmem_spec()] + [any_spec()] * (len(gate) + len(sources)),
        out_specs=[vmem_spec()] * 4,
        out_shape=[part, part, turned, turned],
        scratch_shapes=[pltpu.VMEM((slots, rows, block), f32), pltpu.SemaphoreType.DMA((slots,))],
        compiler_params=params(),
        cost_estimate=pl.CostEstimate(flops=400 * rows * block * block, bytes_accessed=0, transcendentals=0),
        name="right",
    )(offsets, data, image, *sources, *gate)


def left_kernel(slots, begin, pair, offs_ref, keep_in, send_in, high_ref, low_ref, own, first, group, both, two,
                lasts_ref, keep_ref, send_ref, picked, sems):
    start = slots[0]
    for slot in slots:
        sources = (own, first, group, both, lasts_ref.at[slot - 1], two)
        start_pick(offs_ref[0, slot], sources, picked.at[slot - start], sems.at[slot - start])
    half = send_ref.shape[1]
    samp = halves(pair)
    mine = samp * half
    yours = half - mine
    for slot in range(begin, start):
        keep_ref[slot - begin] = keep_in[slot]
        send_ref[slot - begin] = send_in[slot]
    for slot in slots:
        pltpu.make_async_copy(own, picked.at[slot - start], sems.at[slot - start]).wait()
        chosen = split(picked[slot - start])
        for out_ref, in_ref, row in ((send_ref, send_in, yours), (keep_ref, keep_in, mine)):
            rows = pl.ds(pl.multiple_of(row, half), half)
            out_ref[slot - begin] = in_ref[slot] + dot3((high_ref[rows], low_ref[rows]), chosen, NN)


def left(offsets, slots, begin, parts, turned, sources, pair):
    keep = parts[0]
    block, rows = turned[0].shape
    count = slots[-1] + 1 - begin
    part = jax.ShapeDtypeStruct((count,) + keep.shape[1:], f32)
    return pl.pallas_call(
        functools.partial(left_kernel, slots, begin, pair),
        in_specs=[smem_spec()] + [vmem_spec()] * 4 + [any_spec()] * len(sources),
        out_specs=[vmem_spec()] * 2,
        out_shape=[part, part],
        scratch_shapes=[pltpu.VMEM((len(slots), rows, block), f32), pltpu.SemaphoreType.DMA((len(slots),))],
        compiler_params=params(),
        cost_estimate=cost(6 * len(slots) * rows * block * block, 4 * count * block * (2 * block + rows)),
        name="left",
    )(offsets, *parts, *turned, *sources)


def finish_kernel(begin, factor, offs_ref, step_ref, tile_ref, keep_ref, other_ref, *refs):
    out_ref = refs[-1]
    slot = pl.program_id(0) + begin
    half, block = out_ref.shape
    step_size = step_ref[0]
    old = tile_ref[...]
    bound = step_size * penalty_weight
    stepped = old - (step_size * factor) * (keep_ref[...] + other_ref[...])

    def shrunk(value):
        return value - jnp.clip(value, -bound, bound)

    @pl.when(slot == 0)
    def _():
        rows = lax.axis_index("samp") * half + lax.broadcasted_iota(jnp.int32, (half, block), 0)
        on_diag = rows == lax.broadcasted_iota(jnp.int32, (half, block), 1)
        out_ref[...] = jnp.where(on_diag, stepped + step_size / jnp.where(on_diag, old, 1.0), shrunk(stepped))

    @pl.when(slot > 0)
    def _():
        out_ref[...] = jnp.where(offs_ref[0, slot] > 0, shrunk(stepped), 0.0)


def finish(offsets, step, tiles, keep, other, factor, begin, earlier=()):
    slots, block = tiles.shape[:2]
    count, half = keep.shape[:2]
    spec = pl.BlockSpec((None, half, block), lambda j: (j, 0, 0))
    tile_spec = pl.BlockSpec((None, half, block), lambda j: (j + begin, lax.axis_index("samp"), 0))
    return pl.pallas_call(
        functools.partial(finish_kernel, begin, factor),
        grid=(count,),
        in_specs=[smem_spec(), smem_spec(), tile_spec, spec, spec] + [any_spec()] * len(earlier),
        out_specs=pl.BlockSpec((None, half, block), lambda j: (j + begin, 0, 0)),
        out_shape=jax.ShapeDtypeStruct((slots, half, block), f32),
        input_output_aliases={5: 0} if earlier else {},
        compiler_params=params(),
        cost_estimate=cost(6 * keep.size, 16 * keep.size),
        name="finish",
    )(offsets, step, tiles, keep, other, *earlier)


def after(value, other):
    return lax.optimization_barrier((value, other))[0]


def swap(value):
    return lax.ppermute(value, "samp", [(0, 1), (1, 0)])


def shards(data, tiles, offsets, step):
    local_tiles = tiles[0]
    slot_count, block = local_tiles.shape[:2]
    samp_count = lax.axis_size("samp")
    pair = samp_count == 2
    factor = 1.0 / (2.0 * data.shape[0] * samp_count)

    offsets_next = send(offsets, "last")
    data_first = send(data, "first")
    data_group = send(data, "group")
    own, far = forward(data, local_tiles)
    theirs = send(after(far, offsets_next), "last")
    data_both = send(after(data_first, data_group), "group")
    own, bin_first, bin_group, bin_both, bin_two = make_bins(offsets, offsets_next, own, far, theirs)
    bin_group = bin_group + send(bin_both, "first") + send(bin_two, "two", reverse=True)
    data_two = send(after(data_both, own), "column")
    chosen = choose(offsets_next, data, data_first, data_group, data_both, data_two)
    data_sources = (data, data_first, data_group, data_both, send(chosen, "last"))
    got_first = send(after(bin_first, bin_group), "first")
    got_group = send(bin_group, "group", reverse=True)
    image = own + backward(offsets, local_tiles, data_sources) + got_first + got_group

    image_group = send(image, "group")
    image_first = send(image, "first")
    image_both = send(image_group, "first")
    chosen = choose(offsets_next, image, image_first, image_group, image_both)
    image_last = send(chosen, "last")
    keep, other, high, low = right(offsets, data, image, (chosen,), data_sources, pair)
    image_two = send(after(image_both, chosen), "direct")
    image_sources = (image, image_first, image_group, image_both, image_two, image_last)
    if pair:
        begin, result = 0, ()
        for slot in range(1, slot_count):
            keep_now, other_now = left(
                offsets, (slot,), begin, (keep, other), (high, low), image_sources, pair)
            result = (finish(offsets, step, local_tiles, keep_now, swap(other_now), factor, begin, result),)
            begin = slot + 1
        return result[0][None]
    slots = tuple(range(1, slot_count))
    keep, other = left(offsets, slots, 0, (keep, other), (high, low), image_sources, pair)
    summed = lax.psum_scatter(jnp.concatenate([keep, other], axis=1), "samp", scatter_dimension=1, tiled=True)
    none = jnp.zeros_like(summed)
    return finish(offsets, step, local_tiles, summed, none, factor, 0)[None]


def solution(mesh):
    return jax.shard_map(
        shards,
        mesh=mesh,
        in_specs=(P("samp", "var"), P("var", None, None, None), P("var", None), P()),
        out_specs=P("var", None, "samp", None),
        check_vma=False,
    )
```

```python
import functools

import jax
import jax.numpy as jnp
from jax import lax
from jax.experimental import pallas as pl
from jax.experimental.pallas import tpu as pltpu
from jax.sharding import PartitionSpec as P

penalty_weight = 0.05
BAND = 6
VMEM_LIMIT = 48 * 1024 * 1024
NN = (((1,), (0,)), ((), ()))
NT = (((1,), (1,)), ((), ()))
f32, bf16 = jnp.float32, jnp.bfloat16


def params(**kw):
    return pltpu.CompilerParams(vmem_limit_bytes=VMEM_LIMIT, **kw)


def cost(flops, nbytes):
    return pl.CostEstimate(flops=0, bytes_accessed=0, transcendentals=0)


def any_spec():
    return pl.BlockSpec(memory_space=pl.ANY)


def vmem_spec():
    return pl.BlockSpec(memory_space=pltpu.VMEM)


def smem_spec():
    return pl.BlockSpec(memory_space=pltpu.SMEM)


def split(value):
    high = value.astype(bf16)
    return high, (value - high.astype(f32)).astype(bf16)


def dot3(left, right, dims):
    dot = functools.partial(lax.dot_general, dimension_numbers=dims, preferred_element_type=f32)
    return dot(left[0], right[0]) + (dot(left[0], right[1]) + dot(left[1], right[0]))


def route(p, k, flip):
    xbit = k & 1
    ybit = (((p + k) >> 1) ^ (p >> 1)) & 1
    first = jnp.where(flip == 0, xbit, ybit)
    last = jnp.where(flip == 0, ybit, xbit)
    return last, first + 2 * ((p + k) >> 2)


def place():
    return lax.axis_index("var") & 3, lax.axis_index("samp") & 1


def last_partner(p, flip):
    return jnp.where(flip == 0, p ^ 2, p ^ 1)


def wanted(first, last, groups):
    found = set()
    for p in range(4):
        for k in range(1, BAND):
            bits = p ^ ((p + k) & 3)
            if bits & first and (p + k) >> 2 == groups:
                found.add(p ^ (bits & last))
    return found


def hop(var_count, samp_count, kind, reverse=False):
    pairs = []
    for var in range(var_count):
        for samp in range(samp_count):
            first, last = (2, 1) if samp & 1 else (1, 2)
            back = (var - 4) % var_count
            use = True
            if kind == "first":
                target = var ^ first
            elif kind == "last":
                target = var ^ last
            elif kind == "group":
                target = back
            elif kind == "column":
                target = back
                use = (var & 3) in wanted(first, last, 2)
            else:
                target = back ^ last
                use = (var & 3) in wanted(first, last, 2)
            if kind == "column" and not use:
                target, use = var, True
            pair = (var * samp_count + samp, target * samp_count + samp)
            if use:
                pairs.append(pair[::-1] if reverse else pair)
    return pairs


def send(value, kind, reverse=False):
    pairs = hop(lax.axis_size("var"), lax.axis_size("samp"), kind, reverse)
    return lax.ppermute(value, ("var", "samp"), pairs)


def forward_kernel(data_ref, tile_ref, own_ref, far_ref):
    slot = pl.program_id(0)
    value = dot3(split(data_ref[...]), split(tile_ref[...]), NN)

    @pl.when(slot == 0)
    def _():
        own_ref[...] = value

    @pl.when(slot > 0)
    def _():
        far_ref[...] = value


def forward(data, tiles):
    slots, block = tiles.shape[:2]
    rows = data.shape[0]
    return pl.pallas_call(
        forward_kernel,
        grid=(slots,),
        in_specs=[
            pl.BlockSpec((rows, block), lambda j: (0, 0)),
            pl.BlockSpec((None, block, block), lambda j: (j, 0, 0)),
        ],
        out_specs=[
            pl.BlockSpec((rows, block), lambda j: (0, 0)),
            pl.BlockSpec((None, rows, block), lambda j: (jnp.maximum(j - 1, 0), 0, 0)),
        ],
        out_shape=[
            jax.ShapeDtypeStruct((rows, block), f32),
            jax.ShapeDtypeStruct((slots - 1, rows, block), f32),
        ],
        compiler_params=params(),
        cost_estimate=cost(6 * slots * rows * block * block, 4 * slots * block * (block + 2 * rows)),
        name="forward",
    )(data, tiles)


CODES = (0, 1, 2, 3, 5)


def choose_kernel(slots, count, offs_ref, *refs):
    sources, (out, sems) = refs[:count], refs[count:]
    p, flip = place()
    target = last_partner(p, flip)
    copies = []
    for slot in range(slots):
        last, code = route(target, offs_ref[0, slot + 1], flip)
        for value, source in zip(CODES, sources):
            copy = pltpu.make_async_copy(source, out.at[slot], sems.at[slot])
            pl.when((last == 1) & (code == value))(copy.start)
        known = (last == 1) & (code <= CODES[count - 1])
        copies.append((known, pltpu.make_async_copy(sources[0], out.at[slot], sems.at[slot])))
    for known, copy in copies:
        pl.when(known)(copy.wait)


def choose(offsets_next, *sources):
    slots = offsets_next.shape[1] - 1
    own = sources[0]
    return pl.pallas_call(
        functools.partial(choose_kernel, slots, len(sources)),
        in_specs=[smem_spec()] + [any_spec()] * len(sources),
        out_specs=any_spec(),
        out_shape=jax.ShapeDtypeStruct((slots,) + own.shape, f32),
        scratch_shapes=[pltpu.SemaphoreType.DMA((slots,))],
        compiler_params=params(),
        cost_estimate=cost(0, 8 * slots * own.size),
        name="choose",
    )(offsets_next, *sources)


def start_pick(offset, sources, target, sem):
    p, flip = place()
    last, code = route(p, offset, flip)
    for value, source in zip(CODES, sources[:4]):
        pl.when((last == 0) & (code == value))(pltpu.make_async_copy(source, target, sem).start)
    over_last = last == 1
    if len(sources) > 5:
        over_last = over_last & (code != CODES[4])
        pl.when(code == CODES[4])(pltpu.make_async_copy(sources[5], target, sem).start)
    pl.when(over_last)(pltpu.make_async_copy(sources[4], target, sem).start)


def backward_kernel(slots, offs_ref, tile_ref, own, first, group, both, *refs):
    lasts_ref, out_ref, picked, sems = refs
    slot = pl.program_id(0)

    @pl.when(slot == 0)
    def _():
        out_ref[...] = jnp.zeros_like(out_ref)
        for each in range(slots):
            sources = (own, first, group, both, lasts_ref.at[each])
            start_pick(offs_ref[0, each + 1], sources, picked.at[each], sems.at[each])

    pltpu.make_async_copy(own, picked.at[slot], sems.at[slot]).wait()
    mirror = jnp.where(offs_ref[0, slot + 1] > 0, 1.0, 0.0).astype(f32)
    out_ref[...] += mirror * dot3(split(picked[slot]), split(tile_ref[...]), NT)


def backward(offsets, tiles, sources):
    slots, block = tiles.shape[0] - 1, tiles.shape[1]
    own = sources[0]
    rows = own.shape[0]
    return pl.pallas_call(
        functools.partial(backward_kernel, slots),
        grid=(slots,),
        in_specs=[smem_spec(), pl.BlockSpec((None, block, block), lambda j: (j + 1, 0, 0))]
        + [any_spec()] * len(sources),
        out_specs=pl.BlockSpec((rows, block), lambda j: (0, 0)),
        out_shape=jax.ShapeDtypeStruct((rows, block), f32),
        scratch_shapes=[pltpu.VMEM((slots, rows, block), f32), pltpu.SemaphoreType.DMA((slots,))],
        compiler_params=params(),
        cost_estimate=cost(6 * slots * rows * block * block, 4 * slots * block * (block + rows)),
        name="backward",
    )(offsets, tiles, *sources)


def bins_kernel(slots, offs_ref, next_ref, own_in, mine_ref, theirs_ref, own_out, first, group, both, two):
    p, flip = place()
    target = last_partner(p, flip)
    totals = [own_in[...], None, None, None, None]
    for which, value in enumerate((0, 1, 2, 3, 5)):
        total = totals[which]
        for slot in range(slots):
            for there, offs, source in ((0, offs_ref, mine_ref), (1, next_ref, theirs_ref)):
                offset = offs[0, slot + 1]
                last, code = route(jnp.where(there == 1, target, p), offset, flip)
                use = (last == there) & (code == value) & (offset > 0)
                term = jnp.where(use, source[slot], 0.0)
                total = term if total is None else total + term
        totals[which] = total
    for ref, total in zip((own_out, first, group, both, two), totals):
        ref[...] = total


def make_bins(offsets, offsets_next, own, mine, theirs):
    slots, rows, block = mine.shape
    step = rows // 4
    flat = pl.BlockSpec((step, block), lambda i: (i, 0))
    deep = pl.BlockSpec((slots, step, block), lambda i: (0, i, 0))
    return pl.pallas_call(
        functools.partial(bins_kernel, slots),
        grid=(rows // step,),
        in_specs=[smem_spec(), smem_spec(), flat, deep, deep],
        out_specs=[flat] * 5,
        out_shape=[jax.ShapeDtypeStruct((rows, block), f32)] * 5,
        compiler_params=params(),
        cost_estimate=cost(20 * rows * block, 40 * rows * block),
        name="bins",
    )(offsets, offsets_next, own, mine, theirs)


def halves(pair):
    return lax.axis_index("samp") if pair else 0


def right_kernel(slots, pair, offs_ref, data_ref, image_ref, own, first, group, both, *refs):
    lasts_ref = refs[0]
    keep0_ref, send0_ref, keep_ref, send_ref, high_ref, low_ref, picked, sems = refs[-8:]
    for slot in range(slots):
        sources = (own, first, group, both, lasts_ref.at[slot])
        start_pick(offs_ref[0, slot + 1], sources, picked.at[slot], sems.at[slot])
    half = image_ref.shape[1] // 2
    samp = halves(pair)
    data = data_ref[...]
    image = image_ref[...]
    data_turned = split(data.T)
    high_ref[...], low_ref[...] = data_turned
    turned = split(image.T)
    image_pair, data_pair = split(image), split(data)

    def store(keep, send_out, which, total):
        lower, upper = total[:half], total[half:]

        @pl.when(samp == 0)
        def _():
            keep[which] = lower
            send_out[which] = upper

        @pl.when(samp != 0)
        def _():
            keep[which] = upper
            send_out[which] = lower

    store(keep0_ref, send0_ref, 0, dot3(turned, data_pair, NN) + dot3(data_turned, image_pair, NN))
    for slot in range(slots):
        pltpu.make_async_copy(own, picked.at[slot], sems.at[slot]).wait()
        store(keep_ref, send_ref, slot, dot3(turned, split(picked[slot]), NN))


def right(offsets, data, image, gate, sources, pair):
    slots = offsets.shape[1] - 1
    rows, block = data.shape
    part0 = jax.ShapeDtypeStruct((1, block // 2, block), f32)
    part = jax.ShapeDtypeStruct((slots, block // 2, block), f32)
    turned = jax.ShapeDtypeStruct((block, rows), bf16)
    return pl.pallas_call(
        functools.partial(right_kernel, slots, pair),
        in_specs=[smem_spec(), vmem_spec(), vmem_spec()] + [any_spec()] * (len(gate) + len(sources)),
        out_specs=[vmem_spec()] * 6,
        out_shape=[part0, part0, part, part, turned, turned],
        scratch_shapes=[pltpu.VMEM((slots, rows, block), f32), pltpu.SemaphoreType.DMA((slots,))],
        compiler_params=params(),
        cost_estimate=pl.CostEstimate(flops=400 * rows * block * block, bytes_accessed=0, transcendentals=0),
        name="right",
    )(offsets, data, image, *sources, *gate)


def left_kernel(slots, pair, offs_ref, keep_in, send_in, high_ref, low_ref, own, first, group, both, two, lasts_ref,
                keep_ref, send_ref, picked, sems):
    slot = pl.program_id(0)

    @pl.when(slot == 0)
    def _():
        for each in range(slots):
            sources = (own, first, group, both, lasts_ref.at[each], two)
            start_pick(offs_ref[0, each + 1], sources, picked.at[each], sems.at[each])

    pltpu.make_async_copy(own, picked.at[slot], sems.at[slot]).wait()
    half = send_ref.shape[0]
    mine = halves(pair) * half
    chosen = split(picked[slot])
    for out_ref, in_ref, row in ((send_ref, send_in, half - mine), (keep_ref, keep_in, mine)):
        rows = pl.ds(pl.multiple_of(row, half), half)
        out_ref[...] = in_ref[...] + dot3((high_ref[rows], low_ref[rows]), chosen, NN)


def left(offsets, parts, turned, sources, pair):
    keep = parts[0]
    slots, half = keep.shape[:2]
    block, rows = turned[0].shape
    spec = pl.BlockSpec((None, half, block), lambda j: (j, 0, 0))
    whole = pl.BlockSpec((block, rows), lambda j: (0, 0))
    part = jax.ShapeDtypeStruct(keep.shape, f32)
    return pl.pallas_call(
        functools.partial(left_kernel, slots, pair),
        grid=(slots,),
        in_specs=[smem_spec(), spec, spec, whole, whole] + [any_spec()] * len(sources),
        out_specs=[spec, spec],
        out_shape=[part, part],
        scratch_shapes=[pltpu.VMEM((slots, rows, block), f32), pltpu.SemaphoreType.DMA((slots,))],
        compiler_params=params(),
        cost_estimate=cost(6 * slots * rows * block * block, 4 * slots * block * (2 * block + rows)),
        name="left",
    )(offsets, *parts, *turned, *sources)


def finish_kernel(begin, factor, offs_ref, step_ref, tile_ref, keep_ref, other_ref, *refs):
    out_ref = refs[-1]
    slot = pl.program_id(0) + begin
    half, block = out_ref.shape
    step_size = step_ref[0]
    old = tile_ref[...]
    bound = step_size * penalty_weight
    stepped = old - (step_size * factor) * (keep_ref[...] + other_ref[...])

    def shrunk(value):
        return value - jnp.clip(value, -bound, bound)

    @pl.when(slot == 0)
    def _():
        rows = lax.axis_index("samp") * half + lax.broadcasted_iota(jnp.int32, (half, block), 0)
        on_diag = rows == lax.broadcasted_iota(jnp.int32, (half, block), 1)
        out_ref[...] = jnp.where(on_diag, stepped + step_size / jnp.where(on_diag, old, 1.0), shrunk(stepped))

    @pl.when(slot > 0)
    def _():
        out_ref[...] = jnp.where(offs_ref[0, slot] > 0, shrunk(stepped), 0.0)


def finish(offsets, step, tiles, keep, other, factor, begin, earlier=()):
    slots, block = tiles.shape[:2]
    count, half = keep.shape[:2]
    spec = pl.BlockSpec((None, half, block), lambda j: (j, 0, 0))
    tile_spec = pl.BlockSpec((None, half, block), lambda j: (j + begin, lax.axis_index("samp"), 0))
    return pl.pallas_call(
        functools.partial(finish_kernel, begin, factor),
        grid=(count,),
        in_specs=[smem_spec(), smem_spec(), tile_spec, spec, spec] + [any_spec()] * len(earlier),
        out_specs=pl.BlockSpec((None, half, block), lambda j: (j + begin, 0, 0)),
        out_shape=jax.ShapeDtypeStruct((slots, half, block), f32),
        input_output_aliases={5: 0} if earlier else {},
        compiler_params=params(),
        cost_estimate=cost(6 * keep.size, 16 * keep.size),
        name="finish",
    )(offsets, step, tiles, keep, other, *earlier)


def after(value, other):
    return lax.optimization_barrier((value, other))[0]


def swap(value):
    return lax.ppermute(value, "samp", [(0, 1), (1, 0)])


def shards(data, tiles, offsets, step):
    local_tiles = tiles[0]
    slot_count, block = local_tiles.shape[:2]
    samp_count = lax.axis_size("samp")
    pair = samp_count == 2
    factor = 1.0 / (2.0 * data.shape[0] * samp_count)

    offsets_next = send(offsets, "last")
    data_first = send(data, "first")
    data_group = send(data, "group")
    own, far = forward(data, local_tiles)
    theirs = send(after(far, (offsets_next, data_first)), "last")
    data_both = send(after(data_first, data_group), "group")
    own, bin_first, bin_group, bin_both, bin_two = make_bins(offsets, offsets_next, own, far, theirs)
    got_two = send(bin_two, "column", reverse=True)
    got_both = send(bin_both, "first")
    got_first = send(bin_first + got_two, "first")
    onward = (lax.axis_index("var") & 3) == 0
    bin_group = bin_group + got_both + jnp.where(onward, got_first, 0.0)
    data_two = send(after(data_both, own), "column")
    chosen = choose(offsets_next, data, data_first, data_group, data_both, data_two)
    data_sources = (data, data_first, data_group, data_both, send(chosen, "last"))
    got_group = send(bin_group, "group", reverse=True)
    image = own + backward(offsets, local_tiles, data_sources) + jnp.where(onward, 0.0, got_first) + got_group

    image_group = send(image, "group")
    image_first = send(image, "first")
    image_both = send(image_group, "first")
    chosen = choose(offsets_next, image, image_first, image_group, image_both)
    image_last = send(chosen, "last")
    keep0, other0, keep, other, high, low = right(offsets, data, image, (chosen,), data_sources, pair)
    image_two = send(after(image_both, chosen), "direct")
    image_sources = (image, image_first, image_group, image_both, image_two, image_last)

    keep, other = left(offsets, (keep, other), (high, low), image_sources, pair)
    if pair:
        result = finish(offsets, step, local_tiles, keep0, swap(other0), factor, 0)
        return finish(offsets, step, local_tiles, keep, swap(other), factor, 1, (result,))[None]
    keep, other = (jnp.concatenate(both) for both in ((keep0, keep), (other0, other)))
    summed = lax.psum_scatter(jnp.concatenate([keep, other], axis=1), "samp", scatter_dimension=1, tiled=True)
    none = jnp.zeros_like(summed)
    return finish(offsets, step, local_tiles, summed, none, factor, 0)[None]


def solution(mesh):
    return jax.shard_map(
        shards,
        mesh=mesh,
        in_specs=(P("samp", "var"), P("var", None, None, None), P("var", None), P()),
        out_specs=P("var", None, "samp", None),
        check_vma=False,
    )
```

```python
import functools

import jax
import jax.numpy as jnp
from jax import lax
from jax.experimental import pallas as pl
from jax.experimental.pallas import tpu as pltpu
from jax.sharding import PartitionSpec as P

penalty_weight = 0.05
BAND = 6
VMEM_LIMIT = 48 * 1024 * 1024
NN = (((1,), (0,)), ((), ()))
NT = (((1,), (1,)), ((), ()))
f32, bf16 = jnp.float32, jnp.bfloat16


def params(**kw):
    return pltpu.CompilerParams(vmem_limit_bytes=VMEM_LIMIT, **kw)


def cost(flops, nbytes):
    return pl.CostEstimate(flops=0, bytes_accessed=0, transcendentals=0)


def any_spec():
    return pl.BlockSpec(memory_space=pl.ANY)


def vmem_spec():
    return pl.BlockSpec(memory_space=pltpu.VMEM)


def smem_spec():
    return pl.BlockSpec(memory_space=pltpu.SMEM)


def split(value):
    high = value.astype(bf16)
    return high, (value - high.astype(f32)).astype(bf16)


def dot3(left, right, dims):
    dot = functools.partial(lax.dot_general, dimension_numbers=dims, preferred_element_type=f32)
    return dot(left[0], right[0]) + (dot(left[0], right[1]) + dot(left[1], right[0]))


def route(p, k, flip):
    xbit = k & 1
    ybit = (((p + k) >> 1) ^ (p >> 1)) & 1
    first = jnp.where(flip == 0, xbit, ybit)
    last = jnp.where(flip == 0, ybit, xbit)
    return last, first + 2 * ((p + k) >> 2)


def place():
    return lax.axis_index("var") & 3, lax.axis_index("samp") & 1


def last_partner(p, flip):
    return jnp.where(flip == 0, p ^ 2, p ^ 1)


def wanted(first, last, groups):
    found = set()
    for p in range(4):
        for k in range(1, BAND):
            bits = p ^ ((p + k) & 3)
            if bits & first and (p + k) >> 2 == groups:
                found.add(p ^ (bits & last))
    return found


def hop(var_count, samp_count, kind, reverse=False):
    pairs = []
    for var in range(var_count):
        for samp in range(samp_count):
            first, last = (2, 1) if samp & 1 else (1, 2)
            back = (var - 4) % var_count
            use = True
            if kind == "first":
                target = var ^ first
            elif kind == "last":
                target = var ^ last
            elif kind == "group":
                target = back
            elif kind == "column":
                target = back
                use = (var & 3) in wanted(first, last, 2)
            else:
                target = back ^ last
                use = (var & 3) in wanted(first, last, 2)
            if kind == "column" and not use:
                target, use = var, True
            pair = (var * samp_count + samp, target * samp_count + samp)
            if use:
                pairs.append(pair[::-1] if reverse else pair)
    return pairs


def send(value, kind, reverse=False):
    pairs = hop(lax.axis_size("var"), lax.axis_size("samp"), kind, reverse)
    return lax.ppermute(value, ("var", "samp"), pairs)


def forward_kernel(data_ref, tile_ref, own_ref, far_ref):
    slot = pl.program_id(0)
    value = dot3(split(data_ref[...]), split(tile_ref[...]), NN)

    @pl.when(slot == 0)
    def _():
        own_ref[...] = value

    @pl.when(slot > 0)
    def _():
        far_ref[...] = value


def forward(data, tiles):
    slots, block = tiles.shape[:2]
    rows = data.shape[0]
    return pl.pallas_call(
        forward_kernel,
        grid=(slots,),
        in_specs=[
            pl.BlockSpec((rows, block), lambda j: (0, 0)),
            pl.BlockSpec((None, block, block), lambda j: (j, 0, 0)),
        ],
        out_specs=[
            pl.BlockSpec((rows, block), lambda j: (0, 0)),
            pl.BlockSpec((None, rows, block), lambda j: (jnp.maximum(j - 1, 0), 0, 0)),
        ],
        out_shape=[
            jax.ShapeDtypeStruct((rows, block), f32),
            jax.ShapeDtypeStruct((slots - 1, rows, block), f32),
        ],
        compiler_params=params(),
        cost_estimate=cost(6 * slots * rows * block * block, 4 * slots * block * (block + 2 * rows)),
        name="forward",
    )(data, tiles)


CODES = (0, 1, 2, 3, 5)


def choose_kernel(slots, count, offs_ref, *refs):
    sources, (out, sems) = refs[:count], refs[count:]
    p, flip = place()
    target = last_partner(p, flip)
    copies = []
    for slot in range(slots):
        last, code = route(target, offs_ref[0, slot + 1], flip)
        for value, source in zip(CODES, sources):
            copy = pltpu.make_async_copy(source, out.at[slot], sems.at[slot])
            pl.when((last == 1) & (code == value))(copy.start)
        known = (last == 1) & (code <= CODES[count - 1])
        copies.append((known, pltpu.make_async_copy(sources[0], out.at[slot], sems.at[slot])))
    for known, copy in copies:
        pl.when(known)(copy.wait)


def choose(offsets_next, *sources):
    slots = offsets_next.shape[1] - 1
    own = sources[0]
    return pl.pallas_call(
        functools.partial(choose_kernel, slots, len(sources)),
        in_specs=[smem_spec()] + [any_spec()] * len(sources),
        out_specs=any_spec(),
        out_shape=jax.ShapeDtypeStruct((slots,) + own.shape, f32),
        scratch_shapes=[pltpu.SemaphoreType.DMA((slots,))],
        compiler_params=params(),
        cost_estimate=cost(0, 8 * slots * own.size),
        name="choose",
    )(offsets_next, *sources)


def start_pick(offset, sources, target, sem):
    p, flip = place()
    last, code = route(p, offset, flip)
    for value, source in zip(CODES, sources[:4]):
        pl.when((last == 0) & (code == value))(pltpu.make_async_copy(source, target, sem).start)
    over_last = last == 1
    if len(sources) > 5:
        over_last = over_last & (code != CODES[4])
        pl.when(code == CODES[4])(pltpu.make_async_copy(sources[5], target, sem).start)
    pl.when(over_last)(pltpu.make_async_copy(sources[4], target, sem).start)


def backward_kernel(slots, offs_ref, tile_ref, own, first, group, both, *refs):
    lasts_ref, out_ref, picked, sems = refs
    slot = pl.program_id(0)

    @pl.when(slot == 0)
    def _():
        out_ref[...] = jnp.zeros_like(out_ref)
        for each in range(slots):
            sources = (own, first, group, both, lasts_ref.at[each])
            start_pick(offs_ref[0, each + 1], sources, picked.at[each], sems.at[each])

    pltpu.make_async_copy(own, picked.at[slot], sems.at[slot]).wait()
    mirror = jnp.where(offs_ref[0, slot + 1] > 0, 1.0, 0.0).astype(f32)
    out_ref[...] += mirror * dot3(split(picked[slot]), split(tile_ref[...]), NT)


def backward(offsets, tiles, sources):
    slots, block = tiles.shape[0] - 1, tiles.shape[1]
    own = sources[0]
    rows = own.shape[0]
    return pl.pallas_call(
        functools.partial(backward_kernel, slots),
        grid=(slots,),
        in_specs=[smem_spec(), pl.BlockSpec((None, block, block), lambda j: (j + 1, 0, 0))]
        + [any_spec()] * (len(sources) - 1)
        + [vmem_spec()],
        out_specs=pl.BlockSpec((rows, block), lambda j: (0, 0)),
        out_shape=jax.ShapeDtypeStruct((rows, block), f32),
        scratch_shapes=[pltpu.VMEM((slots, rows, block), f32), pltpu.SemaphoreType.DMA((slots,))],
        compiler_params=params(),
        cost_estimate=cost(6 * slots * rows * block * block, 4 * slots * block * (block + rows)),
        name="backward",
    )(offsets, tiles, *sources)


def bins_kernel(slots, offs_ref, next_ref, own_in, mine_ref, theirs_ref, own_out, first, group, both, two):
    p, flip = place()
    target = last_partner(p, flip)
    totals = [own_in[...], None, None, None, None]
    for which, value in enumerate((0, 1, 2, 3, 5)):
        total = totals[which]
        for slot in range(slots):
            for there, offs, source in ((0, offs_ref, mine_ref), (1, next_ref, theirs_ref)):
                offset = offs[0, slot + 1]
                last, code = route(jnp.where(there == 1, target, p), offset, flip)
                use = (last == there) & (code == value) & (offset > 0)
                term = jnp.where(use, source[slot], 0.0)
                total = term if total is None else total + term
        totals[which] = total
    for ref, total in zip((own_out, first, group, both, two), totals):
        ref[...] = total


def make_bins(offsets, offsets_next, own, mine, theirs):
    slots, rows, block = mine.shape
    step = rows // 4
    flat = pl.BlockSpec((step, block), lambda i: (i, 0))
    deep = pl.BlockSpec((slots, step, block), lambda i: (0, i, 0))
    return pl.pallas_call(
        functools.partial(bins_kernel, slots),
        grid=(rows // step,),
        in_specs=[smem_spec(), smem_spec(), flat, deep, deep],
        out_specs=[flat] * 5,
        out_shape=[jax.ShapeDtypeStruct((rows, block), f32)] * 5,
        compiler_params=params(),
        cost_estimate=cost(20 * rows * block, 40 * rows * block),
        name="bins",
    )(offsets, offsets_next, own, mine, theirs)


def halves(pair):
    return lax.axis_index("samp") if pair else 0


def right_kernel(slots, pair, offs_ref, data_ref, image_ref, own, first, group, both, *refs):
    lasts_ref = refs[0]
    keep0_ref, send0_ref, keep_ref, send_ref, high_ref, low_ref, picked, sems = refs[-8:]
    for slot in range(slots):
        sources = (own, first, group, both, lasts_ref.at[slot])
        start_pick(offs_ref[0, slot + 1], sources, picked.at[slot], sems.at[slot])
    half = image_ref.shape[1] // 2
    samp = halves(pair)
    data = data_ref[...]
    image = image_ref[...]
    data_turned = split(data.T)
    high_ref[...], low_ref[...] = data_turned
    turned = split(image.T)
    image_pair, data_pair = split(image), split(data)

    def store(keep, send_out, which, total):
        lower, upper = total[:half], total[half:]

        @pl.when(samp == 0)
        def _():
            keep[which] = lower
            send_out[which] = upper

        @pl.when(samp != 0)
        def _():
            keep[which] = upper
            send_out[which] = lower

    store(keep0_ref, send0_ref, 0, dot3(turned, data_pair, NN) + dot3(data_turned, image_pair, NN))
    for slot in range(slots):
        pltpu.make_async_copy(own, picked.at[slot], sems.at[slot]).wait()
        store(keep_ref, send_ref, slot, dot3(turned, split(picked[slot]), NN))


def right(offsets, data, image, gate, sources, pair):
    slots = offsets.shape[1] - 1
    rows, block = data.shape
    part0 = jax.ShapeDtypeStruct((1, block // 2, block), f32)
    part = jax.ShapeDtypeStruct((slots, block // 2, block), f32)
    turned = jax.ShapeDtypeStruct((block, rows), bf16)
    return pl.pallas_call(
        functools.partial(right_kernel, slots, pair),
        in_specs=[smem_spec(), vmem_spec(), vmem_spec()] + [any_spec()] * (len(gate) + len(sources)),
        out_specs=[vmem_spec()] * 6,
        out_shape=[part0, part0, part, part, turned, turned],
        scratch_shapes=[pltpu.VMEM((slots, rows, block), f32), pltpu.SemaphoreType.DMA((slots,))],
        compiler_params=params(),
        cost_estimate=pl.CostEstimate(flops=400 * rows * block * block, bytes_accessed=0, transcendentals=0),
        name="right",
    )(offsets, data, image, *sources, *gate)


def left_kernel(slots, pair, offs_ref, keep_in, send_in, high_ref, low_ref, own, first, group, both, two, lasts_ref,
                keep_ref, send_ref, picked, sems):
    slot = pl.program_id(0)

    @pl.when(slot == 0)
    def _():
        for each in range(slots):
            sources = (own, first, group, both, lasts_ref.at[each], two)
            start_pick(offs_ref[0, each + 1], sources, picked.at[each], sems.at[each])

    pltpu.make_async_copy(own, picked.at[slot], sems.at[slot]).wait()
    half = send_ref.shape[0]
    mine = halves(pair) * half
    chosen = split(picked[slot])
    for out_ref, in_ref, row in ((send_ref, send_in, half - mine), (keep_ref, keep_in, mine)):
        rows = pl.ds(pl.multiple_of(row, half), half)
        out_ref[...] = in_ref[...] + dot3((high_ref[rows], low_ref[rows]), chosen, NN)


def left(offsets, parts, turned, sources, pair):
    keep = parts[0]
    slots, half = keep.shape[:2]
    block, rows = turned[0].shape
    spec = pl.BlockSpec((None, half, block), lambda j: (j, 0, 0))
    whole = pl.BlockSpec((block, rows), lambda j: (0, 0))
    part = jax.ShapeDtypeStruct(keep.shape, f32)
    return pl.pallas_call(
        functools.partial(left_kernel, slots, pair),
        grid=(slots,),
        in_specs=[smem_spec(), spec, spec, whole, whole] + [any_spec()] * (len(sources) - 1) + [vmem_spec()],
        out_specs=[spec, spec],
        out_shape=[part, part],
        scratch_shapes=[pltpu.VMEM((slots, rows, block), f32), pltpu.SemaphoreType.DMA((slots,))],
        compiler_params=params(),
        cost_estimate=cost(6 * slots * rows * block * block, 4 * slots * block * (2 * block + rows)),
        name="left",
    )(offsets, *parts, *turned, *sources)


def finish_kernel(begin, factor, offs_ref, step_ref, tile_ref, keep_ref, other_ref, *refs):
    out_ref = refs[-1]
    slot = pl.program_id(0) + begin
    half, block = out_ref.shape
    step_size = step_ref[0]
    old = tile_ref[...]
    bound = step_size * penalty_weight
    stepped = old - (step_size * factor) * (keep_ref[...] + other_ref[...])

    def shrunk(value):
        return value - jnp.clip(value, -bound, bound)

    @pl.when(slot == 0)
    def _():
        rows = lax.axis_index("samp") * half + lax.broadcasted_iota(jnp.int32, (half, block), 0)
        on_diag = rows == lax.broadcasted_iota(jnp.int32, (half, block), 1)
        out_ref[...] = jnp.where(on_diag, stepped + step_size / jnp.where(on_diag, old, 1.0), shrunk(stepped))

    @pl.when(slot > 0)
    def _():
        out_ref[...] = jnp.where(offs_ref[0, slot] > 0, shrunk(stepped), 0.0)


def finish(offsets, step, tiles, keep, other, factor, begin, earlier=()):
    slots, block = tiles.shape[:2]
    count, half = keep.shape[:2]
    spec = pl.BlockSpec((None, half, block), lambda j: (j, 0, 0))
    tile_spec = pl.BlockSpec((None, half, block), lambda j: (j + begin, lax.axis_index("samp"), 0))
    return pl.pallas_call(
        functools.partial(finish_kernel, begin, factor),
        grid=(count,),
        in_specs=[smem_spec(), smem_spec(), tile_spec, spec, spec] + [any_spec()] * len(earlier),
        out_specs=pl.BlockSpec((None, half, block), lambda j: (j + begin, 0, 0)),
        out_shape=jax.ShapeDtypeStruct((slots, half, block), f32),
        input_output_aliases={5: 0} if earlier else {},
        compiler_params=params(),
        cost_estimate=cost(6 * keep.size, 16 * keep.size),
        name="finish",
    )(offsets, step, tiles, keep, other, *earlier)


def after(value, other):
    return lax.optimization_barrier((value, other))[0]


def swap(value):
    return lax.ppermute(value, "samp", [(0, 1), (1, 0)])


def shards(data, tiles, offsets, step):
    local_tiles = tiles[0]
    slot_count, block = local_tiles.shape[:2]
    samp_count = lax.axis_size("samp")
    pair = samp_count == 2
    factor = 1.0 / (2.0 * data.shape[0] * samp_count)

    offsets_next = send(offsets, "last")
    data_first = send(data, "first")
    data_group = send(data, "group")
    own, far = forward(data, local_tiles)
    theirs = send(after(far, offsets_next), "last")
    data_both = send(after(data_first, data_group), "group")
    own, bin_first, bin_group, bin_both, bin_two = make_bins(offsets, offsets_next, own, far, theirs)
    got_two = send(bin_two, "column", reverse=True)
    got_both = send(bin_both + got_two, "group", reverse=True)
    got_group = send(after(bin_group, got_both), "group", reverse=True)
    data_two = send(data_both, "column")
    chosen = choose(offsets_next, data, data_first, data_group, data_both, data_two)
    data_sources = (data, data_first, data_group, data_both, send(chosen, "last"))
    got_first = send(bin_first + got_both, "first")
    image = own + backward(offsets, local_tiles, data_sources) + got_first + got_group

    image_group = send(image, "group")
    image_first = send(image, "first")
    image_both = send(image_group, "first")
    chosen = choose(offsets_next, image, image_first, image_group, image_both)
    image_last = send(chosen, "last")
    keep0, other0, keep, other, high, low = right(offsets, data, image, (chosen,), data_sources, pair)
    image_two = send(after(image_both, chosen), "direct")
    image_sources = (image, image_first, image_group, image_both, image_two, image_last)

    if pair:
        result = finish(offsets, step, local_tiles, keep0, swap(other0), factor, 0)
        keep = after(keep, result)
    keep, other = left(offsets, (keep, other), (high, low), image_sources, pair)
    if pair:
        return finish(offsets, step, local_tiles, keep, swap(other), factor, 1, (result,))[None]
    keep, other = (jnp.concatenate(both) for both in ((keep0, keep), (other0, other)))
    summed = lax.psum_scatter(jnp.concatenate([keep, other], axis=1), "samp", scatter_dimension=1, tiled=True)
    none = jnp.zeros_like(summed)
    return finish(offsets, step, local_tiles, summed, none, factor, 0)[None]


def solution(mesh):
    return jax.shard_map(
        shards,
        mesh=mesh,
        in_specs=(P("samp", "var"), P("var", None, None, None), P("var", None), P()),
        out_specs=P("var", None, "samp", None),
        check_vma=False,
    )
```

```python
import functools

import jax
import jax.numpy as jnp
from jax import lax
from jax.experimental import pallas as pl
from jax.experimental.pallas import tpu as pltpu
from jax.sharding import PartitionSpec as P

penalty_weight = 0.05
BAND = 6
VMEM_LIMIT = 48 * 1024 * 1024
NN = (((1,), (0,)), ((), ()))
NT = (((1,), (1,)), ((), ()))
f32, bf16 = jnp.float32, jnp.bfloat16


def params(**kw):
    return pltpu.CompilerParams(vmem_limit_bytes=VMEM_LIMIT, **kw)


def cost(flops, nbytes):
    return pl.CostEstimate(flops=0, bytes_accessed=0, transcendentals=0)


def any_spec():
    return pl.BlockSpec(memory_space=pl.ANY)


def vmem_spec():
    return pl.BlockSpec(memory_space=pltpu.VMEM)


def smem_spec():
    return pl.BlockSpec(memory_space=pltpu.SMEM)


def split(value):
    high = value.astype(bf16)
    return high, (value - high.astype(f32)).astype(bf16)


def dot3(left, right, dims):
    dot = functools.partial(lax.dot_general, dimension_numbers=dims, preferred_element_type=f32)
    return dot(left[0], right[0]) + (dot(left[0], right[1]) + dot(left[1], right[0]))


def route(p, k, flip):
    xbit = k & 1
    ybit = (((p + k) >> 1) ^ (p >> 1)) & 1
    first = jnp.where(flip == 0, xbit, ybit)
    last = jnp.where(flip == 0, ybit, xbit)
    return last, first + 2 * ((p + k) >> 2)


def place():
    return lax.axis_index("var") & 3, lax.axis_index("samp") & 1


def last_partner(p, flip):
    return jnp.where(flip == 0, p ^ 2, p ^ 1)


def wanted(first, last, groups):
    found = set()
    for p in range(4):
        for k in range(1, BAND):
            bits = p ^ ((p + k) & 3)
            if bits & first and (p + k) >> 2 == groups:
                found.add(p ^ (bits & last))
    return found


def hop(var_count, samp_count, kind, reverse=False):
    pairs = []
    for var in range(var_count):
        for samp in range(samp_count):
            first, last = (2, 1) if samp & 1 else (1, 2)
            back = (var - 4) % var_count
            use = True
            if kind == "first":
                target = var ^ first
            elif kind == "last":
                target = var ^ last
            elif kind == "group":
                target = back
            else:
                target = back ^ last
                use = (var & 3) in wanted(first, last, 2)
            pair = (var * samp_count + samp, target * samp_count + samp)
            if use:
                pairs.append(pair[::-1] if reverse else pair)
    return pairs


def send(value, kind, reverse=False):
    pairs = hop(lax.axis_size("var"), lax.axis_size("samp"), kind, reverse)
    return lax.ppermute(value, ("var", "samp"), pairs)


def forward_kernel(offs_ref, data_ref, tile_ref, own_ref, far_ref, two_ref):
    slot = pl.program_id(0)
    value = dot3(split(data_ref[...]), split(tile_ref[...]), NN)
    p, flip = place()
    code = route(p, offs_ref[0, slot], flip)[1]

    @pl.when(slot == 0)
    def _():
        own_ref[...] = value
        two_ref[...] = jnp.zeros_like(two_ref)

    @pl.when(slot > 0)
    def _():
        far_ref[...] = value

    @pl.when(code == CODES[4])
    def _():
        two_ref[...] = value


def forward(offsets, data, tiles):
    slots, block = tiles.shape[:2]
    rows = data.shape[0]
    flat = pl.BlockSpec((rows, block), lambda j: (0, 0))
    return pl.pallas_call(
        forward_kernel,
        grid=(slots,),
        in_specs=[smem_spec(), flat, pl.BlockSpec((None, block, block), lambda j: (j, 0, 0))],
        out_specs=[flat, pl.BlockSpec((None, rows, block), lambda j: (jnp.maximum(j - 1, 0), 0, 0)), flat],
        out_shape=[
            jax.ShapeDtypeStruct((rows, block), f32),
            jax.ShapeDtypeStruct((slots - 1, rows, block), f32),
            jax.ShapeDtypeStruct((rows, block), f32),
        ],
        compiler_params=params(),
        cost_estimate=cost(6 * slots * rows * block * block, 4 * slots * block * (block + 2 * rows)),
        name="forward",
    )(offsets, data, tiles)


CODES = (0, 1, 2, 3, 5)


def choose_kernel(slots, count, offs_ref, *refs):
    sources, (out, sems) = refs[:count], refs[count:]
    p, flip = place()
    target = last_partner(p, flip)
    copies = []
    for slot in range(slots):
        last, code = route(target, offs_ref[0, slot + 1], flip)
        for value, source in zip(CODES, sources):
            copy = pltpu.make_async_copy(source, out.at[slot], sems.at[slot])
            pl.when((last == 1) & (code == value))(copy.start)
        known = (last == 1) & (code < CODES[4])
        copies.append((known, pltpu.make_async_copy(sources[0], out.at[slot], sems.at[slot])))
    for known, copy in copies:
        pl.when(known)(copy.wait)


def choose(offsets_next, *sources):
    slots = offsets_next.shape[1] - 1
    own = sources[0]
    return pl.pallas_call(
        functools.partial(choose_kernel, slots, len(sources)),
        in_specs=[smem_spec()] + [any_spec()] * len(sources),
        out_specs=any_spec(),
        out_shape=jax.ShapeDtypeStruct((slots,) + own.shape, f32),
        scratch_shapes=[pltpu.SemaphoreType.DMA((slots,))],
        compiler_params=params(),
        cost_estimate=cost(0, 8 * slots * own.size),
        name="choose",
    )(offsets_next, *sources)


def start_pick(offset, sources, target, sem):
    p, flip = place()
    last, code = route(p, offset, flip)
    for value, source in zip(CODES[:4], sources[:4]):
        pl.when((last == 0) & (code == value))(pltpu.make_async_copy(source, target, sem).start)
    two, lasts = sources[4:]
    pl.when(code == CODES[4])(pltpu.make_async_copy(two, target, sem).start)
    pl.when((last == 1) & (code != CODES[4]))(pltpu.make_async_copy(lasts, target, sem).start)


def backward_kernel(slots, offs_ref, tile_ref, own, first, group, both, two, *refs):
    lasts_ref, out_ref, picked, sems = refs
    slot = pl.program_id(0)

    @pl.when(slot == 0)
    def _():
        out_ref[...] = jnp.zeros_like(out_ref)
        for each in range(slots):
            sources = (own, first, group, both, two, lasts_ref.at[each])
            start_pick(offs_ref[0, each + 1], sources, picked.at[each], sems.at[each])

    pltpu.make_async_copy(own, picked.at[slot], sems.at[slot]).wait()
    mirror = jnp.where(offs_ref[0, slot + 1] > 0, 1.0, 0.0).astype(f32)
    out_ref[...] += mirror * dot3(split(picked[slot]), split(tile_ref[...]), NT)


def backward(offsets, tiles, sources):
    slots, block = tiles.shape[0] - 1, tiles.shape[1]
    own = sources[0]
    rows = own.shape[0]
    return pl.pallas_call(
        functools.partial(backward_kernel, slots),
        grid=(slots,),
        in_specs=[smem_spec(), pl.BlockSpec((None, block, block), lambda j: (j + 1, 0, 0))]
        + [any_spec()] * (len(sources) - 1)
        + [vmem_spec()],
        out_specs=pl.BlockSpec((rows, block), lambda j: (0, 0)),
        out_shape=jax.ShapeDtypeStruct((rows, block), f32),
        scratch_shapes=[pltpu.VMEM((slots, rows, block), f32), pltpu.SemaphoreType.DMA((slots,))],
        compiler_params=params(),
        cost_estimate=cost(6 * slots * rows * block * block, 4 * slots * block * (block + rows)),
        name="backward",
    )(offsets, tiles, *sources)


def bins_kernel(slots, offs_ref, next_ref, own_in, mine_ref, theirs_ref, own_out, first, group, both):
    p, flip = place()
    target = last_partner(p, flip)
    totals = [own_in[...], None, None, None]
    for which, value in enumerate(CODES[:4]):
        total = totals[which]
        for slot in range(slots):
            for there, offs, source in ((0, offs_ref, mine_ref), (1, next_ref, theirs_ref)):
                offset = offs[0, slot + 1]
                last, code = route(jnp.where(there == 1, target, p), offset, flip)
                use = (last == there) & (code == value) & (offset > 0)
                term = jnp.where(use, source[slot], 0.0)
                total = term if total is None else total + term
        totals[which] = total
    for ref, total in zip((own_out, first, group, both), totals):
        ref[...] = total


def make_bins(offsets, offsets_next, own, mine, theirs):
    slots, rows, block = mine.shape
    step = rows // 4
    flat = pl.BlockSpec((step, block), lambda i: (i, 0))
    deep = pl.BlockSpec((slots, step, block), lambda i: (0, i, 0))
    return pl.pallas_call(
        functools.partial(bins_kernel, slots),
        grid=(rows // step,),
        in_specs=[smem_spec(), smem_spec(), flat, deep, deep],
        out_specs=[flat] * 4,
        out_shape=[jax.ShapeDtypeStruct((rows, block), f32)] * 4,
        compiler_params=params(),
        cost_estimate=cost(20 * rows * block, 40 * rows * block),
        name="bins",
    )(offsets, offsets_next, own, mine, theirs)


def halves(pair):
    return lax.axis_index("samp") if pair else 0


def right_kernel(slots, pair, offs_ref, data_ref, image_ref, own, first, group, both, two, *refs):
    lasts_ref = refs[0]
    keep0_ref, send0_ref, keep_ref, send_ref, high_ref, low_ref, picked, sems = refs[-8:]
    for slot in range(slots):
        sources = (own, first, group, both, two, lasts_ref.at[slot])
        start_pick(offs_ref[0, slot + 1], sources, picked.at[slot], sems.at[slot])
    half = image_ref.shape[1] // 2
    samp = halves(pair)
    data = data_ref[...]
    image = image_ref[...]
    data_turned = split(data.T)
    high_ref[...], low_ref[...] = data_turned
    turned = split(image.T)
    image_pair, data_pair = split(image), split(data)

    def store(keep, send_out, which, total):
        lower, upper = total[:half], total[half:]

        @pl.when(samp == 0)
        def _():
            keep[which] = lower
            send_out[which] = upper

        @pl.when(samp != 0)
        def _():
            keep[which] = upper
            send_out[which] = lower

    store(keep0_ref, send0_ref, 0, dot3(turned, data_pair, NN) + dot3(data_turned, image_pair, NN))
    for slot in range(slots):
        pltpu.make_async_copy(own, picked.at[slot], sems.at[slot]).wait()
        store(keep_ref, send_ref, slot, dot3(turned, split(picked[slot]), NN))


def right(offsets, data, image, gate, sources, pair):
    slots = offsets.shape[1] - 1
    rows, block = data.shape
    part0 = jax.ShapeDtypeStruct((1, block // 2, block), f32)
    part = jax.ShapeDtypeStruct((slots, block // 2, block), f32)
    turned = jax.ShapeDtypeStruct((block, rows), bf16)
    return pl.pallas_call(
        functools.partial(right_kernel, slots, pair),
        in_specs=[smem_spec(), vmem_spec(), vmem_spec()] + [any_spec()] * (len(gate) + len(sources)),
        out_specs=[vmem_spec()] * 6,
        out_shape=[part0, part0, part, part, turned, turned],
        scratch_shapes=[pltpu.VMEM((slots, rows, block), f32), pltpu.SemaphoreType.DMA((slots,))],
        compiler_params=params(),
        cost_estimate=pl.CostEstimate(flops=400 * rows * block * block, bytes_accessed=0, transcendentals=0),
        name="right",
    )(offsets, data, image, *sources, *gate)


def left_kernel(slots, pair, offs_ref, keep_in, send_in, high_ref, low_ref, own, first, group, both, two, lasts_ref,
                keep_ref, send_ref, picked, sems):
    slot = pl.program_id(0)

    @pl.when(slot == 0)
    def _():
        for each in range(slots):
            sources = (own, first, group, both, two, lasts_ref.at[each])
            start_pick(offs_ref[0, each + 1], sources, picked.at[each], sems.at[each])

    pltpu.make_async_copy(own, picked.at[slot], sems.at[slot]).wait()
    half = send_ref.shape[0]
    mine = halves(pair) * half
    chosen = split(picked[slot])
    for out_ref, in_ref, row in ((send_ref, send_in, half - mine), (keep_ref, keep_in, mine)):
        rows = pl.ds(pl.multiple_of(row, half), half)
        out_ref[...] = in_ref[...] + dot3((high_ref[rows], low_ref[rows]), chosen, NN)


def left(offsets, parts, turned, sources, pair):
    keep = parts[0]
    slots, half = keep.shape[:2]
    block, rows = turned[0].shape
    spec = pl.BlockSpec((None, half, block), lambda j: (j, 0, 0))
    whole = pl.BlockSpec((block, rows), lambda j: (0, 0))
    part = jax.ShapeDtypeStruct(keep.shape, f32)
    return pl.pallas_call(
        functools.partial(left_kernel, slots, pair),
        grid=(slots,),
        in_specs=[smem_spec(), spec, spec, whole, whole] + [any_spec()] * (len(sources) - 1) + [vmem_spec()],
        out_specs=[spec, spec],
        out_shape=[part, part],
        scratch_shapes=[pltpu.VMEM((slots, rows, block), f32), pltpu.SemaphoreType.DMA((slots,))],
        compiler_params=params(),
        cost_estimate=cost(6 * slots * rows * block * block, 4 * slots * block * (2 * block + rows)),
        name="left",
    )(offsets, *parts, *turned, *sources)


def finish_kernel(begin, factor, offs_ref, step_ref, tile_ref, keep_ref, other_ref, *refs):
    out_ref = refs[-1]
    slot = pl.program_id(0) + begin
    half, block = out_ref.shape
    step_size = step_ref[0]
    old = tile_ref[...]
    bound = step_size * penalty_weight
    stepped = old - (step_size * factor) * (keep_ref[...] + other_ref[...])

    def shrunk(value):
        return value - jnp.clip(value, -bound, bound)

    @pl.when(slot == 0)
    def _():
        rows = lax.axis_index("samp") * half + lax.broadcasted_iota(jnp.int32, (half, block), 0)
        on_diag = rows == lax.broadcasted_iota(jnp.int32, (half, block), 1)
        out_ref[...] = jnp.where(on_diag, stepped + step_size / jnp.where(on_diag, old, 1.0), shrunk(stepped))

    @pl.when(slot > 0)
    def _():
        out_ref[...] = jnp.where(offs_ref[0, slot] > 0, shrunk(stepped), 0.0)


def finish(offsets, step, tiles, keep, other, factor, begin, earlier=()):
    slots, block = tiles.shape[:2]
    count, half = keep.shape[:2]
    spec = pl.BlockSpec((None, half, block), lambda j: (j, 0, 0))
    tile_spec = pl.BlockSpec((None, half, block), lambda j: (j + begin, lax.axis_index("samp"), 0))
    return pl.pallas_call(
        functools.partial(finish_kernel, begin, factor),
        grid=(count,),
        in_specs=[smem_spec(), smem_spec(), tile_spec, spec, spec] + [any_spec()] * len(earlier),
        out_specs=pl.BlockSpec((None, half, block), lambda j: (j + begin, 0, 0)),
        out_shape=jax.ShapeDtypeStruct((slots, half, block), f32),
        input_output_aliases={5: 0} if earlier else {},
        compiler_params=params(),
        cost_estimate=cost(6 * keep.size, 16 * keep.size),
        name="finish",
    )(offsets, step, tiles, keep, other, *earlier)


def after(value, other):
    return lax.optimization_barrier((value, other))[0]


def swap(value):
    return lax.ppermute(value, "samp", [(0, 1), (1, 0)])


def shards(data, tiles, offsets, step):
    local_tiles = tiles[0]
    slot_count, block = local_tiles.shape[:2]
    samp_count = lax.axis_size("samp")
    pair = samp_count == 2
    factor = 1.0 / (2.0 * data.shape[0] * samp_count)

    offsets_next = send(offsets, "last")
    data_first = send(data, "first")
    data_group = send(data, "group")
    own, far, far_two = forward(offsets, data, local_tiles)
    theirs = send(after(far, offsets_next), "last")
    got_two = send(after(far_two, data_first), "direct", reverse=True)
    data_both = send(after(data_first, data_group), "group")
    own, bin_first, bin_group, bin_both = make_bins(offsets, offsets_next, own, far, theirs)
    got_both = send(bin_both + got_two, "first")
    chosen = choose(offsets_next, data, data_first, data_group, data_both)
    data_last = send(chosen, "last")
    data_two = send(after(data_both, chosen), "direct")
    data_sources = (data, data_first, data_group, data_both, data_two, data_last)

    got_group = send(bin_group + got_both, "group", reverse=True)
    got_first = send(after(bin_first, got_both), "first")
    image = own + backward(offsets, local_tiles, data_sources) + got_first + got_group

    image_group = send(image, "group")
    image_first = send(image, "first")
    image_both = send(image_group, "first")
    chosen = choose(offsets_next, image, image_first, image_group, image_both)
    image_last = send(chosen, "last")
    keep0, other0, keep, other, high, low = right(offsets, data, image, (chosen,), data_sources, pair)
    image_two = send(after(image_both, chosen), "direct")
    image_sources = (image, image_first, image_group, image_both, image_two, image_last)

    if pair:
        result = finish(offsets, step, local_tiles, keep0, swap(other0), factor, 0)
        keep = after(keep, result)
    keep, other = left(offsets, (keep, other), (high, low), image_sources, pair)
    if pair:
        return finish(offsets, step, local_tiles, keep, swap(other), factor, 1, (result,))[None]
    keep, other = (jnp.concatenate(both) for both in ((keep0, keep), (other0, other)))
    summed = lax.psum_scatter(jnp.concatenate([keep, other], axis=1), "samp", scatter_dimension=1, tiled=True)
    none = jnp.zeros_like(summed)
    return finish(offsets, step, local_tiles, summed, none, factor, 0)[None]


def solution(mesh):
    return jax.shard_map(
        shards,
        mesh=mesh,
        in_specs=(P("samp", "var"), P("var", None, None, None), P("var", None), P()),
        out_specs=P("var", None, "samp", None),
        check_vma=False,
    )
```

```python
import functools

import jax
import jax.numpy as jnp
from jax import lax
from jax.experimental import pallas as pl
from jax.experimental.pallas import tpu as pltpu
from jax.sharding import PartitionSpec as P

penalty_weight = 0.05
BAND = 6
VMEM_LIMIT = 48 * 1024 * 1024
NN = (((1,), (0,)), ((), ()))
NT = (((1,), (1,)), ((), ()))
f32, bf16 = jnp.float32, jnp.bfloat16


def params(**kw):
    return pltpu.CompilerParams(vmem_limit_bytes=VMEM_LIMIT, **kw)


def cost(flops, nbytes):
    return pl.CostEstimate(flops=0, bytes_accessed=0, transcendentals=0)


def any_spec():
    return pl.BlockSpec(memory_space=pl.ANY)


def vmem_spec():
    return pl.BlockSpec(memory_space=pltpu.VMEM)


def smem_spec():
    return pl.BlockSpec(memory_space=pltpu.SMEM)


def split(value):
    high = value.astype(bf16)
    return high, (value - high.astype(f32)).astype(bf16)


def dot3(left, right, dims):
    dot = functools.partial(lax.dot_general, dimension_numbers=dims, preferred_element_type=f32)
    return dot(left[0], right[0]) + (dot(left[0], right[1]) + dot(left[1], right[0]))


def route(p, k, flip):
    xbit = k & 1
    ybit = (((p + k) >> 1) ^ (p >> 1)) & 1
    first = jnp.where(flip == 0, xbit, ybit)
    last = jnp.where(flip == 0, ybit, xbit)
    return last, first + 2 * ((p + k) >> 2)


def place():
    return lax.axis_index("var") & 3, lax.axis_index("samp") & 1


def last_partner(p, flip):
    return jnp.where(flip == 0, p ^ 2, p ^ 1)


def wanted(first, last, groups):
    found = set()
    for p in range(4):
        for k in range(1, BAND):
            bits = p ^ ((p + k) & 3)
            if bits & first and (p + k) >> 2 == groups:
                found.add(p ^ (bits & last))
    return found


def hop(var_count, samp_count, kind, reverse=False):
    pairs = []
    for var in range(var_count):
        for samp in range(samp_count):
            first, last = (2, 1) if samp & 1 else (1, 2)
            back = (var - 4) % var_count
            use = True
            if kind == "first":
                target = var ^ first
            elif kind == "last":
                target = var ^ last
            elif kind == "group":
                target = back
            elif kind == "two":
                target = back ^ first
                use = (var & 3) == 0
            elif kind == "column":
                target = back
                use = (var & 3) in wanted(first, last, 2)
            else:
                target = back ^ last
                use = (var & 3) in wanted(first, last, 2)
            pair = (var * samp_count + samp, target * samp_count + samp)
            if use:
                pairs.append(pair[::-1] if reverse else pair)
    return pairs


def send(value, kind, reverse=False):
    pairs = hop(lax.axis_size("var"), lax.axis_size("samp"), kind, reverse)
    return lax.ppermute(value, ("var", "samp"), pairs)


def forward_kernel(data_ref, tile_ref, own_ref, far_ref):
    slot = pl.program_id(0)
    value = dot3(split(data_ref[...]), split(tile_ref[...]), NN)

    @pl.when(slot == 0)
    def _():
        own_ref[...] = value

    @pl.when(slot > 0)
    def _():
        far_ref[...] = value


def forward(data, tiles):
    slots, block = tiles.shape[:2]
    rows = data.shape[0]
    return pl.pallas_call(
        forward_kernel,
        grid=(slots,),
        in_specs=[
            pl.BlockSpec((rows, block), lambda j: (0, 0)),
            pl.BlockSpec((None, block, block), lambda j: (j, 0, 0)),
        ],
        out_specs=[
            pl.BlockSpec((rows, block), lambda j: (0, 0)),
            pl.BlockSpec((None, rows, block), lambda j: (jnp.maximum(j - 1, 0), 0, 0)),
        ],
        out_shape=[
            jax.ShapeDtypeStruct((rows, block), f32),
            jax.ShapeDtypeStruct((slots - 1, rows, block), f32),
        ],
        compiler_params=params(),
        cost_estimate=cost(6 * slots * rows * block * block, 4 * slots * block * (block + 2 * rows)),
        name="forward",
    )(data, tiles)


CODES = (0, 1, 2, 3, 5)


def choose_kernel(slots, count, offs_ref, *refs):
    sources, (out, sems) = refs[:count], refs[count:]
    p, flip = place()
    target = last_partner(p, flip)
    copies = []
    for slot in range(slots):
        last, code = route(target, offs_ref[0, slot + 1], flip)
        for value, source in zip(CODES, sources):
            copy = pltpu.make_async_copy(source, out.at[slot], sems.at[slot])
            pl.when((last == 1) & (code == value))(copy.start)
        known = (last == 1) & (code <= CODES[count - 1])
        copies.append((known, pltpu.make_async_copy(sources[0], out.at[slot], sems.at[slot])))
    for known, copy in copies:
        pl.when(known)(copy.wait)


def choose(offsets_next, *sources):
    slots = offsets_next.shape[1] - 1
    own = sources[0]
    return pl.pallas_call(
        functools.partial(choose_kernel, slots, len(sources)),
        in_specs=[smem_spec()] + [any_spec()] * len(sources),
        out_specs=any_spec(),
        out_shape=jax.ShapeDtypeStruct((slots,) + own.shape, f32),
        scratch_shapes=[pltpu.SemaphoreType.DMA((slots,))],
        compiler_params=params(),
        cost_estimate=cost(0, 8 * slots * own.size),
        name="choose",
    )(offsets_next, *sources)


def start_pick(offset, sources, target, sem):
    p, flip = place()
    last, code = route(p, offset, flip)
    for value, source in zip(CODES[:4], sources[:4]):
        pl.when((last == 0) & (code == value))(pltpu.make_async_copy(source, target, sem).start)
    over_last = last == 1
    if len(sources) > 5:
        over_last = over_last & (code != CODES[4])
        pl.when(code == CODES[4])(pltpu.make_async_copy(sources[5], target, sem).start)
    pl.when(over_last)(pltpu.make_async_copy(sources[4], target, sem).start)


def backward_kernel(slots, offs_ref, tile_ref, own, first, group, both, *refs):
    lasts_ref, out_ref, picked, sems = refs
    slot = pl.program_id(0)

    @pl.when(slot == 0)
    def _():
        out_ref[...] = jnp.zeros_like(out_ref)
        for each in range(slots):
            sources = (own, first, group, both, lasts_ref.at[each])
            start_pick(offs_ref[0, each + 1], sources, picked.at[each], sems.at[each])

    pltpu.make_async_copy(own, picked.at[slot], sems.at[slot]).wait()
    mirror = jnp.where(offs_ref[0, slot + 1] > 0, 1.0, 0.0).astype(f32)
    out_ref[...] += mirror * dot3(split(picked[slot]), split(tile_ref[...]), NT)


def backward(offsets, tiles, sources):
    slots, block = tiles.shape[0] - 1, tiles.shape[1]
    own = sources[0]
    rows = own.shape[0]
    return pl.pallas_call(
        functools.partial(backward_kernel, slots),
        grid=(slots,),
        in_specs=[smem_spec(), pl.BlockSpec((None, block, block), lambda j: (j + 1, 0, 0))]
        + [any_spec()] * (len(sources) - 1)
        + [vmem_spec()],
        out_specs=pl.BlockSpec((rows, block), lambda j: (0, 0)),
        out_shape=jax.ShapeDtypeStruct((rows, block), f32),
        scratch_shapes=[pltpu.VMEM((slots, rows, block), f32), pltpu.SemaphoreType.DMA((slots,))],
        compiler_params=params(),
        cost_estimate=cost(6 * slots * rows * block * block, 4 * slots * block * (block + rows)),
        name="backward",
    )(offsets, tiles, *sources)


def bins_kernel(slots, offs_ref, next_ref, own_in, mine_ref, theirs_ref, own_out, first, group, both, two):
    p, flip = place()
    target = last_partner(p, flip)
    totals = [own_in[...], None, None, None, None]
    for which, value in enumerate((0, 1, 2, 3, 5)):
        total = totals[which]
        for slot in range(slots):
            for there, offs, source in ((0, offs_ref, mine_ref), (1, next_ref, theirs_ref)):
                offset = offs[0, slot + 1]
                last, code = route(jnp.where(there == 1, target, p), offset, flip)
                use = (last == there) & (code == value) & (offset > 0)
                term = jnp.where(use, source[slot], 0.0)
                total = term if total is None else total + term
        totals[which] = total
    for ref, total in zip((own_out, first, group, both, two), totals):
        ref[...] = total


def make_bins(offsets, offsets_next, own, mine, theirs):
    slots, rows, block = mine.shape
    step = rows // 4
    flat = pl.BlockSpec((step, block), lambda i: (i, 0))
    deep = pl.BlockSpec((slots, step, block), lambda i: (0, i, 0))
    return pl.pallas_call(
        functools.partial(bins_kernel, slots),
        grid=(rows // step,),
        in_specs=[smem_spec(), smem_spec(), flat, deep, deep],
        out_specs=[flat] * 5,
        out_shape=[jax.ShapeDtypeStruct((rows, block), f32)] * 5,
        compiler_params=params(),
        cost_estimate=cost(20 * rows * block, 40 * rows * block),
        name="bins",
    )(offsets, offsets_next, own, mine, theirs)


def halves(pair):
    return lax.axis_index("samp") if pair else 0


def right_kernel(slots, pair, offs_ref, data_ref, image_ref, own, first, group, both, *refs):
    lasts_ref = refs[0]
    keep0_ref, send0_ref, keep_ref, send_ref, high_ref, low_ref, picked, sems = refs[-8:]
    for slot in range(slots):
        sources = (own, first, group, both, lasts_ref.at[slot])
        start_pick(offs_ref[0, slot + 1], sources, picked.at[slot], sems.at[slot])
    half = image_ref.shape[1] // 2
    samp = halves(pair)
    data = data_ref[...]
    image = image_ref[...]
    data_turned = split(data.T)
    high_ref[...], low_ref[...] = data_turned
    turned = split(image.T)
    image_pair, data_pair = split(image), split(data)

    def store(keep, send_out, which, total):
        lower, upper = total[:half], total[half:]

        @pl.when(samp == 0)
        def _():
            keep[which] = lower
            send_out[which] = upper

        @pl.when(samp != 0)
        def _():
            keep[which] = upper
            send_out[which] = lower

    store(keep0_ref, send0_ref, 0, dot3(turned, data_pair, NN) + dot3(data_turned, image_pair, NN))
    for slot in range(slots):
        pltpu.make_async_copy(own, picked.at[slot], sems.at[slot]).wait()
        store(keep_ref, send_ref, slot, dot3(turned, split(picked[slot]), NN))


def right(offsets, data, image, gate, sources, pair):
    slots = offsets.shape[1] - 1
    rows, block = data.shape
    part0 = jax.ShapeDtypeStruct((1, block // 2, block), f32)
    part = jax.ShapeDtypeStruct((slots, block // 2, block), f32)
    turned = jax.ShapeDtypeStruct((block, rows), bf16)
    return pl.pallas_call(
        functools.partial(right_kernel, slots, pair),
        in_specs=[smem_spec(), vmem_spec(), vmem_spec()] + [any_spec()] * (len(gate) + len(sources)),
        out_specs=[vmem_spec()] * 6,
        out_shape=[part0, part0, part, part, turned, turned],
        scratch_shapes=[pltpu.VMEM((slots, rows, block), f32), pltpu.SemaphoreType.DMA((slots,))],
        compiler_params=params(),
        cost_estimate=pl.CostEstimate(flops=400 * rows * block * block, bytes_accessed=0, transcendentals=0),
        name="right",
    )(offsets, data, image, *sources, *gate)


def left_kernel(slots, pair, offs_ref, keep_in, send_in, high_ref, low_ref, own, first, group, both, two, lasts_ref,
                keep_ref, send_ref, picked, sems):
    slot = pl.program_id(0)

    @pl.when(slot == 0)
    def _():
        for each in range(slots):
            sources = (own, first, group, both, lasts_ref.at[each], two)
            start_pick(offs_ref[0, each + 1], sources, picked.at[each], sems.at[each])

    pltpu.make_async_copy(own, picked.at[slot], sems.at[slot]).wait()
    half = send_ref.shape[0]
    mine = halves(pair) * half
    chosen = split(picked[slot])
    for out_ref, in_ref, row in ((send_ref, send_in, half - mine), (keep_ref, keep_in, mine)):
        rows = pl.ds(pl.multiple_of(row, half), half)
        out_ref[...] = in_ref[...] + dot3((high_ref[rows], low_ref[rows]), chosen, NN)


def left(offsets, parts, turned, sources, pair):
    keep = parts[0]
    slots, half = keep.shape[:2]
    block, rows = turned[0].shape
    spec = pl.BlockSpec((None, half, block), lambda j: (j, 0, 0))
    whole = pl.BlockSpec((block, rows), lambda j: (0, 0))
    part = jax.ShapeDtypeStruct(keep.shape, f32)
    return pl.pallas_call(
        functools.partial(left_kernel, slots, pair),
        grid=(slots,),
        in_specs=[smem_spec(), spec, spec, whole, whole] + [any_spec()] * (len(sources) - 1) + [vmem_spec()],
        out_specs=[spec, spec],
        out_shape=[part, part],
        scratch_shapes=[pltpu.VMEM((slots, rows, block), f32), pltpu.SemaphoreType.DMA((slots,))],
        compiler_params=params(),
        cost_estimate=cost(6 * slots * rows * block * block, 4 * slots * block * (2 * block + rows)),
        name="left",
    )(offsets, *parts, *turned, *sources)


def finish_kernel(begin, factor, offs_ref, step_ref, tile_ref, keep_ref, other_ref, *refs):
    out_ref = refs[-1]
    slot = pl.program_id(0) + begin
    half, block = out_ref.shape
    step_size = step_ref[0]
    old = tile_ref[...]
    bound = step_size * penalty_weight
    stepped = old - (step_size * factor) * (keep_ref[...] + other_ref[...])

    def shrunk(value):
        return value - jnp.clip(value, -bound, bound)

    @pl.when(slot == 0)
    def _():
        rows = lax.axis_index("samp") * half + lax.broadcasted_iota(jnp.int32, (half, block), 0)
        on_diag = rows == lax.broadcasted_iota(jnp.int32, (half, block), 1)
        out_ref[...] = jnp.where(on_diag, stepped + step_size / jnp.where(on_diag, old, 1.0), shrunk(stepped))

    @pl.when(slot > 0)
    def _():
        out_ref[...] = jnp.where(offs_ref[0, slot] > 0, shrunk(stepped), 0.0)


def finish(offsets, step, tiles, keep, other, factor, begin, earlier=()):
    slots, block = tiles.shape[:2]
    count, half = keep.shape[:2]
    spec = pl.BlockSpec((None, half, block), lambda j: (j, 0, 0))
    tile_spec = pl.BlockSpec((None, half, block), lambda j: (j + begin, lax.axis_index("samp"), 0))
    return pl.pallas_call(
        functools.partial(finish_kernel, begin, factor),
        grid=(count,),
        in_specs=[smem_spec(), smem_spec(), tile_spec, spec, spec] + [any_spec()] * len(earlier),
        out_specs=pl.BlockSpec((None, half, block), lambda j: (j + begin, 0, 0)),
        out_shape=jax.ShapeDtypeStruct((slots, half, block), f32),
        input_output_aliases={5: 0} if earlier else {},
        compiler_params=params(),
        cost_estimate=cost(6 * keep.size, 16 * keep.size),
        name="finish",
    )(offsets, step, tiles, keep, other, *earlier)


def after(value, other):
    return lax.optimization_barrier((value, other))[0]


def swap(value):
    return lax.ppermute(value, "samp", [(0, 1), (1, 0)])


def shards(data, tiles, offsets, step):
    local_tiles = tiles[0]
    slot_count, block = local_tiles.shape[:2]
    samp_count = lax.axis_size("samp")
    pair = samp_count == 2
    factor = 1.0 / (2.0 * data.shape[0] * samp_count)

    offsets_next = send(offsets, "last")
    data_first = send(data, "first")
    own, far = forward(data, local_tiles)
    theirs = send(after(far, offsets_next), "last")
    data_both = send(data_first, "group")
    data_two = send(data_both, "column")
    data_group = send(after(data, data_both), "group")
    own, bin_first, bin_group, bin_both, bin_two = make_bins(offsets, offsets_next, own, far, after(theirs, data_both))
    got_both = send(bin_both, "first")
    got_two = send(bin_two, "two", reverse=True)
    chosen = choose(offsets_next, data, data_first, data_group, data_both, data_two)
    data_last = send(chosen, "last")
    data_sources = (data, data_first, data_group, data_both, data_last)

    bin_group = bin_group + got_both + got_two
    got_group = send(bin_group, "group", reverse=True)
    got_first = send(after(bin_first, bin_group), "first")
    image = own + backward(offsets, local_tiles, data_sources) + got_first + got_group

    image_group = send(image, "group")
    image_first = send(image, "first")
    image_both = send(image_group, "first")
    chosen = choose(offsets_next, image, image_first, image_group, image_both)
    image_last = send(chosen, "last")
    keep0, other0, keep, other, high, low = right(offsets, data, image, (chosen,), data_sources, pair)
    image_two = send(after(image_both, chosen), "direct")
    image_sources = (image, image_first, image_group, image_both, image_two, image_last)

    if pair:
        result = finish(offsets, step, local_tiles, keep0, swap(other0), factor, 0)
        keep = after(keep, result)
    keep, other = left(offsets, (keep, other), (high, low), image_sources, pair)
    if pair:
        return finish(offsets, step, local_tiles, keep, swap(other), factor, 1, (result,))[None]
    keep, other = (jnp.concatenate(both) for both in ((keep0, keep), (other0, other)))
    summed = lax.psum_scatter(jnp.concatenate([keep, other], axis=1), "samp", scatter_dimension=1, tiled=True)
    none = jnp.zeros_like(summed)
    return finish(offsets, step, local_tiles, summed, none, factor, 0)[None]


def solution(mesh):
    return jax.shard_map(
        shards,
        mesh=mesh,
        in_specs=(P("samp", "var"), P("var", None, None, None), P("var", None), P()),
        out_specs=P("var", None, "samp", None),
        check_vma=False,
    )
```

```python
import functools

import jax
import jax.numpy as jnp
from jax import lax
from jax.experimental import pallas as pl
from jax.experimental.pallas import tpu as pltpu
from jax.sharding import PartitionSpec as P

penalty_weight = 0.05
BAND = 6
VMEM_LIMIT = 20 * 1024 * 1024
NN = (((1,), (0,)), ((), ()))
NT = (((1,), (1,)), ((), ()))
f32, bf16 = jnp.float32, jnp.bfloat16


def params(**kw):
    return pltpu.CompilerParams(vmem_limit_bytes=VMEM_LIMIT, **kw)


def cost(flops, nbytes):
    return pl.CostEstimate(flops=0, bytes_accessed=0, transcendentals=0)


def any_spec():
    return pl.BlockSpec(memory_space=pl.ANY)


def vmem_spec():
    return pl.BlockSpec(memory_space=pltpu.VMEM)


def smem_spec():
    return pl.BlockSpec(memory_space=pltpu.SMEM)


def split(value):
    high = value.astype(bf16)
    return high, (value - high.astype(f32)).astype(bf16)


def dot3(left, right, dims):
    dot = functools.partial(lax.dot_general, dimension_numbers=dims, preferred_element_type=f32)
    return dot(left[0], right[0]) + (dot(left[0], right[1]) + dot(left[1], right[0]))


def route(p, k, flip):
    xbit = k & 1
    ybit = (((p + k) >> 1) ^ (p >> 1)) & 1
    first = jnp.where(flip == 0, xbit, ybit)
    last = jnp.where(flip == 0, ybit, xbit)
    return last, first + 2 * ((p + k) >> 2)


def place():
    return lax.axis_index("var") & 3, lax.axis_index("samp") & 1


def last_partner(p, flip):
    return jnp.where(flip == 0, p ^ 2, p ^ 1)


def wanted(first, last, groups):
    found = set()
    for p in range(4):
        for k in range(1, BAND):
            bits = p ^ ((p + k) & 3)
            if bits & first and (p + k) >> 2 == groups:
                found.add(p ^ (bits & last))
    return found


def hop(var_count, samp_count, kind, reverse=False):
    pairs = []
    for var in range(var_count):
        for samp in range(samp_count):
            first, last = (2, 1) if samp & 1 else (1, 2)
            back = (var - 4) % var_count
            use = True
            if kind == "first":
                target = var ^ first
            elif kind == "last":
                target = var ^ last
            elif kind == "group":
                target = back
            elif kind == "two":
                target = back ^ first
                use = (var & 3) == 0
            elif kind == "column":
                target = back
                use = (var & 3) in wanted(first, last, 2)
            else:
                target = back ^ last
                use = (var & 3) in wanted(first, last, 2)
            pair = (var * samp_count + samp, target * samp_count + samp)
            if use:
                pairs.append(pair[::-1] if reverse else pair)
    return pairs


def send(value, kind, reverse=False):
    pairs = hop(lax.axis_size("var"), lax.axis_size("samp"), kind, reverse)
    return lax.ppermute(value, ("var", "samp"), pairs)


def forward_kernel(data_ref, tile_ref, own_ref, far_ref):
    slot = pl.program_id(0)
    value = dot3(split(data_ref[...]), split(tile_ref[...]), NN)

    @pl.when(slot == 0)
    def _():
        own_ref[...] = value

    @pl.when(slot > 0)
    def _():
        far_ref[...] = value


def forward(data, tiles):
    slots, block = tiles.shape[:2]
    rows = data.shape[0]
    return pl.pallas_call(
        forward_kernel,
        grid=(slots,),
        in_specs=[
            pl.BlockSpec((rows, block), lambda j: (0, 0)),
            pl.BlockSpec((None, block, block), lambda j: (j, 0, 0)),
        ],
        out_specs=[
            pl.BlockSpec((rows, block), lambda j: (0, 0)),
            pl.BlockSpec((None, rows, block), lambda j: (jnp.maximum(j - 1, 0), 0, 0)),
        ],
        out_shape=[
            jax.ShapeDtypeStruct((rows, block), f32),
            jax.ShapeDtypeStruct((slots - 1, rows, block), f32),
        ],
        compiler_params=params(),
        cost_estimate=cost(6 * slots * rows * block * block, 4 * slots * block * (block + 2 * rows)),
        name="forward",
    )(data, tiles)


CODES = (0, 1, 2, 3, 5)


def choose_kernel(slots, count, offs_ref, *refs):
    sources, (out, sems) = refs[:count], refs[count:]
    p, flip = place()
    target = last_partner(p, flip)
    copies = []
    for slot in range(slots):
        last, code = route(target, offs_ref[0, slot + 1], flip)
        for value, source in zip(CODES, sources):
            copy = pltpu.make_async_copy(source, out.at[slot], sems.at[slot])
            pl.when((last == 1) & (code == value))(copy.start)
        known = (last == 1) & (code <= CODES[count - 1])
        copies.append((known, pltpu.make_async_copy(sources[0], out.at[slot], sems.at[slot])))
    for known, copy in copies:
        pl.when(known)(copy.wait)


def choose(offsets_next, *sources):
    slots = offsets_next.shape[1] - 1
    own = sources[0]
    return pl.pallas_call(
        functools.partial(choose_kernel, slots, len(sources)),
        in_specs=[smem_spec()] + [any_spec()] * len(sources),
        out_specs=any_spec(),
        out_shape=jax.ShapeDtypeStruct((slots,) + own.shape, f32),
        scratch_shapes=[pltpu.SemaphoreType.DMA((slots,))],
        compiler_params=params(),
        cost_estimate=cost(0, 8 * slots * own.size),
        name="choose",
    )(offsets_next, *sources)


def start_pick(offset, sources, target, sem):
    p, flip = place()
    last, code = route(p, offset, flip)
    for value, source in zip(CODES[:4], sources[:4]):
        pl.when((last == 0) & (code == value))(pltpu.make_async_copy(source, target, sem).start)
    over_last = last == 1
    if len(sources) > 5:
        over_last = over_last & (code != CODES[4])
        pl.when(code == CODES[4])(pltpu.make_async_copy(sources[5], target, sem).start)
    pl.when(over_last)(pltpu.make_async_copy(sources[4], target, sem).start)


def backward_kernel(slots, offs_ref, tile_ref, own, first, group, both, *refs):
    lasts_ref, out_ref, picked, sems = refs
    slot = pl.program_id(0)

    @pl.when(slot == 0)
    def _():
        out_ref[...] = jnp.zeros_like(out_ref)
        for each in range(slots):
            sources = (own, first, group, both, lasts_ref.at[each])
            start_pick(offs_ref[0, each + 1], sources, picked.at[each], sems.at[each])

    pltpu.make_async_copy(own, picked.at[slot], sems.at[slot]).wait()
    mirror = jnp.where(offs_ref[0, slot + 1] > 0, 1.0, 0.0).astype(f32)
    out_ref[...] += mirror * dot3(split(picked[slot]), split(tile_ref[...]), NT)


def backward(offsets, tiles, sources):
    slots, block = tiles.shape[0] - 1, tiles.shape[1]
    own = sources[0]
    rows = own.shape[0]
    return pl.pallas_call(
        functools.partial(backward_kernel, slots),
        grid=(slots,),
        in_specs=[smem_spec(), pl.BlockSpec((None, block, block), lambda j: (j + 1, 0, 0))]
        + [any_spec()] * len(sources),
        out_specs=pl.BlockSpec((rows, block), lambda j: (0, 0)),
        out_shape=jax.ShapeDtypeStruct((rows, block), f32),
        scratch_shapes=[pltpu.VMEM((slots, rows, block), f32), pltpu.SemaphoreType.DMA((slots,))],
        compiler_params=params(),
        cost_estimate=cost(6 * slots * rows * block * block, 4 * slots * block * (block + rows)),
        name="backward",
    )(offsets, tiles, *sources)


def bins_kernel(slots, offs_ref, next_ref, own_in, mine_ref, theirs_ref, own_out, first, group, both, two):
    p, flip = place()
    target = last_partner(p, flip)
    totals = [own_in[...], None, None, None, None]
    for which, value in enumerate((0, 1, 2, 3, 5)):
        total = totals[which]
        for slot in range(slots):
            for there, offs, source in ((0, offs_ref, mine_ref), (1, next_ref, theirs_ref)):
                offset = offs[0, slot + 1]
                last, code = route(jnp.where(there == 1, target, p), offset, flip)
                use = (last == there) & (code == value) & (offset > 0)
                term = jnp.where(use, source[slot], 0.0)
                total = term if total is None else total + term
        totals[which] = total
    for ref, total in zip((own_out, first, group, both, two), totals):
        ref[...] = total


def make_bins(offsets, offsets_next, own, mine, theirs):
    slots, rows, block = mine.shape
    step = rows // 4
    flat = pl.BlockSpec((step, block), lambda i: (i, 0))
    deep = pl.BlockSpec((slots, step, block), lambda i: (0, i, 0))
    return pl.pallas_call(
        functools.partial(bins_kernel, slots),
        grid=(rows // step,),
        in_specs=[smem_spec(), smem_spec(), flat, deep, deep],
        out_specs=[flat] * 5,
        out_shape=[jax.ShapeDtypeStruct((rows, block), f32)] * 5,
        compiler_params=params(),
        cost_estimate=cost(20 * rows * block, 40 * rows * block),
        name="bins",
    )(offsets, offsets_next, own, mine, theirs)


def halves(pair):
    return lax.axis_index("samp") if pair else 0


def right_kernel(slots, pair, offs_ref, data_ref, image_ref, own, first, group, both, *refs):
    lasts_ref = refs[0]
    keep0_ref, send0_ref, keep_ref, send_ref, high_ref, low_ref, picked, sems = refs[-8:]
    for slot in range(slots):
        sources = (own, first, group, both, lasts_ref.at[slot])
        start_pick(offs_ref[0, slot + 1], sources, picked.at[slot], sems.at[slot])
    half = image_ref.shape[1] // 2
    samp = halves(pair)
    data = data_ref[...]
    image = image_ref[...]
    data_turned = split(data.T)
    high_ref[...], low_ref[...] = data_turned
    turned = split(image.T)
    image_pair, data_pair = split(image), split(data)

    def store(keep, send_out, which, total):
        lower, upper = total[:half], total[half:]

        @pl.when(samp == 0)
        def _():
            keep[which] = lower
            send_out[which] = upper

        @pl.when(samp != 0)
        def _():
            keep[which] = upper
            send_out[which] = lower

    store(keep0_ref, send0_ref, 0, dot3(turned, data_pair, NN) + dot3(data_turned, image_pair, NN))
    for slot in range(slots):
        pltpu.make_async_copy(own, picked.at[slot], sems.at[slot]).wait()
        store(keep_ref, send_ref, slot, dot3(turned, split(picked[slot]), NN))


def right(offsets, data, image, gate, sources, pair):
    slots = offsets.shape[1] - 1
    rows, block = data.shape
    part0 = jax.ShapeDtypeStruct((1, block // 2, block), f32)
    part = jax.ShapeDtypeStruct((slots, block // 2, block), f32)
    turned = jax.ShapeDtypeStruct((block, rows), bf16)
    return pl.pallas_call(
        functools.partial(right_kernel, slots, pair),
        in_specs=[smem_spec(), vmem_spec(), vmem_spec()] + [any_spec()] * (len(gate) + len(sources)),
        out_specs=[vmem_spec()] * 6,
        out_shape=[part0, part0, part, part, turned, turned],
        scratch_shapes=[pltpu.VMEM((slots, rows, block), f32), pltpu.SemaphoreType.DMA((slots,))],
        compiler_params=params(),
        cost_estimate=pl.CostEstimate(flops=400 * rows * block * block, bytes_accessed=0, transcendentals=0),
        name="right",
    )(offsets, data, image, *sources, *gate)


def left_kernel(slots, pair, offs_ref, keep_in, send_in, high_ref, low_ref, own, first, group, both, two, lasts_ref,
                keep_ref, send_ref, picked, sems):
    slot = pl.program_id(0)

    @pl.when(slot == 0)
    def _():
        for each in range(slots):
            sources = (own, first, group, both, lasts_ref.at[each], two)
            start_pick(offs_ref[0, each + 1], sources, picked.at[each], sems.at[each])

    pltpu.make_async_copy(own, picked.at[slot], sems.at[slot]).wait()
    half = send_ref.shape[0]
    mine = halves(pair) * half
    chosen = split(picked[slot])
    for out_ref, in_ref, row in ((send_ref, send_in, half - mine), (keep_ref, keep_in, mine)):
        rows = pl.ds(pl.multiple_of(row, half), half)
        out_ref[...] = in_ref[...] + dot3((high_ref[rows], low_ref[rows]), chosen, NN)


def left(offsets, parts, turned, sources, pair):
    keep = parts[0]
    slots, half = keep.shape[:2]
    block, rows = turned[0].shape
    spec = pl.BlockSpec((None, half, block), lambda j: (j, 0, 0))
    whole = pl.BlockSpec((block, rows), lambda j: (0, 0))
    part = jax.ShapeDtypeStruct(keep.shape, f32)
    return pl.pallas_call(
        functools.partial(left_kernel, slots, pair),
        grid=(slots,),
        in_specs=[smem_spec(), spec, spec, whole, whole] + [any_spec()] * len(sources),
        out_specs=[spec, spec],
        out_shape=[part, part],
        scratch_shapes=[pltpu.VMEM((slots, rows, block), f32), pltpu.SemaphoreType.DMA((slots,))],
        compiler_params=params(),
        cost_estimate=cost(6 * slots * rows * block * block, 4 * slots * block * (2 * block + rows)),
        name="left",
    )(offsets, *parts, *turned, *sources)


def finish_kernel(begin, factor, offs_ref, step_ref, tile_ref, keep_ref, other_ref, *refs):
    out_ref = refs[-1]
    slot = pl.program_id(0) + begin
    half, block = out_ref.shape
    step_size = step_ref[0]
    old = tile_ref[...]
    bound = step_size * penalty_weight
    stepped = old - (step_size * factor) * (keep_ref[...] + other_ref[...])

    def shrunk(value):
        return value - jnp.clip(value, -bound, bound)

    @pl.when(slot == 0)
    def _():
        rows = lax.axis_index("samp") * half + lax.broadcasted_iota(jnp.int32, (half, block), 0)
        on_diag = rows == lax.broadcasted_iota(jnp.int32, (half, block), 1)
        out_ref[...] = jnp.where(on_diag, stepped + step_size / jnp.where(on_diag, old, 1.0), shrunk(stepped))

    @pl.when(slot > 0)
    def _():
        out_ref[...] = jnp.where(offs_ref[0, slot] > 0, shrunk(stepped), 0.0)


def finish(offsets, step, tiles, keep, other, factor, begin, earlier=()):
    slots, block = tiles.shape[:2]
    count, half = keep.shape[:2]
    spec = pl.BlockSpec((None, half, block), lambda j: (j, 0, 0))
    tile_spec = pl.BlockSpec((None, half, block), lambda j: (j + begin, lax.axis_index("samp"), 0))
    return pl.pallas_call(
        functools.partial(finish_kernel, begin, factor),
        grid=(count,),
        in_specs=[smem_spec(), smem_spec(), tile_spec, spec, spec] + [any_spec()] * len(earlier),
        out_specs=pl.BlockSpec((None, half, block), lambda j: (j + begin, 0, 0)),
        out_shape=jax.ShapeDtypeStruct((slots, half, block), f32),
        input_output_aliases={5: 0} if earlier else {},
        compiler_params=params(),
        cost_estimate=cost(6 * keep.size, 16 * keep.size),
        name="finish",
    )(offsets, step, tiles, keep, other, *earlier)


def after(value, other):
    return lax.optimization_barrier((value, other))[0]


def swap(value):
    return lax.ppermute(value, "samp", [(0, 1), (1, 0)])


def shards(data, tiles, offsets, step):
    local_tiles = tiles[0]
    slot_count, block = local_tiles.shape[:2]
    samp_count = lax.axis_size("samp")
    pair = samp_count == 2
    factor = 1.0 / (2.0 * data.shape[0] * samp_count)

    offsets_next = send(offsets, "last")
    data_first = send(data, "first")
    own, far = forward(data, local_tiles)
    theirs = send(after(far, (offsets_next, data_first)), "last")
    data_group = send(data, "group")
    data_both = send(after(data_first, data_group), "group")
    data_two = send(data_both, "column")
    own, bin_first, bin_group, bin_both, bin_two = make_bins(offsets, offsets_next, own, far, after(theirs, data_both))
    got_both = send(bin_both, "first")
    got_two = send(bin_two, "two", reverse=True)
    chosen = choose(offsets_next, data, data_first, data_group, data_both, data_two)
    data_last = send(chosen, "last")
    data_sources = (data, data_first, data_group, data_both, data_last)

    bin_group = bin_group + got_both + got_two
    got_group = send(bin_group, "group", reverse=True)
    got_first = send(bin_first, "first")
    image = own + backward(offsets, local_tiles, data_sources) + got_first + got_group

    image_group = send(image, "group")
    image_first = send(image, "first")
    image_both = send(image_group, "first")
    chosen = choose(offsets_next, image, image_first, image_group, image_both)
    image_last = send(chosen, "last")
    keep0, other0, keep, other, high, low = right(offsets, data, image, (chosen,), data_sources, pair)
    image_two = send(after(image_both, chosen), "direct")
    image_sources = (image, image_first, image_group, image_both, image_two, image_last)

    if pair:
        result = finish(offsets, step, local_tiles, keep0, swap(other0), factor, 0)
        keep = after(keep, result)
    keep, other = left(offsets, (keep, other), (high, low), image_sources, pair)
    if pair:
        return finish(offsets, step, local_tiles, keep, swap(other), factor, 1, (result,))[None]
    keep, other = (jnp.concatenate(both) for both in ((keep0, keep), (other0, other)))
    summed = lax.psum_scatter(jnp.concatenate([keep, other], axis=1), "samp", scatter_dimension=1, tiled=True)
    none = jnp.zeros_like(summed)
    return finish(offsets, step, local_tiles, summed, none, factor, 0)[None]


def solution(mesh):
    return jax.shard_map(
        shards,
        mesh=mesh,
        in_specs=(P("samp", "var"), P("var", None, None, None), P("var", None), P()),
        out_specs=P("var", None, "samp", None),
        check_vma=False,
    )
```

```python
import functools

import jax
import jax.numpy as jnp
from jax import lax
from jax.experimental import pallas as pl
from jax.experimental.pallas import tpu as pltpu
from jax.sharding import PartitionSpec as P

penalty_weight = 0.05
BAND = 6
VMEM_LIMIT = 20 * 1024 * 1024
NN = (((1,), (0,)), ((), ()))
NT = (((1,), (1,)), ((), ()))
f32, bf16 = jnp.float32, jnp.bfloat16


def params(**kw):
    return pltpu.CompilerParams(vmem_limit_bytes=VMEM_LIMIT, **kw)


def cost(flops, nbytes):
    return pl.CostEstimate(flops=0, bytes_accessed=0, transcendentals=0)


def any_spec():
    return pl.BlockSpec(memory_space=pl.ANY)


def vmem_spec():
    return pl.BlockSpec(memory_space=pltpu.VMEM)


def smem_spec():
    return pl.BlockSpec(memory_space=pltpu.SMEM)


def split(value):
    high = value.astype(bf16)
    return high, (value - high.astype(f32)).astype(bf16)


def dot3(left, right, dims):
    dot = functools.partial(lax.dot_general, dimension_numbers=dims, preferred_element_type=f32)
    return dot(left[0], right[0]) + (dot(left[0], right[1]) + dot(left[1], right[0]))


def route(p, k, flip):
    xbit = k & 1
    ybit = (((p + k) >> 1) ^ (p >> 1)) & 1
    first = jnp.where(flip == 0, xbit, ybit)
    last = jnp.where(flip == 0, ybit, xbit)
    return last, first + 2 * ((p + k) >> 2)


def place():
    return lax.axis_index("var") & 3, lax.axis_index("samp") & 1


def last_partner(p, flip):
    return jnp.where(flip == 0, p ^ 2, p ^ 1)


def wanted(first, last, groups):
    found = set()
    for p in range(4):
        for k in range(1, BAND):
            bits = p ^ ((p + k) & 3)
            if bits & first and (p + k) >> 2 == groups:
                found.add(p ^ (bits & last))
    return found


def hop(var_count, samp_count, kind, reverse=False):
    pairs = []
    for var in range(var_count):
        for samp in range(samp_count):
            first, last = (2, 1) if samp & 1 else (1, 2)
            back = (var - 4) % var_count
            use = True
            if kind == "first":
                target = var ^ first
            elif kind == "last":
                target = var ^ last
            elif kind == "group":
                target = back
            elif kind == "two":
                target = back ^ first
                use = (var & 3) == 0
            elif kind == "column":
                target = (var - 8) % var_count
                use = (var & 3) in wanted(first, last, 2)
            else:
                target = back ^ last
                use = (var & 3) in wanted(first, last, 2)
            pair = (var * samp_count + samp, target * samp_count + samp)
            if use:
                pairs.append(pair[::-1] if reverse else pair)
    return pairs


def send(value, kind, reverse=False):
    pairs = hop(lax.axis_size("var"), lax.axis_size("samp"), kind, reverse)
    return lax.ppermute(value, ("var", "samp"), pairs)


def forward_kernel(data_ref, tile_ref, own_ref, far_ref):
    slot = pl.program_id(0)
    value = dot3(split(data_ref[...]), split(tile_ref[...]), NN)

    @pl.when(slot == 0)
    def _():
        own_ref[...] = value

    @pl.when(slot > 0)
    def _():
        far_ref[...] = value


def forward(data, tiles):
    slots, block = tiles.shape[:2]
    rows = data.shape[0]
    return pl.pallas_call(
        forward_kernel,
        grid=(slots,),
        in_specs=[
            pl.BlockSpec((rows, block), lambda j: (0, 0)),
            pl.BlockSpec((None, block, block), lambda j: (j, 0, 0)),
        ],
        out_specs=[
            pl.BlockSpec((rows, block), lambda j: (0, 0)),
            pl.BlockSpec((None, rows, block), lambda j: (jnp.maximum(j - 1, 0), 0, 0)),
        ],
        out_shape=[
            jax.ShapeDtypeStruct((rows, block), f32),
            jax.ShapeDtypeStruct((slots - 1, rows, block), f32),
        ],
        compiler_params=params(),
        cost_estimate=cost(6 * slots * rows * block * block, 4 * slots * block * (block + 2 * rows)),
        name="forward",
    )(data, tiles)


CODES = (0, 1, 2, 3, 5)


def choose_kernel(slots, count, offs_ref, *refs):
    sources, (out, sems) = refs[:count], refs[count:]
    p, flip = place()
    target = last_partner(p, flip)
    copies = []
    for slot in range(slots):
        last, code = route(target, offs_ref[0, slot + 1], flip)
        for value, source in zip(CODES, sources):
            copy = pltpu.make_async_copy(source, out.at[slot], sems.at[slot])
            pl.when((last == 1) & (code == value))(copy.start)
        known = (last == 1) & (code <= CODES[count - 1])
        copies.append((known, pltpu.make_async_copy(sources[0], out.at[slot], sems.at[slot])))
    for known, copy in copies:
        pl.when(known)(copy.wait)


def choose(offsets_next, *sources):
    slots = offsets_next.shape[1] - 1
    own = sources[0]
    return pl.pallas_call(
        functools.partial(choose_kernel, slots, len(sources)),
        in_specs=[smem_spec()] + [any_spec()] * len(sources),
        out_specs=any_spec(),
        out_shape=jax.ShapeDtypeStruct((slots,) + own.shape, f32),
        scratch_shapes=[pltpu.SemaphoreType.DMA((slots,))],
        compiler_params=params(),
        cost_estimate=cost(0, 8 * slots * own.size),
        name="choose",
    )(offsets_next, *sources)


def start_pick(offset, sources, target, sem):
    p, flip = place()
    last, code = route(p, offset, flip)
    for value, source in zip(CODES[:4], sources[:4]):
        pl.when((last == 0) & (code == value))(pltpu.make_async_copy(source, target, sem).start)
    over_last = last == 1
    if len(sources) > 5:
        over_last = over_last & (code != CODES[4])
        pl.when(code == CODES[4])(pltpu.make_async_copy(sources[5], target, sem).start)
    pl.when(over_last)(pltpu.make_async_copy(sources[4], target, sem).start)


def backward_kernel(slots, offs_ref, tile_ref, own, first, group, both, *refs):
    lasts_ref, out_ref, picked, sems = refs
    slot = pl.program_id(0)

    @pl.when(slot == 0)
    def _():
        out_ref[...] = jnp.zeros_like(out_ref)
        for each in range(slots):
            sources = (own, first, group, both, lasts_ref.at[each])
            start_pick(offs_ref[0, each + 1], sources, picked.at[each], sems.at[each])

    pltpu.make_async_copy(own, picked.at[slot], sems.at[slot]).wait()
    mirror = jnp.where(offs_ref[0, slot + 1] > 0, 1.0, 0.0).astype(f32)
    out_ref[...] += mirror * dot3(split(picked[slot]), split(tile_ref[...]), NT)


def backward(offsets, tiles, sources):
    slots, block = tiles.shape[0] - 1, tiles.shape[1]
    own = sources[0]
    rows = own.shape[0]
    return pl.pallas_call(
        functools.partial(backward_kernel, slots),
        grid=(slots,),
        in_specs=[smem_spec(), pl.BlockSpec((None, block, block), lambda j: (j + 1, 0, 0))]
        + [any_spec()] * len(sources),
        out_specs=pl.BlockSpec((rows, block), lambda j: (0, 0)),
        out_shape=jax.ShapeDtypeStruct((rows, block), f32),
        scratch_shapes=[pltpu.VMEM((slots, rows, block), f32), pltpu.SemaphoreType.DMA((slots,))],
        compiler_params=params(),
        cost_estimate=cost(6 * slots * rows * block * block, 4 * slots * block * (block + rows)),
        name="backward",
    )(offsets, tiles, *sources)


def bins_kernel(slots, offs_ref, next_ref, own_in, mine_ref, theirs_ref, own_out, first, group, both, two):
    p, flip = place()
    target = last_partner(p, flip)
    totals = [own_in[...], None, None, None, None]
    for which, value in enumerate((0, 1, 2, 3, 5)):
        total = totals[which]
        for slot in range(slots):
            for there, offs, source in ((0, offs_ref, mine_ref), (1, next_ref, theirs_ref)):
                offset = offs[0, slot + 1]
                last, code = route(jnp.where(there == 1, target, p), offset, flip)
                use = (last == there) & (code == value) & (offset > 0)
                term = jnp.where(use, source[slot], 0.0)
                total = term if total is None else total + term
        totals[which] = total
    for ref, total in zip((own_out, first, group, both, two), totals):
        ref[...] = total


def make_bins(offsets, offsets_next, own, mine, theirs):
    slots, rows, block = mine.shape
    step = rows // 4
    flat = pl.BlockSpec((step, block), lambda i: (i, 0))
    deep = pl.BlockSpec((slots, step, block), lambda i: (0, i, 0))
    return pl.pallas_call(
        functools.partial(bins_kernel, slots),
        grid=(rows // step,),
        in_specs=[smem_spec(), smem_spec(), flat, deep, deep],
        out_specs=[flat] * 5,
        out_shape=[jax.ShapeDtypeStruct((rows, block), f32)] * 5,
        compiler_params=params(),
        cost_estimate=cost(20 * rows * block, 40 * rows * block),
        name="bins",
    )(offsets, offsets_next, own, mine, theirs)


def halves(pair):
    return lax.axis_index("samp") if pair else 0


def right_kernel(slots, pair, offs_ref, data_ref, image_ref, own, first, group, both, *refs):
    lasts_ref = refs[0]
    keep0_ref, send0_ref, keep_ref, send_ref, high_ref, low_ref, picked, sems = refs[-8:]
    for slot in range(slots):
        sources = (own, first, group, both, lasts_ref.at[slot])
        start_pick(offs_ref[0, slot + 1], sources, picked.at[slot], sems.at[slot])
    half = image_ref.shape[1] // 2
    samp = halves(pair)
    data = data_ref[...]
    image = image_ref[...]
    data_turned = split(data.T)
    high_ref[...], low_ref[...] = data_turned
    turned = split(image.T)
    image_pair, data_pair = split(image), split(data)

    def store(keep, send_out, which, total):
        lower, upper = total[:half], total[half:]

        @pl.when(samp == 0)
        def _():
            keep[which] = lower
            send_out[which] = upper

        @pl.when(samp != 0)
        def _():
            keep[which] = upper
            send_out[which] = lower

    store(keep0_ref, send0_ref, 0, dot3(turned, data_pair, NN) + dot3(data_turned, image_pair, NN))
    for slot in range(slots):
        pltpu.make_async_copy(own, picked.at[slot], sems.at[slot]).wait()
        store(keep_ref, send_ref, slot, dot3(turned, split(picked[slot]), NN))


def right(offsets, data, image, gate, sources, pair):
    slots = offsets.shape[1] - 1
    rows, block = data.shape
    part0 = jax.ShapeDtypeStruct((1, block // 2, block), f32)
    part = jax.ShapeDtypeStruct((slots, block // 2, block), f32)
    turned = jax.ShapeDtypeStruct((block, rows), bf16)
    return pl.pallas_call(
        functools.partial(right_kernel, slots, pair),
        in_specs=[smem_spec(), vmem_spec(), vmem_spec()] + [any_spec()] * (len(gate) + len(sources)),
        out_specs=[vmem_spec()] * 6,
        out_shape=[part0, part0, part, part, turned, turned],
        scratch_shapes=[pltpu.VMEM((slots, rows, block), f32), pltpu.SemaphoreType.DMA((slots,))],
        compiler_params=params(),
        cost_estimate=pl.CostEstimate(flops=400 * rows * block * block, bytes_accessed=0, transcendentals=0),
        name="right",
    )(offsets, data, image, *sources, *gate)


def left_kernel(slots, pair, offs_ref, keep_in, send_in, high_ref, low_ref, own, first, group, both, two, lasts_ref,
                keep_ref, send_ref, picked, sems):
    slot = pl.program_id(0)

    @pl.when(slot == 0)
    def _():
        for each in range(slots):
            sources = (own, first, group, both, lasts_ref.at[each], two)
            start_pick(offs_ref[0, each + 1], sources, picked.at[each], sems.at[each])

    pltpu.make_async_copy(own, picked.at[slot], sems.at[slot]).wait()
    half = send_ref.shape[0]
    mine = halves(pair) * half
    chosen = split(picked[slot])
    for out_ref, in_ref, row in ((send_ref, send_in, half - mine), (keep_ref, keep_in, mine)):
        rows = pl.ds(pl.multiple_of(row, half), half)
        out_ref[...] = in_ref[...] + dot3((high_ref[rows], low_ref[rows]), chosen, NN)


def left(offsets, parts, turned, sources, pair):
    keep = parts[0]
    slots, half = keep.shape[:2]
    block, rows = turned[0].shape
    spec = pl.BlockSpec((None, half, block), lambda j: (j, 0, 0))
    whole = pl.BlockSpec((block, rows), lambda j: (0, 0))
    part = jax.ShapeDtypeStruct(keep.shape, f32)
    return pl.pallas_call(
        functools.partial(left_kernel, slots, pair),
        grid=(slots,),
        in_specs=[smem_spec(), spec, spec, whole, whole] + [any_spec()] * len(sources),
        out_specs=[spec, spec],
        out_shape=[part, part],
        scratch_shapes=[pltpu.VMEM((slots, rows, block), f32), pltpu.SemaphoreType.DMA((slots,))],
        compiler_params=params(),
        cost_estimate=cost(6 * slots * rows * block * block, 4 * slots * block * (2 * block + rows)),
        name="left",
    )(offsets, *parts, *turned, *sources)


def finish_kernel(begin, factor, offs_ref, step_ref, tile_ref, keep_ref, other_ref, *refs):
    out_ref = refs[-1]
    slot = pl.program_id(0) + begin
    half, block = out_ref.shape
    step_size = step_ref[0]
    old = tile_ref[...]
    bound = step_size * penalty_weight
    stepped = old - (step_size * factor) * (keep_ref[...] + other_ref[...])

    def shrunk(value):
        return value - jnp.clip(value, -bound, bound)

    @pl.when(slot == 0)
    def _():
        rows = lax.axis_index("samp") * half + lax.broadcasted_iota(jnp.int32, (half, block), 0)
        on_diag = rows == lax.broadcasted_iota(jnp.int32, (half, block), 1)
        out_ref[...] = jnp.where(on_diag, stepped + step_size / jnp.where(on_diag, old, 1.0), shrunk(stepped))

    @pl.when(slot > 0)
    def _():
        out_ref[...] = jnp.where(offs_ref[0, slot] > 0, shrunk(stepped), 0.0)


def finish(offsets, step, tiles, keep, other, factor, begin, earlier=()):
    slots, block = tiles.shape[:2]
    count, half = keep.shape[:2]
    spec = pl.BlockSpec((None, half, block), lambda j: (j, 0, 0))
    tile_spec = pl.BlockSpec((None, half, block), lambda j: (j + begin, lax.axis_index("samp"), 0))
    return pl.pallas_call(
        functools.partial(finish_kernel, begin, factor),
        grid=(count,),
        in_specs=[smem_spec(), smem_spec(), tile_spec, spec, spec] + [any_spec()] * len(earlier),
        out_specs=pl.BlockSpec((None, half, block), lambda j: (j + begin, 0, 0)),
        out_shape=jax.ShapeDtypeStruct((slots, half, block), f32),
        input_output_aliases={5: 0} if earlier else {},
        compiler_params=params(),
        cost_estimate=cost(6 * keep.size, 16 * keep.size),
        name="finish",
    )(offsets, step, tiles, keep, other, *earlier)


def after(value, other):
    return lax.optimization_barrier((value, other))[0]


def swap(value):
    return lax.ppermute(value, "samp", [(0, 1), (1, 0)])


def shards(data, tiles, offsets, step):
    local_tiles = tiles[0]
    slot_count, block = local_tiles.shape[:2]
    samp_count = lax.axis_size("samp")
    pair = samp_count == 2
    factor = 1.0 / (2.0 * data.shape[0] * samp_count)

    offsets_next = send(offsets, "last")
    data_first = send(data, "first")
    own, far = forward(data, local_tiles)
    theirs = send(after(far, (offsets_next, data_first)), "last")
    data_both = send(data_first, "group")
    data_two = send(data_first, "column")
    data_group = send(data, "group")
    own, bin_first, bin_group, bin_both, bin_two = make_bins(offsets, offsets_next, own, far, theirs)
    got_both = send(bin_both, "first")
    got_two = send(bin_two, "two", reverse=True)
    chosen = choose(offsets_next, data, data_first, data_group, data_both, data_two)
    data_last = send(chosen, "last")
    data_sources = (data, data_first, data_group, data_both, data_last)

    bin_group = bin_group + got_both + got_two
    got_group = send(bin_group, "group", reverse=True)
    got_first = send(bin_first, "first")
    image = own + backward(offsets, local_tiles, data_sources) + got_first + got_group

    image_group = send(image, "group")
    image_first = send(image, "first")
    image_both = send(image_group, "first")
    chosen = choose(offsets_next, image, image_first, image_group, image_both)
    image_last = send(chosen, "last")
    keep0, other0, keep, other, high, low = right(offsets, data, image, (chosen,), data_sources, pair)
    image_two = send(after(image_both, chosen), "direct")
    image_sources = (image, image_first, image_group, image_both, image_two, image_last)

    if pair:
        result = finish(offsets, step, local_tiles, keep0, swap(other0), factor, 0)
        keep = after(keep, result)
    keep, other = left(offsets, (keep, other), (high, low), image_sources, pair)
    if pair:
        return finish(offsets, step, local_tiles, keep, swap(other), factor, 1, (result,))[None]
    keep, other = (jnp.concatenate(both) for both in ((keep0, keep), (other0, other)))
    summed = lax.psum_scatter(jnp.concatenate([keep, other], axis=1), "samp", scatter_dimension=1, tiled=True)
    none = jnp.zeros_like(summed)
    return finish(offsets, step, local_tiles, summed, none, factor, 0)[None]


def solution(mesh):
    return jax.shard_map(
        shards,
        mesh=mesh,
        in_specs=(P("samp", "var"), P("var", None, None, None), P("var", None), P()),
        out_specs=P("var", None, "samp", None),
        check_vma=False,
    )
```

```python
import functools

import jax
import jax.numpy as jnp
from jax import lax
from jax.experimental import pallas as pl
from jax.experimental.pallas import tpu as pltpu
from jax.sharding import PartitionSpec as P

penalty_weight = 0.05
BAND = 6
VMEM_LIMIT = 20 * 1024 * 1024
NN = (((1,), (0,)), ((), ()))
NT = (((1,), (1,)), ((), ()))
f32, bf16 = jnp.float32, jnp.bfloat16


def params(**kw):
    return pltpu.CompilerParams(vmem_limit_bytes=VMEM_LIMIT, **kw)


def cost(flops, nbytes):
    return pl.CostEstimate(flops=0, bytes_accessed=0, transcendentals=0)


def any_spec():
    return pl.BlockSpec(memory_space=pl.ANY)


def vmem_spec():
    return pl.BlockSpec(memory_space=pltpu.VMEM)


def smem_spec():
    return pl.BlockSpec(memory_space=pltpu.SMEM)


def split(value):
    high = value.astype(bf16)
    return high, (value - high.astype(f32)).astype(bf16)


def dot3(left, right, dims):
    dot = functools.partial(lax.dot_general, dimension_numbers=dims, preferred_element_type=f32)
    return dot(left[0], right[0]) + (dot(left[0], right[1]) + dot(left[1], right[0]))


def route(p, k, flip):
    xbit = k & 1
    ybit = (((p + k) >> 1) ^ (p >> 1)) & 1
    first = jnp.where(flip == 0, xbit, ybit)
    last = jnp.where(flip == 0, ybit, xbit)
    return last, first + 2 * ((p + k) >> 2)


def place():
    return lax.axis_index("var") & 3, lax.axis_index("samp") & 1


def last_partner(p, flip):
    return jnp.where(flip == 0, p ^ 2, p ^ 1)


def wanted(first, last, groups):
    found = set()
    for p in range(4):
        for k in range(1, BAND):
            bits = p ^ ((p + k) & 3)
            if bits & first and (p + k) >> 2 == groups:
                found.add(p ^ (bits & last))
    return found


def hop(var_count, samp_count, kind, reverse=False):
    pairs = []
    for var in range(var_count):
        for samp in range(samp_count):
            first, last = (2, 1) if samp & 1 else (1, 2)
            back = (var - 4) % var_count
            use = True
            if kind == "first":
                target = var ^ first
            elif kind == "last":
                target = var ^ last
            elif kind == "group":
                target = back
            elif kind == "two":
                target = back ^ first
                use = (var & 3) == 0
            elif kind == "column":
                target = (var - 8) % var_count
                use = (var & 3) in wanted(first, last, 2)
            else:
                target = back ^ last
                use = (var & 3) in wanted(first, last, 2)
            pair = (var * samp_count + samp, target * samp_count + samp)
            if use:
                pairs.append(pair[::-1] if reverse else pair)
    return pairs


def send(value, kind, reverse=False):
    pairs = hop(lax.axis_size("var"), lax.axis_size("samp"), kind, reverse)
    return lax.ppermute(value, ("var", "samp"), pairs)


def forward_kernel(data_ref, tile_ref, *out_refs):
    slot = pl.program_id(0)
    value = dot3(split(data_ref[...]), split(tile_ref[...]), NN)
    for which, ref in enumerate(out_refs):

        @pl.when(slot == which)
        def _():
            ref[...] = value


def forward(data, tiles):
    slots, block = tiles.shape[:2]
    rows = data.shape[0]
    flat = pl.BlockSpec((rows, block), lambda j: (0, 0))
    return pl.pallas_call(
        forward_kernel,
        grid=(slots,),
        in_specs=[flat, pl.BlockSpec((None, block, block), lambda j: (j, 0, 0))],
        out_specs=[flat] * slots,
        out_shape=[jax.ShapeDtypeStruct((rows, block), f32)] * slots,
        compiler_params=params(),
        cost_estimate=cost(6 * slots * rows * block * block, 4 * slots * block * (block + 2 * rows)),
        name="forward",
    )(data, tiles)


CODES = (0, 1, 2, 3, 5)


def choose_kernel(slots, count, offs_ref, *refs):
    sources, (out, sems) = refs[:count], refs[count:]
    p, flip = place()
    target = last_partner(p, flip)
    copies = []
    for slot in range(slots):
        last, code = route(target, offs_ref[0, slot + 1], flip)
        for value, source in zip(CODES, sources):
            copy = pltpu.make_async_copy(source, out.at[slot], sems.at[slot])
            pl.when((last == 1) & (code == value))(copy.start)
        known = (last == 1) & (code <= CODES[count - 1])
        copies.append((known, pltpu.make_async_copy(sources[0], out.at[slot], sems.at[slot])))
    for known, copy in copies:
        pl.when(known)(copy.wait)


def choose(offsets_next, *sources):
    slots = offsets_next.shape[1] - 1
    own = sources[0]
    return pl.pallas_call(
        functools.partial(choose_kernel, slots, len(sources)),
        in_specs=[smem_spec()] + [any_spec()] * len(sources),
        out_specs=any_spec(),
        out_shape=jax.ShapeDtypeStruct((slots,) + own.shape, f32),
        scratch_shapes=[pltpu.SemaphoreType.DMA((slots,))],
        compiler_params=params(),
        cost_estimate=cost(0, 8 * slots * own.size),
        name="choose",
    )(offsets_next, *sources)


def start_pick(offset, sources, target, sem):
    p, flip = place()
    last, code = route(p, offset, flip)
    for value, source in zip(CODES[:4], sources[:4]):
        pl.when((last == 0) & (code == value))(pltpu.make_async_copy(source, target, sem).start)
    over_last = last == 1
    if len(sources) > 5:
        over_last = over_last & (code != CODES[4])
        pl.when(code == CODES[4])(pltpu.make_async_copy(sources[5], target, sem).start)
    pl.when(over_last)(pltpu.make_async_copy(sources[4], target, sem).start)


def backward_kernel(slots, offs_ref, tile_ref, own, first, group, both, *refs):
    lasts_ref, out_ref, picked, sems = refs
    slot = pl.program_id(0)

    @pl.when(slot == 0)
    def _():
        out_ref[...] = jnp.zeros_like(out_ref)
        for each in range(slots):
            sources = (own, first, group, both, lasts_ref.at[each])
            start_pick(offs_ref[0, each + 1], sources, picked.at[each], sems.at[each])

    pltpu.make_async_copy(own, picked.at[slot], sems.at[slot]).wait()
    mirror = jnp.where(offs_ref[0, slot + 1] > 0, 1.0, 0.0).astype(f32)
    out_ref[...] += mirror * dot3(split(picked[slot]), split(tile_ref[...]), NT)


def backward(offsets, tiles, sources):
    slots, block = tiles.shape[0] - 1, tiles.shape[1]
    own = sources[0]
    rows = own.shape[0]
    return pl.pallas_call(
        functools.partial(backward_kernel, slots),
        grid=(slots,),
        in_specs=[smem_spec(), pl.BlockSpec((None, block, block), lambda j: (j + 1, 0, 0))]
        + [any_spec()] * len(sources),
        out_specs=pl.BlockSpec((rows, block), lambda j: (0, 0)),
        out_shape=jax.ShapeDtypeStruct((rows, block), f32),
        scratch_shapes=[pltpu.VMEM((slots, rows, block), f32), pltpu.SemaphoreType.DMA((slots,))],
        compiler_params=params(),
        cost_estimate=cost(6 * slots * rows * block * block, 4 * slots * block * (block + rows)),
        name="backward",
    )(offsets, tiles, *sources)


def bins_kernel(slots, offs_ref, next_ref, own_in, *refs):
    p, flip = place()
    target = last_partner(p, flip)
    mine, theirs, outs = refs[:slots], refs[slots : 2 * slots], refs[2 * slots :]
    totals = [own_in[...], None, None, None, None]
    for which, value in enumerate((0, 1, 2, 3, 5)):
        total = totals[which]
        for slot in range(slots):
            for there, offs, source in ((0, offs_ref, mine), (1, next_ref, theirs)):
                offset = offs[0, slot + 1]
                last, code = route(jnp.where(there == 1, target, p), offset, flip)
                use = (last == there) & (code == value) & (offset > 0)
                term = jnp.where(use, source[slot][...], 0.0)
                total = term if total is None else total + term
        totals[which] = total
    for ref, total in zip(outs, totals):
        ref[...] = total


def make_bins(offsets, offsets_next, own, mine, theirs):
    slots = len(mine)
    rows, block = own.shape
    step = rows // 4
    flat = pl.BlockSpec((step, block), lambda i: (i, 0))
    return pl.pallas_call(
        functools.partial(bins_kernel, slots),
        grid=(rows // step,),
        in_specs=[smem_spec(), smem_spec()] + [flat] * (1 + 2 * slots),
        out_specs=[flat] * 5,
        out_shape=[jax.ShapeDtypeStruct((rows, block), f32)] * 5,
        compiler_params=params(),
        cost_estimate=cost(20 * rows * block, 40 * rows * block),
        name="bins",
    )(offsets, offsets_next, own, *mine, *theirs)


def halves(pair):
    return lax.axis_index("samp") if pair else 0


def right_kernel(slots, pair, offs_ref, data_ref, image_ref, own, first, group, both, *refs):
    lasts_ref = refs[0]
    keep0_ref, send0_ref, keep_ref, send_ref, high_ref, low_ref, picked, sems = refs[-8:]
    for slot in range(slots):
        sources = (own, first, group, both, lasts_ref.at[slot])
        start_pick(offs_ref[0, slot + 1], sources, picked.at[slot], sems.at[slot])
    half = image_ref.shape[1] // 2
    samp = halves(pair)
    data = data_ref[...]
    image = image_ref[...]
    data_turned = split(data.T)
    high_ref[...], low_ref[...] = data_turned
    turned = split(image.T)
    image_pair, data_pair = split(image), split(data)

    def store(keep, send_out, which, total):
        lower, upper = total[:half], total[half:]

        @pl.when(samp == 0)
        def _():
            keep[which] = lower
            send_out[which] = upper

        @pl.when(samp != 0)
        def _():
            keep[which] = upper
            send_out[which] = lower

    store(keep0_ref, send0_ref, 0, dot3(turned, data_pair, NN) + dot3(data_turned, image_pair, NN))
    for slot in range(slots):
        pltpu.make_async_copy(own, picked.at[slot], sems.at[slot]).wait()
        store(keep_ref, send_ref, slot, dot3(turned, split(picked[slot]), NN))


def right(offsets, data, image, gate, sources, pair):
    slots = offsets.shape[1] - 1
    rows, block = data.shape
    part0 = jax.ShapeDtypeStruct((1, block // 2, block), f32)
    part = jax.ShapeDtypeStruct((slots, block // 2, block), f32)
    turned = jax.ShapeDtypeStruct((block, rows), bf16)
    return pl.pallas_call(
        functools.partial(right_kernel, slots, pair),
        in_specs=[smem_spec(), vmem_spec(), vmem_spec()] + [any_spec()] * (len(gate) + len(sources)),
        out_specs=[vmem_spec()] * 6,
        out_shape=[part0, part0, part, part, turned, turned],
        scratch_shapes=[pltpu.VMEM((slots, rows, block), f32), pltpu.SemaphoreType.DMA((slots,))],
        compiler_params=params(),
        cost_estimate=pl.CostEstimate(flops=400 * rows * block * block, bytes_accessed=0, transcendentals=0),
        name="right",
    )(offsets, data, image, *sources, *gate)


def left_kernel(slots, pair, offs_ref, keep_in, send_in, high_ref, low_ref, own, first, group, both, two, lasts_ref,
                keep_ref, send_ref, picked, sems):
    slot = pl.program_id(0)

    @pl.when(slot == 0)
    def _():
        for each in range(slots):
            sources = (own, first, group, both, lasts_ref.at[each], two)
            start_pick(offs_ref[0, each + 1], sources, picked.at[each], sems.at[each])

    pltpu.make_async_copy(own, picked.at[slot], sems.at[slot]).wait()
    half = send_ref.shape[0]
    mine = halves(pair) * half
    chosen = split(picked[slot])
    for out_ref, in_ref, row in ((send_ref, send_in, half - mine), (keep_ref, keep_in, mine)):
        rows = pl.ds(pl.multiple_of(row, half), half)
        out_ref[...] = in_ref[...] + dot3((high_ref[rows], low_ref[rows]), chosen, NN)


def left(offsets, parts, turned, sources, pair):
    keep = parts[0]
    slots, half = keep.shape[:2]
    block, rows = turned[0].shape
    spec = pl.BlockSpec((None, half, block), lambda j: (j, 0, 0))
    whole = pl.BlockSpec((block, rows), lambda j: (0, 0))
    part = jax.ShapeDtypeStruct(keep.shape, f32)
    return pl.pallas_call(
        functools.partial(left_kernel, slots, pair),
        grid=(slots,),
        in_specs=[smem_spec(), spec, spec, whole, whole] + [any_spec()] * len(sources),
        out_specs=[spec, spec],
        out_shape=[part, part],
        scratch_shapes=[pltpu.VMEM((slots, rows, block), f32), pltpu.SemaphoreType.DMA((slots,))],
        compiler_params=params(),
        cost_estimate=cost(6 * slots * rows * block * block, 4 * slots * block * (2 * block + rows)),
        name="left",
    )(offsets, *parts, *turned, *sources)


def finish_kernel(begin, factor, offs_ref, step_ref, tile_ref, keep_ref, other_ref, *refs):
    out_ref = refs[-1]
    slot = pl.program_id(0) + begin
    half, block = out_ref.shape
    step_size = step_ref[0]
    old = tile_ref[...]
    bound = step_size * penalty_weight
    stepped = old - (step_size * factor) * (keep_ref[...] + other_ref[...])

    def shrunk(value):
        return value - jnp.clip(value, -bound, bound)

    @pl.when(slot == 0)
    def _():
        rows = lax.axis_index("samp") * half + lax.broadcasted_iota(jnp.int32, (half, block), 0)
        on_diag = rows == lax.broadcasted_iota(jnp.int32, (half, block), 1)
        out_ref[...] = jnp.where(on_diag, stepped + step_size / jnp.where(on_diag, old, 1.0), shrunk(stepped))

    @pl.when(slot > 0)
    def _():
        out_ref[...] = jnp.where(offs_ref[0, slot] > 0, shrunk(stepped), 0.0)


def finish(offsets, step, tiles, keep, other, factor, begin, earlier=()):
    slots, block = tiles.shape[:2]
    count, half = keep.shape[:2]
    spec = pl.BlockSpec((None, half, block), lambda j: (j, 0, 0))
    tile_spec = pl.BlockSpec((None, half, block), lambda j: (j + begin, lax.axis_index("samp"), 0))
    return pl.pallas_call(
        functools.partial(finish_kernel, begin, factor),
        grid=(count,),
        in_specs=[smem_spec(), smem_spec(), tile_spec, spec, spec] + [any_spec()] * len(earlier),
        out_specs=pl.BlockSpec((None, half, block), lambda j: (j + begin, 0, 0)),
        out_shape=jax.ShapeDtypeStruct((slots, half, block), f32),
        input_output_aliases={5: 0} if earlier else {},
        compiler_params=params(),
        cost_estimate=cost(6 * keep.size, 16 * keep.size),
        name="finish",
    )(offsets, step, tiles, keep, other, *earlier)


def after(value, other):
    return lax.optimization_barrier((value, other))[0]


def swap(value):
    return lax.ppermute(value, "samp", [(0, 1), (1, 0)])


def shards(data, tiles, offsets, step):
    local_tiles = tiles[0]
    slot_count, block = local_tiles.shape[:2]
    samp_count = lax.axis_size("samp")
    pair = samp_count == 2
    factor = 1.0 / (2.0 * data.shape[0] * samp_count)

    offsets_next = send(offsets, "last")
    data_first = send(data, "first")
    own, *far = forward(data, local_tiles)
    theirs = [send(after(each, (offsets_next, data_first)), "last") for each in far]
    data_group = send(data, "group")
    data_both = send(data_group, "first")
    data_two = send(data_first, "column")
    own, bin_first, bin_group, bin_both, bin_two = make_bins(offsets, offsets_next, own, far, theirs)
    got_both = send(bin_both, "first")
    got_two = send(bin_two, "two", reverse=True)
    chosen = choose(offsets_next, data, data_first, data_group, data_both, data_two)
    data_last = send(chosen, "last")
    data_sources = (data, data_first, data_group, data_both, data_last)

    bin_group = bin_group + got_both + got_two
    got_group = send(bin_group, "group", reverse=True)
    got_first = send(bin_first, "first")
    image = own + backward(offsets, local_tiles, data_sources) + got_first + got_group

    image_group = send(image, "group")
    image_first = send(image, "first")
    image_both = send(image_group, "first")
    chosen = choose(offsets_next, image, image_first, image_group, image_both)
    image_last = send(chosen, "last")
    keep0, other0, keep, other, high, low = right(offsets, data, image, (chosen,), data_sources, pair)
    image_two = send(after(image_both, chosen), "direct")
    image_sources = (image, image_first, image_group, image_both, image_two, image_last)

    if pair:
        result = finish(offsets, step, local_tiles, keep0, swap(other0), factor, 0)
        keep = after(keep, result)
    keep, other = left(offsets, (keep, other), (high, low), image_sources, pair)
    if pair:
        return finish(offsets, step, local_tiles, keep, swap(other), factor, 1, (result,))[None]
    keep, other = (jnp.concatenate(both) for both in ((keep0, keep), (other0, other)))
    summed = lax.psum_scatter(jnp.concatenate([keep, other], axis=1), "samp", scatter_dimension=1, tiled=True)
    none = jnp.zeros_like(summed)
    return finish(offsets, step, local_tiles, summed, none, factor, 0)[None]


def solution(mesh):
    return jax.shard_map(
        shards,
        mesh=mesh,
        in_specs=(P("samp", "var"), P("var", None, None, None), P("var", None), P()),
        out_specs=P("var", None, "samp", None),
        check_vma=False,
    )
```

```python
import functools

import jax
import jax.numpy as jnp
from jax import lax
from jax.experimental import pallas as pl
from jax.experimental.pallas import tpu as pltpu
from jax.sharding import PartitionSpec as P

penalty_weight = 0.05
BAND = 6
PARTS = 2
VMEM_LIMIT = 20 * 1024 * 1024
NN = (((1,), (0,)), ((), ()))
NT = (((1,), (1,)), ((), ()))
f32, bf16 = jnp.float32, jnp.bfloat16


def params(**kw):
    return pltpu.CompilerParams(vmem_limit_bytes=VMEM_LIMIT, **kw)


def cost(flops, nbytes):
    return pl.CostEstimate(flops=0, bytes_accessed=0, transcendentals=0)


def any_spec():
    return pl.BlockSpec(memory_space=pl.ANY)


def vmem_spec():
    return pl.BlockSpec(memory_space=pltpu.VMEM)


def smem_spec():
    return pl.BlockSpec(memory_space=pltpu.SMEM)


def split(value):
    high = value.astype(bf16)
    return high, (value - high.astype(f32)).astype(bf16)


def dot3(left, right, dims):
    dot = functools.partial(lax.dot_general, dimension_numbers=dims, preferred_element_type=f32)
    return dot(left[0], right[0]) + (dot(left[0], right[1]) + dot(left[1], right[0]))


def route(p, k, flip):
    xbit = k & 1
    ybit = (((p + k) >> 1) ^ (p >> 1)) & 1
    first = jnp.where(flip == 0, xbit, ybit)
    last = jnp.where(flip == 0, ybit, xbit)
    return last, first + 2 * ((p + k) >> 2)


def place():
    return lax.axis_index("var") & 3, lax.axis_index("samp") & 1


def last_partner(p, flip):
    return jnp.where(flip == 0, p ^ 2, p ^ 1)


def wanted(first, last, groups):
    found = set()
    for p in range(4):
        for k in range(1, BAND):
            bits = p ^ ((p + k) & 3)
            if bits & first and (p + k) >> 2 == groups:
                found.add(p ^ (bits & last))
    return found


def hop(var_count, samp_count, kind, reverse=False):
    pairs = []
    for var in range(var_count):
        for samp in range(samp_count):
            first, last = (2, 1) if samp & 1 else (1, 2)
            back = (var - 4) % var_count
            use = True
            if kind == "first":
                target = var ^ first
            elif kind == "last":
                target = var ^ last
            elif kind == "group":
                target = back
            elif kind == "two":
                target = back ^ first
                use = (var & 3) == 0
            elif kind == "column":
                target = (var - 8) % var_count
                use = (var & 3) in wanted(first, last, 2)
            else:
                target = back ^ last
                use = (var & 3) in wanted(first, last, 2)
            pair = (var * samp_count + samp, target * samp_count + samp)
            if use:
                pairs.append(pair[::-1] if reverse else pair)
    return pairs


def send(value, kind, reverse=False):
    pairs = hop(lax.axis_size("var"), lax.axis_size("samp"), kind, reverse)
    return lax.ppermute(value, ("var", "samp"), pairs)


def forward_kernel(data_ref, tile_ref, *out_refs):
    slot = pl.program_id(0)
    value = dot3(split(data_ref[...]), split(tile_ref[...]), NN)
    for which, ref in enumerate(out_refs):

        @pl.when(slot == which)
        def _():
            ref[...] = value


def forward(data, tiles):
    slots, block = tiles.shape[:2]
    rows = data.shape[0]
    flat = pl.BlockSpec((rows, block), lambda j: (0, 0))
    return pl.pallas_call(
        forward_kernel,
        grid=(slots,),
        in_specs=[flat, pl.BlockSpec((None, block, block), lambda j: (j, 0, 0))],
        out_specs=[flat] * slots,
        out_shape=[jax.ShapeDtypeStruct((rows, block), f32)] * slots,
        compiler_params=params(),
        cost_estimate=cost(6 * slots * rows * block * block, 4 * slots * block * (block + 2 * rows)),
        name="forward",
    )(data, tiles)


CODES = (0, 1, 2, 3, 5)


def choose_kernel(slots, count, part, offs_ref, *refs):
    sources, (out, sems) = refs[:count], refs[count:]
    size = out.shape[1]
    sources = [ref if ref.shape[0] == size else ref.at[pl.ds(part * size, size)] for ref in sources]
    p, flip = place()
    target = last_partner(p, flip)
    copies = []
    for slot in range(slots):
        last, code = route(target, offs_ref[0, slot + 1], flip)
        for value, source in zip(CODES, sources):
            copy = pltpu.make_async_copy(source, out.at[slot], sems.at[slot])
            pl.when((last == 1) & (code == value))(copy.start)
        known = (last == 1) & (code <= CODES[count - 1])
        copies.append((known, pltpu.make_async_copy(sources[0], out.at[slot], sems.at[slot])))
    for known, copy in copies:
        pl.when(known)(copy.wait)


def choose(offsets_next, *sources, part=0):
    slots = offsets_next.shape[1] - 1
    shape = sources[3].shape
    return pl.pallas_call(
        functools.partial(choose_kernel, slots, len(sources), part),
        in_specs=[smem_spec()] + [any_spec()] * len(sources),
        out_specs=any_spec(),
        out_shape=jax.ShapeDtypeStruct((slots,) + shape, f32),
        scratch_shapes=[pltpu.SemaphoreType.DMA((slots,))],
        compiler_params=params(),
        cost_estimate=cost(0, 8 * slots * shape[0] * shape[1]),
        name="choose",
    )(offsets_next, *sources)


def start_pick(offset, sources, target, sem):
    p, flip = place()
    last, code = route(p, offset, flip)
    for value, source in zip(CODES[:4], sources[:4]):
        pl.when((last == 0) & (code == value))(pltpu.make_async_copy(source, target, sem).start)
    over_last = last == 1
    if len(sources) > 5:
        over_last = over_last & (code != CODES[4])
        pl.when(code == CODES[4])(pltpu.make_async_copy(sources[5], target, sem).start)
    pl.when(over_last)(pltpu.make_async_copy(sources[4], target, sem).start)


def backward_kernel(slots, offs_ref, tile_ref, own, first, group, both, *refs):
    lasts_ref, out_ref, picked, sems = refs
    slot = pl.program_id(0)

    @pl.when(slot == 0)
    def _():
        out_ref[...] = jnp.zeros_like(out_ref)
        for each in range(slots):
            sources = (own, first, group, both, lasts_ref.at[each])
            start_pick(offs_ref[0, each + 1], sources, picked.at[each], sems.at[each])

    pltpu.make_async_copy(own, picked.at[slot], sems.at[slot]).wait()
    mirror = jnp.where(offs_ref[0, slot + 1] > 0, 1.0, 0.0).astype(f32)
    out_ref[...] += mirror * dot3(split(picked[slot]), split(tile_ref[...]), NT)


def backward(offsets, tiles, sources):
    slots, block = tiles.shape[0] - 1, tiles.shape[1]
    own = sources[0]
    rows = own.shape[0]
    return pl.pallas_call(
        functools.partial(backward_kernel, slots),
        grid=(slots,),
        in_specs=[smem_spec(), pl.BlockSpec((None, block, block), lambda j: (j + 1, 0, 0))]
        + [any_spec()] * len(sources),
        out_specs=pl.BlockSpec((rows, block), lambda j: (0, 0)),
        out_shape=jax.ShapeDtypeStruct((rows, block), f32),
        scratch_shapes=[pltpu.VMEM((slots, rows, block), f32), pltpu.SemaphoreType.DMA((slots,))],
        compiler_params=params(),
        cost_estimate=cost(6 * slots * rows * block * block, 4 * slots * block * (block + rows)),
        name="backward",
    )(offsets, tiles, *sources)


def bins_kernel(slots, offs_ref, next_ref, own_in, *refs):
    p, flip = place()
    target = last_partner(p, flip)
    mine, theirs, outs = refs[:slots], refs[slots : 2 * slots], refs[2 * slots :]
    totals = [own_in[...], None, None, None, None]
    for which, value in enumerate((0, 1, 2, 3, 5)):
        total = totals[which]
        for slot in range(slots):
            for there, offs, source in ((0, offs_ref, mine), (1, next_ref, theirs)):
                offset = offs[0, slot + 1]
                last, code = route(jnp.where(there == 1, target, p), offset, flip)
                use = (last == there) & (code == value) & (offset > 0)
                term = jnp.where(use, source[slot][...], 0.0)
                total = term if total is None else total + term
        totals[which] = total
    for ref, total in zip(outs, totals):
        ref[...] = total


def make_bins(offsets, offsets_next, own, mine, theirs):
    slots = len(mine)
    rows, block = own.shape
    step = rows // 4
    flat = pl.BlockSpec((step, block), lambda i: (i, 0))
    return pl.pallas_call(
        functools.partial(bins_kernel, slots),
        grid=(rows // step,),
        in_specs=[smem_spec(), smem_spec()] + [flat] * (1 + 2 * slots),
        out_specs=[flat] * 5,
        out_shape=[jax.ShapeDtypeStruct((rows, block), f32)] * 5,
        compiler_params=params(),
        cost_estimate=cost(20 * rows * block, 40 * rows * block),
        name="bins",
    )(offsets, offsets_next, own, *mine, *theirs)


def halves(pair):
    return lax.axis_index("samp") if pair else 0


def right_kernel(slots, pair, offs_ref, data_ref, image_ref, own, first, group, both, *refs):
    lasts_ref = refs[0]
    keep0_ref, send0_ref, keep_ref, send_ref, high_ref, low_ref, picked, sems = refs[-8:]
    for slot in range(slots):
        sources = (own, first, group, both, lasts_ref.at[slot])
        start_pick(offs_ref[0, slot + 1], sources, picked.at[slot], sems.at[slot])
    half = image_ref.shape[1] // 2
    samp = halves(pair)
    data = data_ref[...]
    image = image_ref[...]
    data_turned = split(data.T)
    high_ref[...], low_ref[...] = data_turned
    turned = split(image.T)
    image_pair, data_pair = split(image), split(data)

    def store(keep, send_out, which, total):
        lower, upper = total[:half], total[half:]

        @pl.when(samp == 0)
        def _():
            keep[which] = lower
            send_out[which] = upper

        @pl.when(samp != 0)
        def _():
            keep[which] = upper
            send_out[which] = lower

    store(keep0_ref, send0_ref, 0, dot3(turned, data_pair, NN) + dot3(data_turned, image_pair, NN))
    for slot in range(slots):
        pltpu.make_async_copy(own, picked.at[slot], sems.at[slot]).wait()
        store(keep_ref, send_ref, slot, dot3(turned, split(picked[slot]), NN))


def right(offsets, data, image, gate, sources, pair):
    slots = offsets.shape[1] - 1
    rows, block = data.shape
    part0 = jax.ShapeDtypeStruct((1, block // 2, block), f32)
    part = jax.ShapeDtypeStruct((slots, block // 2, block), f32)
    turned = jax.ShapeDtypeStruct((block, rows), bf16)
    return pl.pallas_call(
        functools.partial(right_kernel, slots, pair),
        in_specs=[smem_spec(), vmem_spec(), vmem_spec()] + [any_spec()] * (len(gate) + len(sources)),
        out_specs=[vmem_spec()] * 6,
        out_shape=[part0, part0, part, part, turned, turned],
        scratch_shapes=[pltpu.VMEM((slots, rows, block), f32), pltpu.SemaphoreType.DMA((slots,))],
        compiler_params=params(),
        cost_estimate=pl.CostEstimate(flops=400 * rows * block * block, bytes_accessed=0, transcendentals=0),
        name="right",
    )(offsets, data, image, *sources, *gate)


def left_kernel(slots, pair, offs_ref, keep_in, send_in, high_ref, low_ref, own, first, *refs):
    slot = pl.program_id(0)
    keep_ref, send_ref, picked, sems = refs[-4:]
    parts = (len(refs) - 4) // 4
    groups, boths, twos, lasts = (refs[i * parts : (i + 1) * parts] for i in range(4))
    size = groups[0].shape[0]

    @pl.when(slot == 0)
    def _():
        for each in range(slots):
            for part in range(parts):
                rows = pl.ds(part * size, size)
                sources = (own.at[rows], first.at[rows], groups[part], boths[part], lasts[part].at[each], twos[part])
                start_pick(offs_ref[0, each + 1], sources, picked.at[each, rows], sems.at[each])

    pltpu.make_async_copy(own, picked.at[slot], sems.at[slot]).wait()
    half = send_ref.shape[0]
    mine = halves(pair) * half
    chosen = split(picked[slot])
    for out_ref, in_ref, row in ((send_ref, send_in, half - mine), (keep_ref, keep_in, mine)):
        rows = pl.ds(pl.multiple_of(row, half), half)
        out_ref[...] = in_ref[...] + dot3((high_ref[rows], low_ref[rows]), chosen, NN)


def left(offsets, parts, turned, sources, pair):
    keep = parts[0]
    slots, half = keep.shape[:2]
    block, rows = turned[0].shape
    spec = pl.BlockSpec((None, half, block), lambda j: (j, 0, 0))
    whole = pl.BlockSpec((block, rows), lambda j: (0, 0))
    part = jax.ShapeDtypeStruct(keep.shape, f32)
    return pl.pallas_call(
        functools.partial(left_kernel, slots, pair),
        grid=(slots,),
        in_specs=[smem_spec(), spec, spec, whole, whole] + [any_spec()] * len(sources),
        out_specs=[spec, spec],
        out_shape=[part, part],
        scratch_shapes=[pltpu.VMEM((slots, rows, block), f32), pltpu.SemaphoreType.DMA((slots,))],
        compiler_params=params(),
        cost_estimate=cost(6 * slots * rows * block * block, 4 * slots * block * (2 * block + rows)),
        name="left",
    )(offsets, *parts, *turned, *sources)


def finish_kernel(begin, factor, offs_ref, step_ref, tile_ref, keep_ref, other_ref, *refs):
    out_ref = refs[-1]
    slot = pl.program_id(0) + begin
    half, block = out_ref.shape
    step_size = step_ref[0]
    old = tile_ref[...]
    bound = step_size * penalty_weight
    stepped = old - (step_size * factor) * (keep_ref[...] + other_ref[...])

    def shrunk(value):
        return value - jnp.clip(value, -bound, bound)

    @pl.when(slot == 0)
    def _():
        rows = lax.axis_index("samp") * half + lax.broadcasted_iota(jnp.int32, (half, block), 0)
        on_diag = rows == lax.broadcasted_iota(jnp.int32, (half, block), 1)
        out_ref[...] = jnp.where(on_diag, stepped + step_size / jnp.where(on_diag, old, 1.0), shrunk(stepped))

    @pl.when(slot > 0)
    def _():
        out_ref[...] = jnp.where(offs_ref[0, slot] > 0, shrunk(stepped), 0.0)


def finish(offsets, step, tiles, keep, other, factor, begin, earlier=()):
    slots, block = tiles.shape[:2]
    count, half = keep.shape[:2]
    spec = pl.BlockSpec((None, half, block), lambda j: (j, 0, 0))
    tile_spec = pl.BlockSpec((None, half, block), lambda j: (j + begin, lax.axis_index("samp"), 0))
    return pl.pallas_call(
        functools.partial(finish_kernel, begin, factor),
        grid=(count,),
        in_specs=[smem_spec(), smem_spec(), tile_spec, spec, spec] + [any_spec()] * len(earlier),
        out_specs=pl.BlockSpec((None, half, block), lambda j: (j + begin, 0, 0)),
        out_shape=jax.ShapeDtypeStruct((slots, half, block), f32),
        input_output_aliases={5: 0} if earlier else {},
        compiler_params=params(),
        cost_estimate=cost(6 * keep.size, 16 * keep.size),
        name="finish",
    )(offsets, step, tiles, keep, other, *earlier)


def after(value, other):
    return lax.optimization_barrier((value, other))[0]


def swap(value):
    return lax.ppermute(value, "samp", [(0, 1), (1, 0)])


def shards(data, tiles, offsets, step):
    local_tiles = tiles[0]
    slot_count, block = local_tiles.shape[:2]
    samp_count = lax.axis_size("samp")
    pair = samp_count == 2
    factor = 1.0 / (2.0 * data.shape[0] * samp_count)

    offsets_next = send(offsets, "last")
    data_first = send(data, "first")
    own, *far = forward(data, local_tiles)
    theirs = [send(after(each, (offsets_next, data_first)), "last") for each in far]
    data_group = send(data, "group")
    data_both = send(data_group, "first")
    data_two = send(data_first, "column")
    own, bin_first, bin_group, bin_both, bin_two = make_bins(offsets, offsets_next, own, far, theirs)
    got_both = send(bin_both, "first")
    got_two = send(bin_two, "two", reverse=True)
    chosen = choose(offsets_next, data, data_first, data_group, data_both, data_two)
    data_last = send(chosen, "last")
    data_sources = (data, data_first, data_group, data_both, data_last)

    bin_group = bin_group + got_both + got_two
    got_group = send(bin_group, "group", reverse=True)
    got_first = send(bin_first, "first")
    image = own + backward(offsets, local_tiles, data_sources) + got_first + got_group

    size = image.shape[0] // PARTS
    image_groups = [send(image[part * size : (part + 1) * size], "group") for part in range(PARTS)]
    image_first = send(image, "first")
    image_boths = [send(each, "first") for each in image_groups]
    image_lasts, ready = [], after(offsets_next, image_groups[-1])
    for part in range(PARTS):
        chosen = choose(ready, image, image_first, image_groups[part], image_boths[part], part=part)
        image_lasts.append(send(chosen, "last"))
        ready = after(offsets_next, image_lasts[-1])
    keep0, other0, keep, other, high, low = right(offsets, data, image, (chosen,), data_sources, pair)
    image_twos = [send(after(each, chosen), "direct") for each in image_boths]
    image_sources = (image, image_first, *image_groups, *image_boths, *image_twos, *image_lasts)

    if pair:
        result = finish(offsets, step, local_tiles, keep0, swap(other0), factor, 0)
    keep, other = left(offsets, (keep, other), (high, low), image_sources, pair)
    if pair:
        return finish(offsets, step, local_tiles, keep, swap(other), factor, 1, (result,))[None]
    keep, other = (jnp.concatenate(both) for both in ((keep0, keep), (other0, other)))
    summed = lax.psum_scatter(jnp.concatenate([keep, other], axis=1), "samp", scatter_dimension=1, tiled=True)
    none = jnp.zeros_like(summed)
    return finish(offsets, step, local_tiles, summed, none, factor, 0)[None]


def solution(mesh):
    return jax.shard_map(
        shards,
        mesh=mesh,
        in_specs=(P("samp", "var"), P("var", None, None, None), P("var", None), P()),
        out_specs=P("var", None, "samp", None),
        check_vma=False,
    )
```

```python
import functools

import jax
import jax.numpy as jnp
from jax import lax
from jax.experimental import pallas as pl
from jax.experimental.pallas import tpu as pltpu
from jax.sharding import PartitionSpec as P

penalty_weight = 0.05
BAND = 6
VMEM_LIMIT = 20 * 1024 * 1024
NN = (((1,), (0,)), ((), ()))
NT = (((1,), (1,)), ((), ()))
f32, bf16 = jnp.float32, jnp.bfloat16


def params(**kw):
    return pltpu.CompilerParams(vmem_limit_bytes=VMEM_LIMIT, **kw)


def cost(flops, nbytes):
    return pl.CostEstimate(flops=0, bytes_accessed=0, transcendentals=0)


def any_spec():
    return pl.BlockSpec(memory_space=pl.ANY)


def vmem_spec():
    return pl.BlockSpec(memory_space=pltpu.VMEM)


def smem_spec():
    return pl.BlockSpec(memory_space=pltpu.SMEM)


def split(value):
    high = value.astype(bf16)
    return high, (value - high.astype(f32)).astype(bf16)


def dot3(left, right, dims):
    dot = functools.partial(lax.dot_general, dimension_numbers=dims, preferred_element_type=f32)
    return dot(left[0], right[0]) + (dot(left[0], right[1]) + dot(left[1], right[0]))


def route(p, k, flip):
    xbit = k & 1
    ybit = (((p + k) >> 1) ^ (p >> 1)) & 1
    first = jnp.where(flip == 0, xbit, ybit)
    last = jnp.where(flip == 0, ybit, xbit)
    return last, first + 2 * ((p + k) >> 2)


def place():
    return lax.axis_index("var") & 3, lax.axis_index("samp") & 1


def last_partner(p, flip):
    return jnp.where(flip == 0, p ^ 2, p ^ 1)


def wanted(first, last, groups):
    found = set()
    for p in range(4):
        for k in range(1, BAND):
            bits = p ^ ((p + k) & 3)
            if bits & first and (p + k) >> 2 == groups:
                found.add(p ^ (bits & last))
    return found


def hop(var_count, samp_count, kind, reverse=False):
    pairs = []
    for var in range(var_count):
        for samp in range(samp_count):
            first, last = (2, 1) if samp & 1 else (1, 2)
            back = (var - 4) % var_count
            use = True
            if kind == "first":
                target = var ^ first
            elif kind == "near":
                target = var ^ first
                use = (target & 3) in wanted(first, last, 0)
            elif kind == "last":
                target = var ^ last
            elif kind == "group":
                target = back
            elif kind == "two":
                target = back ^ first
                use = (var & 3) == 0
            elif kind == "column":
                target = (var - 8) % var_count
                use = (var & 3) in wanted(first, last, 2)
            else:
                target = back ^ last
                use = (var & 3) in wanted(first, last, 2)
            pair = (var * samp_count + samp, target * samp_count + samp)
            if use:
                pairs.append(pair[::-1] if reverse else pair)
    return pairs


def send(value, kind, reverse=False):
    pairs = hop(lax.axis_size("var"), lax.axis_size("samp"), kind, reverse)
    return lax.ppermute(value, ("var", "samp"), pairs)


def forward_kernel(data_ref, tile_ref, *out_refs):
    slot = pl.program_id(0)
    value = dot3(split(data_ref[...]), split(tile_ref[...]), NN)
    for which, ref in enumerate(out_refs):

        @pl.when(slot == which)
        def _():
            ref[...] = value


def forward(data, tiles):
    slots, block = tiles.shape[:2]
    rows = data.shape[0]
    flat = pl.BlockSpec((rows, block), lambda j: (0, 0))
    return pl.pallas_call(
        forward_kernel,
        grid=(slots,),
        in_specs=[flat, pl.BlockSpec((None, block, block), lambda j: (j, 0, 0))],
        out_specs=[flat] * slots,
        out_shape=[jax.ShapeDtypeStruct((rows, block), f32)] * slots,
        compiler_params=params(),
        cost_estimate=cost(6 * slots * rows * block * block, 4 * slots * block * (block + 2 * rows)),
        name="forward",
    )(data, tiles)


CODES = (0, 1, 2, 3, 5)


def choose_kernel(slots, count, offs_ref, *refs):
    sources, (out, sems) = refs[:count], refs[count:]
    p, flip = place()
    target = last_partner(p, flip)
    copies = []
    for slot in range(slots):
        last, code = route(target, offs_ref[0, slot + 1], flip)
        for value, source in zip(CODES, sources):
            copy = pltpu.make_async_copy(source, out.at[slot], sems.at[slot])
            pl.when((last == 1) & (code == value))(copy.start)
        known = (last == 1) & (code <= CODES[count - 1])
        copies.append((known, pltpu.make_async_copy(sources[0], out.at[slot], sems.at[slot])))
    for known, copy in copies:
        pl.when(known)(copy.wait)


def choose(offsets_next, *sources):
    slots = offsets_next.shape[1] - 1
    own = sources[0]
    return pl.pallas_call(
        functools.partial(choose_kernel, slots, len(sources)),
        in_specs=[smem_spec()] + [any_spec()] * len(sources),
        out_specs=any_spec(),
        out_shape=jax.ShapeDtypeStruct((slots,) + own.shape, f32),
        scratch_shapes=[pltpu.SemaphoreType.DMA((slots,))],
        compiler_params=params(),
        cost_estimate=cost(0, 8 * slots * own.size),
        name="choose",
    )(offsets_next, *sources)


def start_pick(offset, sources, target, sem):
    p, flip = place()
    last, code = route(p, offset, flip)
    for value, source in zip(CODES[:4], sources[:4]):
        pl.when((last == 0) & (code == value))(pltpu.make_async_copy(source, target, sem).start)
    over_last = last == 1
    if len(sources) > 5:
        over_last = over_last & (code != CODES[4])
        pl.when(code == CODES[4])(pltpu.make_async_copy(sources[5], target, sem).start)
    pl.when(over_last)(pltpu.make_async_copy(sources[4], target, sem).start)


def backward_kernel(slots, offs_ref, tile_ref, own, first, group, both, *refs):
    lasts_ref, out_ref, picked, sems = refs
    slot = pl.program_id(0)

    @pl.when(slot == 0)
    def _():
        out_ref[...] = jnp.zeros_like(out_ref)
        for each in range(slots):
            sources = (own, first, group, both, lasts_ref.at[each])
            start_pick(offs_ref[0, each + 1], sources, picked.at[each], sems.at[each])

    pltpu.make_async_copy(own, picked.at[slot], sems.at[slot]).wait()
    mirror = jnp.where(offs_ref[0, slot + 1] > 0, 1.0, 0.0).astype(f32)
    out_ref[...] += mirror * dot3(split(picked[slot]), split(tile_ref[...]), NT)


def backward(offsets, tiles, sources):
    slots, block = tiles.shape[0] - 1, tiles.shape[1]
    own = sources[0]
    rows = own.shape[0]
    return pl.pallas_call(
        functools.partial(backward_kernel, slots),
        grid=(slots,),
        in_specs=[smem_spec(), pl.BlockSpec((None, block, block), lambda j: (j + 1, 0, 0))]
        + [any_spec()] * len(sources),
        out_specs=pl.BlockSpec((rows, block), lambda j: (0, 0)),
        out_shape=jax.ShapeDtypeStruct((rows, block), f32),
        scratch_shapes=[pltpu.VMEM((slots, rows, block), f32), pltpu.SemaphoreType.DMA((slots,))],
        compiler_params=params(),
        cost_estimate=cost(6 * slots * rows * block * block, 4 * slots * block * (block + rows)),
        name="backward",
    )(offsets, tiles, *sources)


def bins_kernel(slots, offs_ref, next_ref, own_in, *refs):
    p, flip = place()
    target = last_partner(p, flip)
    mine, theirs, outs = refs[:slots], refs[slots : 2 * slots], refs[2 * slots :]
    totals = [own_in[...], None, None, None, None]
    for which, value in enumerate((0, 1, 2, 3, 5)):
        total = totals[which]
        for slot in range(slots):
            for there, offs, source in ((0, offs_ref, mine), (1, next_ref, theirs)):
                offset = offs[0, slot + 1]
                last, code = route(jnp.where(there == 1, target, p), offset, flip)
                use = (last == there) & (code == value) & (offset > 0)
                term = jnp.where(use, source[slot][...], 0.0)
                total = term if total is None else total + term
        totals[which] = total
    for ref, total in zip(outs, totals):
        ref[...] = total


def make_bins(offsets, offsets_next, own, mine, theirs):
    slots = len(mine)
    rows, block = own.shape
    step = rows // 4
    flat = pl.BlockSpec((step, block), lambda i: (i, 0))
    return pl.pallas_call(
        functools.partial(bins_kernel, slots),
        grid=(rows // step,),
        in_specs=[smem_spec(), smem_spec()] + [flat] * (1 + 2 * slots),
        out_specs=[flat] * 5,
        out_shape=[jax.ShapeDtypeStruct((rows, block), f32)] * 5,
        compiler_params=params(),
        cost_estimate=cost(20 * rows * block, 40 * rows * block),
        name="bins",
    )(offsets, offsets_next, own, *mine, *theirs)


def halves(pair):
    return lax.axis_index("samp") if pair else 0


def right_kernel(slots, pair, offs_ref, data_ref, image_ref, own, first, group, both, *refs):
    lasts_ref = refs[0]
    keep0_ref, send0_ref, keep_ref, send_ref, high_ref, low_ref, picked, sems = refs[-8:]
    for slot in range(slots):
        sources = (own, first, group, both, lasts_ref.at[slot])
        start_pick(offs_ref[0, slot + 1], sources, picked.at[slot], sems.at[slot])
    half = image_ref.shape[1] // 2
    samp = halves(pair)
    data = data_ref[...]
    image = image_ref[...]
    data_turned = split(data.T)
    high_ref[...], low_ref[...] = data_turned
    turned = split(image.T)
    image_pair, data_pair = split(image), split(data)

    def store(keep, send_out, which, total):
        lower, upper = total[:half], total[half:]

        @pl.when(samp == 0)
        def _():
            keep[which] = lower
            send_out[which] = upper

        @pl.when(samp != 0)
        def _():
            keep[which] = upper
            send_out[which] = lower

    store(keep0_ref, send0_ref, 0, dot3(turned, data_pair, NN) + dot3(data_turned, image_pair, NN))
    for slot in range(slots):
        pltpu.make_async_copy(own, picked.at[slot], sems.at[slot]).wait()
        store(keep_ref, send_ref, slot, dot3(turned, split(picked[slot]), NN))


def right(offsets, data, image, gate, sources, pair):
    slots = offsets.shape[1] - 1
    rows, block = data.shape
    part0 = jax.ShapeDtypeStruct((1, block // 2, block), f32)
    part = jax.ShapeDtypeStruct((slots, block // 2, block), f32)
    turned = jax.ShapeDtypeStruct((block, rows), bf16)
    return pl.pallas_call(
        functools.partial(right_kernel, slots, pair),
        in_specs=[smem_spec(), vmem_spec(), vmem_spec()] + [any_spec()] * (len(gate) + len(sources)),
        out_specs=[vmem_spec()] * 6,
        out_shape=[part0, part0, part, part, turned, turned],
        scratch_shapes=[pltpu.VMEM((slots, rows, block), f32), pltpu.SemaphoreType.DMA((slots,))],
        compiler_params=params(),
        cost_estimate=pl.CostEstimate(flops=400 * rows * block * block, bytes_accessed=0, transcendentals=0),
        name="right",
    )(offsets, data, image, *sources, *gate)


def left_kernel(slots, pair, offs_ref, keep_in, send_in, high_ref, low_ref, own, first, group, both, two, lasts_ref,
                keep_ref, send_ref, picked, sems):
    slot = pl.program_id(0)

    @pl.when(slot == 0)
    def _():
        for each in range(slots):
            sources = (own, first, group, both, lasts_ref.at[each], two)
            start_pick(offs_ref[0, each + 1], sources, picked.at[each], sems.at[each])

    pltpu.make_async_copy(own, picked.at[slot], sems.at[slot]).wait()
    half = send_ref.shape[0]
    mine = halves(pair) * half
    chosen = split(picked[slot])
    for out_ref, in_ref, row in ((send_ref, send_in, half - mine), (keep_ref, keep_in, mine)):
        rows = pl.ds(pl.multiple_of(row, half), half)
        out_ref[...] = in_ref[...] + dot3((high_ref[rows], low_ref[rows]), chosen, NN)


def left(offsets, parts, turned, sources, pair):
    keep = parts[0]
    slots, half = keep.shape[:2]
    block, rows = turned[0].shape
    spec = pl.BlockSpec((None, half, block), lambda j: (j, 0, 0))
    whole = pl.BlockSpec((block, rows), lambda j: (0, 0))
    part = jax.ShapeDtypeStruct(keep.shape, f32)
    return pl.pallas_call(
        functools.partial(left_kernel, slots, pair),
        grid=(slots,),
        in_specs=[smem_spec(), spec, spec, whole, whole] + [any_spec()] * len(sources),
        out_specs=[spec, spec],
        out_shape=[part, part],
        scratch_shapes=[pltpu.VMEM((slots, rows, block), f32), pltpu.SemaphoreType.DMA((slots,))],
        compiler_params=params(),
        cost_estimate=cost(6 * slots * rows * block * block, 4 * slots * block * (2 * block + rows)),
        name="left",
    )(offsets, *parts, *turned, *sources)


def finish_kernel(begin, factor, offs_ref, step_ref, tile_ref, keep_ref, other_ref, *refs):
    out_ref = refs[-1]
    slot = pl.program_id(0) + begin
    half, block = out_ref.shape
    step_size = step_ref[0]
    old = tile_ref[...]
    bound = step_size * penalty_weight
    stepped = old - (step_size * factor) * (keep_ref[...] + other_ref[...])

    def shrunk(value):
        return value - jnp.clip(value, -bound, bound)

    @pl.when(slot == 0)
    def _():
        rows = lax.axis_index("samp") * half + lax.broadcasted_iota(jnp.int32, (half, block), 0)
        on_diag = rows == lax.broadcasted_iota(jnp.int32, (half, block), 1)
        out_ref[...] = jnp.where(on_diag, stepped + step_size / jnp.where(on_diag, old, 1.0), shrunk(stepped))

    @pl.when(slot > 0)
    def _():
        out_ref[...] = jnp.where(offs_ref[0, slot] > 0, shrunk(stepped), 0.0)


def finish(offsets, step, tiles, keep, other, factor, begin, earlier=()):
    slots, block = tiles.shape[:2]
    count, half = keep.shape[:2]
    spec = pl.BlockSpec((None, half, block), lambda j: (j, 0, 0))
    tile_spec = pl.BlockSpec((None, half, block), lambda j: (j + begin, lax.axis_index("samp"), 0))
    return pl.pallas_call(
        functools.partial(finish_kernel, begin, factor),
        grid=(count,),
        in_specs=[smem_spec(), smem_spec(), tile_spec, spec, spec] + [any_spec()] * len(earlier),
        out_specs=pl.BlockSpec((None, half, block), lambda j: (j + begin, 0, 0)),
        out_shape=jax.ShapeDtypeStruct((slots, half, block), f32),
        input_output_aliases={5: 0} if earlier else {},
        compiler_params=params(),
        cost_estimate=cost(6 * keep.size, 16 * keep.size),
        name="finish",
    )(offsets, step, tiles, keep, other, *earlier)


def after(value, other):
    return lax.optimization_barrier((value, other))[0]


def swap(value):
    return lax.ppermute(value, "samp", [(0, 1), (1, 0)])


def shards(data, tiles, offsets, step):
    local_tiles = tiles[0]
    slot_count, block = local_tiles.shape[:2]
    samp_count = lax.axis_size("samp")
    pair = samp_count == 2
    factor = 1.0 / (2.0 * data.shape[0] * samp_count)

    offsets_next = send(offsets, "last")
    data_first = send(data, "first")
    own, *far = forward(data, local_tiles)
    theirs = [send(after(each, (offsets_next, data_first)), "last") for each in far]
    data_group = send(data, "group")
    data_both = send(data_group, "first")
    data_two = send(data_first, "column")
    own, bin_first, bin_group, bin_both, bin_two = make_bins(offsets, offsets_next, own, far, theirs)
    got_both = send(bin_both, "first")
    got_two = send(bin_two, "two", reverse=True)
    chosen = choose(offsets_next, data, data_first, data_group, data_both, data_two)
    data_last = send(chosen, "last")
    data_sources = (data, data_first, data_group, data_both, data_last)

    bin_group = bin_group + got_both + got_two
    got_group = send(bin_group, "group", reverse=True)
    got_first = send(bin_first, "near", reverse=True)
    image = own + backward(offsets, local_tiles, data_sources) + got_first + got_group

    image_group = send(image, "group")
    image_first = send(image, "first")
    image_both = send(image_group, "first")
    chosen = choose(offsets_next, image, image_first, image_group, image_both)
    image_last = send(chosen, "last")
    keep0, other0, keep, other, high, low = right(offsets, data, image, (chosen,), data_sources, pair)
    image_two = send(after(image_both, chosen), "direct")
    image_sources = (image, image_first, image_group, image_both, image_two, image_last)

    if pair:
        result = finish(offsets, step, local_tiles, keep0, swap(other0), factor, 0)
        keep = after(keep, result)
    keep, other = left(offsets, (keep, other), (high, low), image_sources, pair)
    if pair:
        return finish(offsets, step, local_tiles, keep, swap(other), factor, 1, (result,))[None]
    keep, other = (jnp.concatenate(both) for both in ((keep0, keep), (other0, other)))
    summed = lax.psum_scatter(jnp.concatenate([keep, other], axis=1), "samp", scatter_dimension=1, tiled=True)
    none = jnp.zeros_like(summed)
    return finish(offsets, step, local_tiles, summed, none, factor, 0)[None]


def solution(mesh):
    return jax.shard_map(
        shards,
        mesh=mesh,
        in_specs=(P("samp", "var"), P("var", None, None, None), P("var", None), P()),
        out_specs=P("var", None, "samp", None),
        check_vma=False,
    )
```

```python
import functools

import jax
import jax.numpy as jnp
from jax import lax
from jax.experimental import pallas as pl
from jax.experimental.pallas import tpu as pltpu
from jax.sharding import PartitionSpec as P

penalty_weight = 0.05
BAND = 6
VMEM_LIMIT = 20 * 1024 * 1024
NN = (((1,), (0,)), ((), ()))
NT = (((1,), (1,)), ((), ()))
f32, bf16 = jnp.float32, jnp.bfloat16


def params(**kw):
    return pltpu.CompilerParams(vmem_limit_bytes=VMEM_LIMIT, **kw)


def cost(flops, nbytes):
    return pl.CostEstimate(flops=0, bytes_accessed=0, transcendentals=0)


def any_spec():
    return pl.BlockSpec(memory_space=pl.ANY)


def vmem_spec():
    return pl.BlockSpec(memory_space=pltpu.VMEM)


def smem_spec():
    return pl.BlockSpec(memory_space=pltpu.SMEM)


def split(value):
    high = value.astype(bf16)
    return high, (value - high.astype(f32)).astype(bf16)


def dot3(left, right, dims):
    dot = functools.partial(lax.dot_general, dimension_numbers=dims, preferred_element_type=f32)
    return dot(left[0], right[0]) + (dot(left[0], right[1]) + dot(left[1], right[0]))


def route(p, k, flip):
    xbit = k & 1
    ybit = (((p + k) >> 1) ^ (p >> 1)) & 1
    first = jnp.where(flip == 0, xbit, ybit)
    last = jnp.where(flip == 0, ybit, xbit)
    return last, first + 2 * ((p + k) >> 2)


def place():
    return lax.axis_index("var") & 3, lax.axis_index("samp") & 1


def last_partner(p, flip):
    return jnp.where(flip == 0, p ^ 2, p ^ 1)


def wanted(first, last, groups):
    found = set()
    for p in range(4):
        for k in range(1, BAND):
            bits = p ^ ((p + k) & 3)
            if bits & first and (p + k) >> 2 == groups:
                found.add(p ^ (bits & last))
    return found


def hop(var_count, samp_count, kind, reverse=False):
    pairs = []
    for var in range(var_count):
        for samp in range(samp_count):
            first, last = (2, 1) if samp & 1 else (1, 2)
            back = (var - 4) % var_count
            use = True
            if kind == "first":
                target = var ^ first
            elif kind == "near":
                target = var ^ first
                use = (target & 3) in wanted(first, last, 0)
            elif kind == "last":
                target = var ^ last
            elif kind == "group":
                target = back
            elif kind == "two":
                target = back ^ first
                use = (var & 3) == 0
            elif kind == "column":
                target = (var - 8) % var_count
                use = (var & 3) in wanted(first, last, 2)
            else:
                target = back ^ last
                use = (var & 3) in wanted(first, last, 2)
            pair = (var * samp_count + samp, target * samp_count + samp)
            if use:
                pairs.append(pair[::-1] if reverse else pair)
    return pairs


def send(value, kind, reverse=False):
    pairs = hop(lax.axis_size("var"), lax.axis_size("samp"), kind, reverse)
    return lax.ppermute(value, ("var", "samp"), pairs)


def forward_kernel(data_ref, tile_ref, *out_refs):
    slot = pl.program_id(0)
    value = dot3(split(data_ref[...]), split(tile_ref[...]), NN)
    for which, ref in enumerate(out_refs):

        @pl.when(slot == which)
        def _():
            ref[...] = value


def forward(data, tiles):
    slots, block = tiles.shape[:2]
    rows = data.shape[0]
    flat = pl.BlockSpec((rows, block), lambda j: (0, 0))
    return pl.pallas_call(
        forward_kernel,
        grid=(slots,),
        in_specs=[flat, pl.BlockSpec((None, block, block), lambda j: (j, 0, 0))],
        out_specs=[flat] * slots,
        out_shape=[jax.ShapeDtypeStruct((rows, block), f32)] * slots,
        compiler_params=params(),
        cost_estimate=cost(6 * slots * rows * block * block, 4 * slots * block * (block + 2 * rows)),
        name="forward",
    )(data, tiles)


CODES = (0, 1, 2, 3, 5)


def choose_kernel(slots, count, offs_ref, *refs):
    sources, (out, sems) = refs[:count], refs[count:]
    p, flip = place()
    target = last_partner(p, flip)
    copies = []
    for slot in range(slots):
        last, code = route(target, offs_ref[0, slot + 1], flip)
        for value, source in zip(CODES, sources):
            copy = pltpu.make_async_copy(source, out.at[slot], sems.at[slot])
            pl.when((last == 1) & (code == value))(copy.start)
        known = (last == 1) & (code <= CODES[count - 1])
        copies.append((known, pltpu.make_async_copy(sources[0], out.at[slot], sems.at[slot])))
    for known, copy in copies:
        pl.when(known)(copy.wait)


def choose(offsets_next, *sources):
    slots = offsets_next.shape[1] - 1
    own = sources[0]
    return pl.pallas_call(
        functools.partial(choose_kernel, slots, len(sources)),
        in_specs=[smem_spec()] + [any_spec()] * len(sources),
        out_specs=any_spec(),
        out_shape=jax.ShapeDtypeStruct((slots,) + own.shape, f32),
        scratch_shapes=[pltpu.SemaphoreType.DMA((slots,))],
        compiler_params=params(),
        cost_estimate=cost(0, 8 * slots * own.size),
        name="choose",
    )(offsets_next, *sources)


def start_pick(offset, sources, target, sem):
    p, flip = place()
    last, code = route(p, offset, flip)
    for value, source in zip(CODES[:4], sources[:4]):
        pl.when((last == 0) & (code == value))(pltpu.make_async_copy(source, target, sem).start)
    over_last = last == 1
    if len(sources) > 5:
        over_last = over_last & (code != CODES[4])
        pl.when(code == CODES[4])(pltpu.make_async_copy(sources[5], target, sem).start)
    pl.when(over_last)(pltpu.make_async_copy(sources[4], target, sem).start)


def backward_kernel(slots, offs_ref, tile_ref, own, first, group, both, *refs):
    lasts_ref, out_ref, picked, sems = refs
    slot = pl.program_id(0)

    @pl.when(slot == 0)
    def _():
        out_ref[...] = jnp.zeros_like(out_ref)
        for each in range(slots):
            sources = (own, first, group, both, lasts_ref.at[each])
            start_pick(offs_ref[0, each + 1], sources, picked.at[each], sems.at[each])

    pltpu.make_async_copy(own, picked.at[slot], sems.at[slot]).wait()
    mirror = jnp.where(offs_ref[0, slot + 1] > 0, 1.0, 0.0).astype(f32)
    out_ref[...] += mirror * dot3(split(picked[slot]), split(tile_ref[...]), NT)


def backward(offsets, tiles, sources):
    slots, block = tiles.shape[0] - 1, tiles.shape[1]
    own = sources[0]
    rows = own.shape[0]
    return pl.pallas_call(
        functools.partial(backward_kernel, slots),
        grid=(slots,),
        in_specs=[smem_spec(), pl.BlockSpec((None, block, block), lambda j: (j + 1, 0, 0))]
        + [any_spec()] * len(sources),
        out_specs=pl.BlockSpec((rows, block), lambda j: (0, 0)),
        out_shape=jax.ShapeDtypeStruct((rows, block), f32),
        scratch_shapes=[pltpu.VMEM((slots, rows, block), f32), pltpu.SemaphoreType.DMA((slots,))],
        compiler_params=params(),
        cost_estimate=cost(6 * slots * rows * block * block, 4 * slots * block * (block + rows)),
        name="backward",
    )(offsets, tiles, *sources)


def bins_kernel(slots, offs_ref, next_ref, own_in, *refs):
    p, flip = place()
    target = last_partner(p, flip)
    mine, theirs, outs = refs[:slots], refs[slots : 2 * slots], refs[2 * slots :]
    totals = [own_in[...], None, None, None, None]
    for which, value in enumerate((0, 1, 2, 3, 5)):
        total = totals[which]
        for slot in range(slots):
            for there, offs, source in ((0, offs_ref, mine), (1, next_ref, theirs)):
                offset = offs[0, slot + 1]
                last, code = route(jnp.where(there == 1, target, p), offset, flip)
                use = (last == there) & (code == value) & (offset > 0)
                term = jnp.where(use, source[slot][...], 0.0)
                total = term if total is None else total + term
        totals[which] = total
    for ref, total in zip(outs, totals):
        ref[...] = total


def make_bins(offsets, offsets_next, own, mine, theirs):
    slots = len(mine)
    rows, block = own.shape
    step = rows // 4
    flat = pl.BlockSpec((step, block), lambda i: (i, 0))
    return pl.pallas_call(
        functools.partial(bins_kernel, slots),
        grid=(rows // step,),
        in_specs=[smem_spec(), smem_spec()] + [flat] * (1 + 2 * slots),
        out_specs=[flat] * 5,
        out_shape=[jax.ShapeDtypeStruct((rows, block), f32)] * 5,
        compiler_params=params(),
        cost_estimate=cost(20 * rows * block, 40 * rows * block),
        name="bins",
    )(offsets, offsets_next, own, *mine, *theirs)


def halves(pair):
    return lax.axis_index("samp") if pair else 0


def right_kernel(slots, pair, offs_ref, data_ref, image_ref, own, first, group, both, *refs):
    lasts_ref = refs[0]
    keep0_ref, send0_ref, keep_ref, send_ref, high_ref, low_ref, picked, sems = refs[-8:]
    for slot in range(slots):
        sources = (own, first, group, both, lasts_ref.at[slot])
        start_pick(offs_ref[0, slot + 1], sources, picked.at[slot], sems.at[slot])
    half = image_ref.shape[1] // 2
    samp = halves(pair)
    data = data_ref[...]
    image = image_ref[...]
    data_turned = split(data.T)
    high_ref[...], low_ref[...] = data_turned
    turned = split(image.T)
    image_pair, data_pair = split(image), split(data)

    def store(keep, send_out, which, total):
        lower, upper = total[:half], total[half:]

        @pl.when(samp == 0)
        def _():
            keep[which] = lower
            send_out[which] = upper

        @pl.when(samp != 0)
        def _():
            keep[which] = upper
            send_out[which] = lower

    store(keep0_ref, send0_ref, 0, dot3(turned, data_pair, NN) + dot3(data_turned, image_pair, NN))
    for slot in range(slots):
        pltpu.make_async_copy(own, picked.at[slot], sems.at[slot]).wait()
        store(keep_ref, send_ref, slot, dot3(turned, split(picked[slot]), NN))


def right(offsets, data, image, gate, sources, pair):
    slots = offsets.shape[1] - 1
    rows, block = data.shape
    part0 = jax.ShapeDtypeStruct((1, block // 2, block), f32)
    part = jax.ShapeDtypeStruct((slots, block // 2, block), f32)
    turned = jax.ShapeDtypeStruct((block, rows), bf16)
    return pl.pallas_call(
        functools.partial(right_kernel, slots, pair),
        in_specs=[smem_spec(), vmem_spec(), vmem_spec()] + [any_spec()] * (len(gate) + len(sources)),
        out_specs=[vmem_spec()] * 6,
        out_shape=[part0, part0, part, part, turned, turned],
        scratch_shapes=[pltpu.VMEM((slots, rows, block), f32), pltpu.SemaphoreType.DMA((slots,))],
        compiler_params=params(),
        cost_estimate=pl.CostEstimate(flops=400 * rows * block * block, bytes_accessed=0, transcendentals=0),
        name="right",
    )(offsets, data, image, *sources, *gate)


def left_kernel(slots, pair, offs_ref, keep_in, send_in, high_ref, low_ref, own, first, group, both, two, lasts_ref,
                keep_ref, send_ref, picked, sems):
    slot = pl.program_id(0)

    @pl.when(slot == 0)
    def _():
        for each in range(slots):
            sources = (own, first, group, both, lasts_ref.at[each], two)
            start_pick(offs_ref[0, each + 1], sources, picked.at[each], sems.at[each])

    pltpu.make_async_copy(own, picked.at[slot], sems.at[slot]).wait()
    half = send_ref.shape[0]
    mine = halves(pair) * half
    chosen = split(picked[slot])
    for out_ref, in_ref, row in ((send_ref, send_in, half - mine), (keep_ref, keep_in, mine)):
        rows = pl.ds(pl.multiple_of(row, half), half)
        out_ref[...] = in_ref[...] + dot3((high_ref[rows], low_ref[rows]), chosen, NN)


def left(offsets, parts, turned, sources, pair):
    keep = parts[0]
    slots, half = keep.shape[:2]
    block, rows = turned[0].shape
    spec = pl.BlockSpec((None, half, block), lambda j: (j, 0, 0))
    whole = pl.BlockSpec((block, rows), lambda j: (0, 0))
    part = jax.ShapeDtypeStruct(keep.shape, f32)
    return pl.pallas_call(
        functools.partial(left_kernel, slots, pair),
        grid=(slots,),
        in_specs=[smem_spec(), spec, spec, whole, whole] + [any_spec()] * len(sources),
        out_specs=[spec, spec],
        out_shape=[part, part],
        scratch_shapes=[pltpu.VMEM((slots, rows, block), f32), pltpu.SemaphoreType.DMA((slots,))],
        compiler_params=params(),
        cost_estimate=cost(6 * slots * rows * block * block, 4 * slots * block * (2 * block + rows)),
        name="left",
    )(offsets, *parts, *turned, *sources)


def finish_kernel(begin, factor, offs_ref, step_ref, tile_ref, keep_ref, other_ref, *refs):
    out_ref = refs[-1]
    slot = pl.program_id(0) + begin
    half, block = out_ref.shape
    step_size = step_ref[0]
    old = tile_ref[...]
    bound = step_size * penalty_weight
    stepped = old - (step_size * factor) * (keep_ref[...] + other_ref[...])

    def shrunk(value):
        return value - jnp.clip(value, -bound, bound)

    @pl.when(slot == 0)
    def _():
        rows = lax.axis_index("samp") * half + lax.broadcasted_iota(jnp.int32, (half, block), 0)
        on_diag = rows == lax.broadcasted_iota(jnp.int32, (half, block), 1)
        out_ref[...] = jnp.where(on_diag, stepped + step_size / jnp.where(on_diag, old, 1.0), shrunk(stepped))

    @pl.when(slot > 0)
    def _():
        out_ref[...] = jnp.where(offs_ref[0, slot] > 0, shrunk(stepped), 0.0)


def finish(offsets, step, tiles, keep, other, factor, begin, earlier=()):
    slots, block = tiles.shape[:2]
    count, half = keep.shape[:2]
    spec = pl.BlockSpec((None, half, block), lambda j: (j, 0, 0))
    tile_spec = pl.BlockSpec((None, half, block), lambda j: (j + begin, lax.axis_index("samp"), 0))
    return pl.pallas_call(
        functools.partial(finish_kernel, begin, factor),
        grid=(count,),
        in_specs=[smem_spec(), smem_spec(), tile_spec, spec, spec] + [any_spec()] * len(earlier),
        out_specs=pl.BlockSpec((None, half, block), lambda j: (j + begin, 0, 0)),
        out_shape=jax.ShapeDtypeStruct((slots, half, block), f32),
        input_output_aliases={5: 0} if earlier else {},
        compiler_params=params(),
        cost_estimate=cost(6 * keep.size, 16 * keep.size),
        name="finish",
    )(offsets, step, tiles, keep, other, *earlier)


def after(value, other):
    return lax.optimization_barrier((value, other))[0]


def swap(value):
    return lax.ppermute(value, "samp", [(0, 1), (1, 0)])


def shards(data, tiles, offsets, step):
    local_tiles = tiles[0]
    slot_count, block = local_tiles.shape[:2]
    samp_count = lax.axis_size("samp")
    pair = samp_count == 2
    factor = 1.0 / (2.0 * data.shape[0] * samp_count)

    offsets_next = send(offsets, "last")
    data_first = send(data, "first")
    own, *far = forward(data, local_tiles)
    theirs = [send(after(each, (offsets_next, data_first)), "last") for each in far]
    data_group = send(data, "group")
    data_both = send(data_group, "first")
    data_two = send(data_first, "column")
    own, bin_first, bin_group, bin_both, bin_two = make_bins(offsets, offsets_next, own, far, theirs)
    got_both = send(bin_both, "first")
    got_two = send(bin_two, "two", reverse=True)
    chosen = choose(after(offsets_next, got_both), data, data_first, data_group, data_both, data_two)
    data_last = send(chosen, "last")
    data_sources = (data, data_first, data_group, data_both, data_last)

    bin_group = bin_group + got_both + got_two
    got_group = send(bin_group, "group", reverse=True)
    got_first = send(bin_first, "near", reverse=True)
    image = own + backward(offsets, local_tiles, data_sources) + got_first + got_group

    image_group = send(image, "group")
    image_first = send(image, "first")
    image_both = send(image_group, "first")
    chosen = choose(offsets_next, image, image_first, image_group, image_both)
    image_last = send(chosen, "last")
    keep0, other0, keep, other, high, low = right(offsets, data, image, (chosen,), data_sources, pair)
    image_two = send(after(image_both, chosen), "direct")
    image_sources = (image, image_first, image_group, image_both, image_two, image_last)

    if pair:
        result = finish(offsets, step, local_tiles, keep0, swap(other0), factor, 0)
        keep = after(keep, result)
    keep, other = left(offsets, (keep, other), (high, low), image_sources, pair)
    if pair:
        return finish(offsets, step, local_tiles, keep, swap(other), factor, 1, (result,))[None]
    keep, other = (jnp.concatenate(both) for both in ((keep0, keep), (other0, other)))
    summed = lax.psum_scatter(jnp.concatenate([keep, other], axis=1), "samp", scatter_dimension=1, tiled=True)
    none = jnp.zeros_like(summed)
    return finish(offsets, step, local_tiles, summed, none, factor, 0)[None]


def solution(mesh):
    return jax.shard_map(
        shards,
        mesh=mesh,
        in_specs=(P("samp", "var"), P("var", None, None, None), P("var", None), P()),
        out_specs=P("var", None, "samp", None),
        check_vma=False,
    )
```

```python
import functools

import jax
import jax.numpy as jnp
from jax import lax
from jax.experimental import pallas as pl
from jax.experimental.pallas import tpu as pltpu
from jax.sharding import PartitionSpec as P

penalty_weight = 0.05
BAND = 6
VMEM_LIMIT = 20 * 1024 * 1024
NN = (((1,), (0,)), ((), ()))
NT = (((1,), (1,)), ((), ()))
f32, bf16 = jnp.float32, jnp.bfloat16


def params(**kw):
    return pltpu.CompilerParams(vmem_limit_bytes=VMEM_LIMIT, **kw)


def cost(flops, nbytes):
    return pl.CostEstimate(flops=0, bytes_accessed=0, transcendentals=0)


def any_spec():
    return pl.BlockSpec(memory_space=pl.ANY)


def vmem_spec():
    return pl.BlockSpec(memory_space=pltpu.VMEM)


def smem_spec():
    return pl.BlockSpec(memory_space=pltpu.SMEM)


def split(value):
    high = value.astype(bf16)
    return high, (value - high.astype(f32)).astype(bf16)


def dot3(left, right, dims):
    dot = functools.partial(lax.dot_general, dimension_numbers=dims, preferred_element_type=f32)
    return dot(left[0], right[0]) + (dot(left[0], right[1]) + dot(left[1], right[0]))


def route(p, k, flip):
    xbit = k & 1
    ybit = (((p + k) >> 1) ^ (p >> 1)) & 1
    first = jnp.where(flip == 0, xbit, ybit)
    last = jnp.where(flip == 0, ybit, xbit)
    return last, first + 2 * ((p + k) >> 2)


def place():
    return lax.axis_index("var") & 3, lax.axis_index("samp") & 1


def last_partner(p, flip):
    return jnp.where(flip == 0, p ^ 2, p ^ 1)


def wanted(first, last, groups):
    found = set()
    for p in range(4):
        for k in range(1, BAND):
            bits = p ^ ((p + k) & 3)
            if bits & first and (p + k) >> 2 == groups:
                found.add(p ^ (bits & last))
    return found


def hop(var_count, samp_count, kind, reverse=False):
    pairs = []
    for var in range(var_count):
        for samp in range(samp_count):
            first, last = (2, 1) if samp & 1 else (1, 2)
            back = (var - 4) % var_count
            use = True
            if kind == "first":
                target = var ^ first
            elif kind == "near":
                target = var ^ first
                use = (target & 3) in wanted(first, last, 0)
            elif kind == "last":
                target = var ^ last
            elif kind == "group":
                target = back
            elif kind == "two":
                target = back ^ first
                use = (var & 3) == 0
            elif kind == "column":
                target = (var - 8) % var_count
                use = (var & 3) in wanted(first, last, 2)
            else:
                target = back ^ last
                use = (var & 3) in wanted(first, last, 2)
            pair = (var * samp_count + samp, target * samp_count + samp)
            if use:
                pairs.append(pair[::-1] if reverse else pair)
    return pairs


def send(value, kind, reverse=False):
    pairs = hop(lax.axis_size("var"), lax.axis_size("samp"), kind, reverse)
    return lax.ppermute(value, ("var", "samp"), pairs)


def forward_kernel(data_hbm, tiles_hbm, *refs):
    slots = tiles_hbm.shape[0]
    out_refs, (data_ref, tiles_ref, sems) = refs[:slots], refs[slots:]
    data_copy = pltpu.make_async_copy(data_hbm, data_ref, sems.at[slots])
    copies = [pltpu.make_async_copy(tiles_hbm.at[slot], tiles_ref.at[slot], sems.at[slot]) for slot in range(slots)]
    order = list(range(1, slots)) + [0]
    data_copy.start()
    for slot in order:
        copies[slot].start()
    data_copy.wait()
    data = split(data_ref[...])
    for slot in order:
        copies[slot].wait()
        out_refs[slot][...] = dot3(data, split(tiles_ref[slot]), NN)


def forward(data, tiles):
    slots, block = tiles.shape[:2]
    rows = data.shape[0]
    return pl.pallas_call(
        forward_kernel,
        in_specs=[pl.BlockSpec(memory_space=pltpu.HBM)] * 2,
        out_specs=[vmem_spec()] * slots,
        out_shape=[jax.ShapeDtypeStruct((rows, block), f32)] * slots,
        scratch_shapes=[
            pltpu.VMEM((rows, block), f32),
            pltpu.VMEM((slots, block, block), f32),
            pltpu.SemaphoreType.DMA((slots + 1,)),
        ],
        compiler_params=params(),
        cost_estimate=cost(6 * slots * rows * block * block, 4 * slots * block * (block + 2 * rows)),
        name="forward",
    )(*(pltpu.with_memory_space_constraint(each, pltpu.HBM) for each in (data, tiles)))


CODES = (0, 1, 2, 3, 5)


def choose_kernel(slots, count, offs_ref, *refs):
    sources, (out, sems) = refs[:count], refs[count:]
    p, flip = place()
    target = last_partner(p, flip)
    copies = []
    for slot in range(slots):
        last, code = route(target, offs_ref[0, slot + 1], flip)
        for value, source in zip(CODES, sources):
            copy = pltpu.make_async_copy(source, out.at[slot], sems.at[slot])
            pl.when((last == 1) & (code == value))(copy.start)
        known = (last == 1) & (code <= CODES[count - 1])
        copies.append((known, pltpu.make_async_copy(sources[0], out.at[slot], sems.at[slot])))
    for known, copy in copies:
        pl.when(known)(copy.wait)


def choose(offsets_next, *sources):
    slots = offsets_next.shape[1] - 1
    own = sources[0]
    return pl.pallas_call(
        functools.partial(choose_kernel, slots, len(sources)),
        in_specs=[smem_spec()] + [any_spec()] * len(sources),
        out_specs=any_spec(),
        out_shape=jax.ShapeDtypeStruct((slots,) + own.shape, f32),
        scratch_shapes=[pltpu.SemaphoreType.DMA((slots,))],
        compiler_params=params(),
        cost_estimate=cost(0, 8 * slots * own.size),
        name="choose",
    )(offsets_next, *sources)


def start_pick(offset, sources, target, sem):
    p, flip = place()
    last, code = route(p, offset, flip)
    for value, source in zip(CODES[:4], sources[:4]):
        pl.when((last == 0) & (code == value))(pltpu.make_async_copy(source, target, sem).start)
    over_last = last == 1
    if len(sources) > 5:
        over_last = over_last & (code != CODES[4])
        pl.when(code == CODES[4])(pltpu.make_async_copy(sources[5], target, sem).start)
    pl.when(over_last)(pltpu.make_async_copy(sources[4], target, sem).start)


def backward_kernel(slots, offs_ref, tile_ref, own, first, group, both, *refs):
    lasts_ref, out_ref, picked, sems = refs
    slot = pl.program_id(0)

    @pl.when(slot == 0)
    def _():
        out_ref[...] = jnp.zeros_like(out_ref)
        for each in range(slots):
            sources = (own, first, group, both, lasts_ref.at[each])
            start_pick(offs_ref[0, each + 1], sources, picked.at[each], sems.at[each])

    pltpu.make_async_copy(own, picked.at[slot], sems.at[slot]).wait()
    mirror = jnp.where(offs_ref[0, slot + 1] > 0, 1.0, 0.0).astype(f32)
    out_ref[...] += mirror * dot3(split(picked[slot]), split(tile_ref[...]), NT)


def backward(offsets, tiles, sources):
    slots, block = tiles.shape[0] - 1, tiles.shape[1]
    own = sources[0]
    rows = own.shape[0]
    return pl.pallas_call(
        functools.partial(backward_kernel, slots),
        grid=(slots,),
        in_specs=[smem_spec(), pl.BlockSpec((None, block, block), lambda j: (j + 1, 0, 0))]
        + [any_spec()] * len(sources),
        out_specs=pl.BlockSpec((rows, block), lambda j: (0, 0)),
        out_shape=jax.ShapeDtypeStruct((rows, block), f32),
        scratch_shapes=[pltpu.VMEM((slots, rows, block), f32), pltpu.SemaphoreType.DMA((slots,))],
        compiler_params=params(),
        cost_estimate=cost(6 * slots * rows * block * block, 4 * slots * block * (block + rows)),
        name="backward",
    )(offsets, tiles, *sources)


def bins_kernel(slots, offs_ref, next_ref, own_in, *refs):
    p, flip = place()
    target = last_partner(p, flip)
    mine, theirs, outs = refs[:slots], refs[slots : 2 * slots], refs[2 * slots :]
    totals = [own_in[...], None, None, None, None]
    for which, value in enumerate((0, 1, 2, 3, 5)):
        total = totals[which]
        for slot in range(slots):
            for there, offs, source in ((0, offs_ref, mine), (1, next_ref, theirs)):
                offset = offs[0, slot + 1]
                last, code = route(jnp.where(there == 1, target, p), offset, flip)
                use = (last == there) & (code == value) & (offset > 0)
                term = jnp.where(use, source[slot][...], 0.0)
                total = term if total is None else total + term
        totals[which] = total
    for ref, total in zip(outs, totals):
        ref[...] = total


def make_bins(offsets, offsets_next, own, mine, theirs):
    slots = len(mine)
    rows, block = own.shape
    step = rows // 4
    flat = pl.BlockSpec((step, block), lambda i: (i, 0))
    return pl.pallas_call(
        functools.partial(bins_kernel, slots),
        grid=(rows // step,),
        in_specs=[smem_spec(), smem_spec()] + [flat] * (1 + 2 * slots),
        out_specs=[flat] * 5,
        out_shape=[jax.ShapeDtypeStruct((rows, block), f32)] * 5,
        compiler_params=params(),
        cost_estimate=cost(20 * rows * block, 40 * rows * block),
        name="bins",
    )(offsets, offsets_next, own, *mine, *theirs)


def halves(pair):
    return lax.axis_index("samp") if pair else 0


def right_kernel(slots, pair, offs_ref, data_ref, image_ref, own, first, group, both, *refs):
    lasts_ref = refs[0]
    keep0_ref, send0_ref, keep_ref, send_ref, high_ref, low_ref, picked, sems = refs[-8:]
    for slot in range(slots):
        sources = (own, first, group, both, lasts_ref.at[slot])
        start_pick(offs_ref[0, slot + 1], sources, picked.at[slot], sems.at[slot])
    half = image_ref.shape[1] // 2
    samp = halves(pair)
    data = data_ref[...]
    image = image_ref[...]
    data_turned = split(data.T)
    high_ref[...], low_ref[...] = data_turned
    turned = split(image.T)
    image_pair, data_pair = split(image), split(data)

    def store(keep, send_out, which, total):
        lower, upper = total[:half], total[half:]

        @pl.when(samp == 0)
        def _():
            keep[which] = lower
            send_out[which] = upper

        @pl.when(samp != 0)
        def _():
            keep[which] = upper
            send_out[which] = lower

    store(keep0_ref, send0_ref, 0, dot3(turned, data_pair, NN) + dot3(data_turned, image_pair, NN))
    for slot in range(slots):
        pltpu.make_async_copy(own, picked.at[slot], sems.at[slot]).wait()
        store(keep_ref, send_ref, slot, dot3(turned, split(picked[slot]), NN))


def right(offsets, data, image, gate, sources, pair):
    slots = offsets.shape[1] - 1
    rows, block = data.shape
    part0 = jax.ShapeDtypeStruct((1, block // 2, block), f32)
    part = jax.ShapeDtypeStruct((slots, block // 2, block), f32)
    turned = jax.ShapeDtypeStruct((block, rows), bf16)
    return pl.pallas_call(
        functools.partial(right_kernel, slots, pair),
        in_specs=[smem_spec(), vmem_spec(), vmem_spec()] + [any_spec()] * (len(gate) + len(sources)),
        out_specs=[vmem_spec()] * 6,
        out_shape=[part0, part0, part, part, turned, turned],
        scratch_shapes=[pltpu.VMEM((slots, rows, block), f32), pltpu.SemaphoreType.DMA((slots,))],
        compiler_params=params(),
        cost_estimate=pl.CostEstimate(flops=400 * rows * block * block, bytes_accessed=0, transcendentals=0),
        name="right",
    )(offsets, data, image, *sources, *gate)


def left_kernel(slots, pair, offs_ref, keep_in, send_in, high_ref, low_ref, own, first, group, both, two, lasts_ref,
                keep_ref, send_ref, picked, sems):
    slot = pl.program_id(0)

    @pl.when(slot == 0)
    def _():
        for each in range(slots):
            sources = (own, first, group, both, lasts_ref.at[each], two)
            start_pick(offs_ref[0, each + 1], sources, picked.at[each], sems.at[each])

    pltpu.make_async_copy(own, picked.at[slot], sems.at[slot]).wait()
    half = send_ref.shape[0]
    mine = halves(pair) * half
    chosen = split(picked[slot])
    for out_ref, in_ref, row in ((send_ref, send_in, half - mine), (keep_ref, keep_in, mine)):
        rows = pl.ds(pl.multiple_of(row, half), half)
        out_ref[...] = in_ref[...] + dot3((high_ref[rows], low_ref[rows]), chosen, NN)


def left(offsets, parts, turned, sources, pair):
    keep = parts[0]
    slots, half = keep.shape[:2]
    block, rows = turned[0].shape
    spec = pl.BlockSpec((None, half, block), lambda j: (j, 0, 0))
    whole = pl.BlockSpec((block, rows), lambda j: (0, 0))
    part = jax.ShapeDtypeStruct(keep.shape, f32)
    return pl.pallas_call(
        functools.partial(left_kernel, slots, pair),
        grid=(slots,),
        in_specs=[smem_spec(), spec, spec, whole, whole] + [any_spec()] * len(sources),
        out_specs=[spec, spec],
        out_shape=[part, part],
        scratch_shapes=[pltpu.VMEM((slots, rows, block), f32), pltpu.SemaphoreType.DMA((slots,))],
        compiler_params=params(),
        cost_estimate=cost(6 * slots * rows * block * block, 4 * slots * block * (2 * block + rows)),
        name="left",
    )(offsets, *parts, *turned, *sources)


def finish_kernel(begin, factor, offs_ref, step_ref, tile_ref, keep_ref, other_ref, *refs):
    out_ref = refs[-1]
    slot = pl.program_id(0) + begin
    half, block = out_ref.shape
    step_size = step_ref[0]
    old = tile_ref[...]
    bound = step_size * penalty_weight
    stepped = old - (step_size * factor) * (keep_ref[...] + other_ref[...])

    def shrunk(value):
        return value - jnp.clip(value, -bound, bound)

    @pl.when(slot == 0)
    def _():
        rows = lax.axis_index("samp") * half + lax.broadcasted_iota(jnp.int32, (half, block), 0)
        on_diag = rows == lax.broadcasted_iota(jnp.int32, (half, block), 1)
        out_ref[...] = jnp.where(on_diag, stepped + step_size / jnp.where(on_diag, old, 1.0), shrunk(stepped))

    @pl.when(slot > 0)
    def _():
        out_ref[...] = jnp.where(offs_ref[0, slot] > 0, shrunk(stepped), 0.0)


def finish(offsets, step, tiles, keep, other, factor, begin, earlier=()):
    slots, block = tiles.shape[:2]
    count, half = keep.shape[:2]
    spec = pl.BlockSpec((None, half, block), lambda j: (j, 0, 0))
    tile_spec = pl.BlockSpec((None, half, block), lambda j: (j + begin, lax.axis_index("samp"), 0))
    return pl.pallas_call(
        functools.partial(finish_kernel, begin, factor),
        grid=(count,),
        in_specs=[smem_spec(), smem_spec(), tile_spec, spec, spec] + [any_spec()] * len(earlier),
        out_specs=pl.BlockSpec((None, half, block), lambda j: (j + begin, 0, 0)),
        out_shape=jax.ShapeDtypeStruct((slots, half, block), f32),
        input_output_aliases={5: 0} if earlier else {},
        compiler_params=params(),
        cost_estimate=cost(6 * keep.size, 16 * keep.size),
        name="finish",
    )(offsets, step, tiles, keep, other, *earlier)


def after(value, other):
    return lax.optimization_barrier((value, other))[0]


def swap(value):
    return lax.ppermute(value, "samp", [(0, 1), (1, 0)])


def shards(data, tiles, offsets, step):
    local_tiles = tiles[0]
    slot_count, block = local_tiles.shape[:2]
    samp_count = lax.axis_size("samp")
    pair = samp_count == 2
    factor = 1.0 / (2.0 * data.shape[0] * samp_count)

    offsets_next = send(offsets, "last")
    data_first = send(data, "first")
    own, *far = forward(data, local_tiles)
    theirs = [send(after(each, (offsets_next, data_first)), "last") for each in far]
    data_group = send(data, "group")
    data_both = send(data_group, "first")
    data_two = send(data_first, "column")
    own, bin_first, bin_group, bin_both, bin_two = make_bins(offsets, offsets_next, own, far, theirs)
    got_both = send(bin_both, "first")
    got_two = send(bin_two, "two", reverse=True)
    chosen = choose(offsets_next, data, data_first, data_group, data_both, data_two)
    data_last = send(chosen, "last")
    data_sources = (data, data_first, data_group, data_both, data_last)

    bin_group = bin_group + got_both + got_two
    got_group = send(bin_group, "group", reverse=True)
    got_first = send(bin_first, "near", reverse=True)
    image = own + backward(offsets, local_tiles, data_sources) + got_first + got_group

    image_group = send(image, "group")
    image_first = send(image, "first")
    image_both = send(image_group, "first")
    chosen = choose(offsets_next, image, image_first, image_group, image_both)
    image_last = send(chosen, "last")
    keep0, other0, keep, other, high, low = right(offsets, data, image, (chosen,), data_sources, pair)
    image_two = send(after(image_both, chosen), "direct")
    image_sources = (image, image_first, image_group, image_both, image_two, image_last)

    if pair:
        result = finish(offsets, step, local_tiles, keep0, swap(other0), factor, 0)
        keep = after(keep, result)
    keep, other = left(offsets, (keep, other), (high, low), image_sources, pair)
    if pair:
        return finish(offsets, step, local_tiles, keep, swap(other), factor, 1, (result,))[None]
    keep, other = (jnp.concatenate(both) for both in ((keep0, keep), (other0, other)))
    summed = lax.psum_scatter(jnp.concatenate([keep, other], axis=1), "samp", scatter_dimension=1, tiled=True)
    none = jnp.zeros_like(summed)
    return finish(offsets, step, local_tiles, summed, none, factor, 0)[None]


def solution(mesh):
    return jax.shard_map(
        shards,
        mesh=mesh,
        in_specs=(P("samp", "var"), P("var", None, None, None), P("var", None), P()),
        out_specs=P("var", None, "samp", None),
        check_vma=False,
    )
```
